32 devices in a mesh: dp: 4 (over x, core), fsdp: 8 (over z, y).
Axes of the slice: x: 2, y: 2, z: 4, core: 2. Of those that a mesh axis runs over, the one named last changes fastest.
Arguments:
- targets: float32 [32, 64, 768], P(('dp', 'fsdp')), may hold values from -6 to 6
- passages: bfloat16 [32, 1920, 768], P('dp', 'fsdp'), may hold values from -6 to 6
- tgt_len: int32 [32], P(('dp', 'fsdp')), may hold values from 8 to 64, as said below
- out_grad: float32 [32, 64, 768], P(('dp', 'fsdp')), may hold values from -6 to 6
- ln_self: bfloat16 [768], P(('dp', 'fsdp')), may hold values from 0.099609375 to 1.8984375
- rel_bias: bfloat16 [384], P(('dp', 'fsdp')), may hold values from -6 to 6
- self_q: bfloat16 [768, 768], P(('dp', 'fsdp')), may hold values from -0.0546875 to 0.0546875
- self_kv: bfloat16 [768, 1536], P(('dp', 'fsdp')), may hold values from -0.21875 to 0.21875
- self_out: bfloat16 [768, 768], P(('dp', 'fsdp')), may hold values from -0.3125 to 0.3125
- ln_cross: bfloat16 [768], P(('dp', 'fsdp')), may hold values from 0.099609375 to 1.8984375
- cross_q: bfloat16 [768, 768], P(('dp', 'fsdp')), may hold values from -0.0546875 to 0.0546875
- cross_kv: bfloat16 [768, 1536], P(('dp', 'fsdp')), may hold values from -0.21875 to 0.21875
- cross_out: bfloat16 [768, 768], P(('dp', 'fsdp')), may hold values from -1.25 to 1.25
- ln_ff: bfloat16 [768], P(('dp', 'fsdp')), may hold values from 0.099609375 to 1.8984375
- ff_in: bfloat16 [768, 3072], P(('dp', 'fsdp')), may hold values from -0.21875 to 0.21875
- ff_out: bfloat16 [3072, 768], P(('dp', 'fsdp')), may hold values from -0.109375 to 0.109375
Outputs:
- block_out: float32 [32, 64, 768], P(('dp', 'fsdp'))
- target_grad: float32 [32, 64, 768], P(('dp', 'fsdp'))
- passage_grad: bfloat16 [32, 1920, 768], P('dp', 'fsdp')
- ln_self_grad: float32 [768], P(('dp', 'fsdp'))
- rel_bias_grad: float32 [384], P(('dp', 'fsdp'))
- self_q_grad: float32 [768, 768], P(('dp', 'fsdp'))
- self_kv_grad: float32 [768, 1536], P(('dp', 'fsdp'))
- self_out_grad: float32 [768, 768], P(('dp', 'fsdp'))
- ln_cross_grad: float32 [768], P(('dp', 'fsdp'))
- cross_q_grad: float32 [768, 768], P(('dp', 'fsdp'))
- cross_kv_grad: float32 [768, 1536], P(('dp', 'fsdp'))
- cross_out_grad: float32 [768, 768], P(('dp', 'fsdp'))
- ln_ff_grad: float32 [768], P(('dp', 'fsdp'))
- ff_in_grad: float32 [768, 3072], P(('dp', 'fsdp'))
- ff_out_grad: float32 [3072, 768], P(('dp', 'fsdp'))
The draws below stay inside these ranges and needn't reach their ends.
Inputs may be any that keep to these rules, and one draw needn't show every extreme that they name: `tgt_len`: each query's length is 64, 32 or 8 by its task (about 6, 6 and 4 queries in 16); the first query has 64.
All inputs are finite; a program needn't handle non-finite values.
Results may differ from the reference program's by a relative error of at most 0.03.
Values may be sent and summed in bfloat16 or wider, within the bound.
A program may use at most 192 MiB of HBM per device.

```python
import math
import jax
import jax.numpy as jnp
from jax import lax

D = 768
FF = 3072
HEADS = 12
DK = 64
BUCKETS = 32
TMAX = 64
ENC_ROWS = 1920
QUERIES = 32


def draw_tgt_len(key, part):
    key = jax.random.fold_in(key, 11)
    tasks = jax.random.randint(key, (QUERIES,), 0, 16)
    lengths = jnp.where(tasks < 6, TMAX, jnp.where(tasks < 12, TMAX // 2, TMAX // 8))
    return jnp.where(jnp.arange(QUERIES) == 0, TMAX, lengths).astype(jnp.int32)


def levels(own_key, extent, cuts, low, top_value):
    def one(axis_at, blocks):
        heights = jax.random.uniform(jax.random.fold_in(jax.random.fold_in(own_key, 6), axis_at), (blocks,), jnp.float32, low / len(cuts), top_value / len(cuts))
        return jnp.repeat(jnp.exp(heights), extent[axis_at] // blocks).reshape((-1,) + (1,) * (len(extent) - axis_at - 1))

    factor_of = one(*cuts[0])
    for cut in cuts[1:]:
        factor_of = factor_of * one(*cut)
    return factor_of


def scatter_about(key, extent, scale, limit, split=(), kind=jnp.bfloat16):
    factor_of = levels(key, extent, split, -0.22, 0.18) if split else 1.0
    values = jax.random.normal(key, extent, jnp.float32) * scale * factor_of
    return jnp.minimum(jnp.maximum(values, -limit), limit).astype(kind)


def setup_inputs(seed: int = 0) -> dict:
    key_list = jax.random.split(jax.random.key(seed), 17)
    return {
        "targets": scatter_about(key_list[0], (QUERIES, TMAX, D), 1.0, 6.0, ((0, 32),), jnp.float32),
        "passages": scatter_about(key_list[1], (QUERIES, ENC_ROWS, D), 1.0, 6.0, ((0, 4), (1, 8))),
        "tgt_len": draw_tgt_len(jax.random.fold_in(key_list[16], 71), 0),
        "out_grad": scatter_about(key_list[3], (QUERIES, TMAX, D), 1.0, 6.0, ((0, 32),), jnp.float32),
        "ln_self": jnp.clip(1.0 + 0.18 * jax.random.normal(key_list[4], (D,), jnp.float32), 0.099609375, 1.8984375).astype(jnp.bfloat16),
        "rel_bias": scatter_about(key_list[5], (HEADS * BUCKETS,), 1.0, 6.0, ((0, 32),)),
        "self_q": scatter_about(key_list[6], (D, D), (16 * D) ** -0.5, 0.0546875, ((0, 32),)),
        "self_kv": scatter_about(key_list[7], (D, 2 * D), D ** -0.5, 0.21875, ((0, 32),)),
        "self_out": scatter_about(key_list[8], (D, D), (D // 2) ** -0.5, 0.3125, ((0, 32),)),
        "ln_cross": jnp.clip(1.0 + 0.18 * jax.random.normal(key_list[9], (D,), jnp.float32), 0.099609375, 1.8984375).astype(jnp.bfloat16),
        "cross_q": scatter_about(key_list[10], (D, D), (16 * D) ** -0.5, 0.0546875, ((0, 32),)),
        "cross_kv": scatter_about(key_list[11], (D, 2 * D), D ** -0.5, 0.21875, ((0, 32),)),
        "cross_out": scatter_about(key_list[12], (D, D), (max(1, D * 55 // ENC_ROWS)) ** -0.5, 1.25, ((0, 32),)),
        "ln_ff": jnp.clip(1.0 + 0.18 * jax.random.normal(key_list[13], (D,), jnp.float32), 0.099609375, 1.8984375).astype(jnp.bfloat16),
        "ff_in": scatter_about(key_list[14], (D, FF), D ** -0.5, 0.21875, ((0, 32),)),
        "ff_out": scatter_about(key_list[15], (FF, D), FF ** -0.5, 0.109375, ((0, 32),)),
    }


@jax.custom_vjp
def low(v):
    return lax.optimization_barrier(v.astype(jnp.bfloat16)).astype(jnp.float32)

@jax.custom_vjp
def low_back(v):
    return v

def low_keep(v):
    return (low(v), None)

def low_pass(kept, grad):
    return (grad,)

def back_keep(v):
    return (v, None)

def back_low(kept, grad):
    return (low(grad),)
low.defvjp(low_keep, low_pass)
low_back.defvjp(back_keep, back_low)
EPS = 1e-06
NEG = -1e+30
HIGH = lax.Precision.HIGHEST

def bucket_limits():
    limits = []
    for target_bucket in range(1, 16):
        distance = 16
        while int(math.log(distance / 16.0) / math.log(8.0) * 16.0) < target_bucket:
            distance = distance + 1
        limits.append(distance)
    return limits

def bucket_table(length):
    positions = jnp.arange(length, dtype=jnp.int32)
    distance = jnp.maximum(positions[:, None] - positions[None, :], 0)
    larger = jnp.full_like(distance, 16)
    for limit_value in bucket_limits():
        larger = larger + (distance >= limit_value).astype(jnp.int32)
    return jnp.where(distance < 16, distance, jnp.minimum(larger, 31))

def normed(values, gain_vec):
    return values * lax.rsqrt(lax.optimization_barrier(jnp.mean(values * values, axis=-1, keepdims=True)) + EPS) * gain_vec

def gelu_fn(values):
    return jax.nn.gelu(values, approximate=True)

def matmul(left, right):
    return jnp.dot(left, right, precision=HIGH)

def both(values):
    return low_back(low(values))

def attention(queries, key_rows, value_rows, extra, allowed):
    query_rows = queries.shape[0]
    q_heads = queries.reshape(query_rows, HEADS, DK)
    key_heads = key_rows.reshape(key_rows.shape[0], HEADS, DK)
    value_heads = value_rows.reshape(value_rows.shape[0], HEADS, DK)
    scores = jnp.einsum('ihd,jhd->hij', q_heads, key_heads, precision=HIGH) + extra
    scores = low_back(scores)
    scores = jnp.where(allowed, scores, NEG)
    probs = low(jax.nn.softmax(scores, axis=-1))
    mixed = jnp.einsum('hij,jhd->ihd', probs, value_heads, precision=HIGH)
    return both(mixed.reshape(query_rows, HEADS * DK))

def layer(tokens, enc_rows, live_row, gain_self, bias_flat, selfq_w, selfkv_w, selfout_w, gain_cross, crossq_w, crosskv_w, crossout_w, gain_ff, ffin_w, ffout_w):
    tmax_rows = tokens.shape[0]
    model_width = tokens.shape[1]
    h_one = low(normed(tokens, gain_self))
    q_self = both(matmul(h_one, selfq_w))
    kv_self = both(matmul(h_one, selfkv_w))
    positions = jnp.arange(tmax_rows)
    extra = bias_flat.reshape(HEADS, BUCKETS)[:, bucket_table(tmax_rows)]
    allowed = positions[:, None] >= positions[None, :]
    att_self = attention(q_self, kv_self[:, :model_width], kv_self[:, model_width:], extra, allowed)
    x_one = tokens + low_back(matmul(att_self, selfout_w))
    h_two = low(normed(x_one, gain_cross))
    q_cross = both(matmul(h_two, crossq_w))
    kv_cross = both(matmul(enc_rows, crosskv_w))
    att_cross = attention(q_cross, kv_cross[:, :model_width], kv_cross[:, model_width:], 0.0, True)
    x_two = x_one + low_back(matmul(att_cross, crossout_w))
    h_three = low(normed(x_two, gain_ff))
    pre_act = low_back(matmul(h_three, ffin_w))
    act_low = low(gelu_fn(pre_act))
    return live_row[:, None] * (x_two + low_back(matmul(act_low, ffout_w)))

def reference(targets, passages, tgt_len, out_grad, ln_self, rel_bias, self_q, self_kv, self_out, ln_cross, cross_q, cross_kv, cross_out, ln_ff, ff_in, ff_out):
    weights = tuple((member.astype(jnp.float32) for member in (ln_self, rel_bias, self_q, self_kv, self_out, ln_cross, cross_q, cross_kv, cross_out, ln_ff, ff_in, ff_out)))
    live = (jnp.arange(TMAX)[None, :] < tgt_len[:, None]).astype(jnp.float32)

    def forward(tokens_all, passages_all, weight_set):

        def advance(carried, packed):
            tokens, enc_rows, live_row = packed
            return (carried, layer(tokens, enc_rows.astype(jnp.float32), live_row, *weight_set))
        return lax.scan(jax.checkpoint(advance), jnp.zeros((), jnp.float32), (tokens_all, passages_all, live))[1]
    block_out, pullback = jax.vjp(forward, targets, passages, weights)
    target_grad, passage_grad, grads = pullback(out_grad)
    return (block_out, target_grad, passage_grad, grads[0], grads[1], grads[2], grads[3], grads[4], grads[5], grads[6], grads[7], grads[8], grads[9], grads[10], grads[11])
```

```python
import functools
import math

import jax
import jax.numpy as jnp
from jax import lax
from jax.experimental import pallas as pl
from jax.experimental.pallas import tpu as pltpu
from jax.sharding import PartitionSpec as P

HEADS = 12
DK = 64
BUCKETS = 32
QUAD = 4
WIDE = QUAD * DK
EPS = 1e-06
NEG = -1e30
HIGH = lax.Precision.HIGHEST
BF = jnp.bfloat16
F32 = jnp.float32
PIECES = 8
SQ, SK, SV, SO, CQ, CK, CV, CO = range(PIECES)
ZDIM = 4


def up16(n):
    return (n + 15) // 16 * 16


def bucket_limits():
    limits = []
    for target_bucket in range(1, 16):
        distance = 16
        while int(math.log(distance / 16.0) / math.log(8.0) * 16.0) < target_bucket:
            distance = distance + 1
        limits.append(distance)
    return limits


def bucket_of(distance):
    larger = jnp.full_like(distance, 16)
    for limit_value in bucket_limits():
        larger = larger + (distance >= limit_value).astype(jnp.int32)
    return jnp.where(distance < 16, distance, jnp.minimum(larger, 31))


def iota(shape, axis):
    return lax.broadcasted_iota(jnp.int32, shape, axis)


def nn(a, b):
    return lax.dot_general(a, b, (((1,), (0,)), ((), ())), preferred_element_type=F32)


def nt(a, b):
    return lax.dot_general(a, b, (((1,), (1,)), ((), ())), preferred_element_type=F32)


def tn(a, b):
    return lax.dot_general(a, b, (((0,), (0,)), ((), ())), preferred_element_type=F32)


def nn_high(a, b):
    return lax.dot_general(
        a, b, (((1,), (0,)), ((), ())), preferred_element_type=F32, precision=HIGH
    )


def normed(v, gain):
    return v * lax.rsqrt(jnp.mean(v * v, axis=-1, keepdims=True) + EPS) * gain


def norm_back(v, gain, dy):
    s = lax.rsqrt(jnp.mean(v * v, axis=-1, keepdims=True) + EPS)
    dyg = dy * gain
    gain_grad = jnp.sum(dy * v * s, axis=0, keepdims=True)
    dv = s * dyg - v * (s * s * s) * jnp.mean(dyg * v, axis=-1, keepdims=True)
    return dv, gain_grad


def gelu_pair(u):
    cst = 0.7978845608028654
    cubic = 0.044715
    th = jnp.tanh(cst * (u + cubic * u * u * u))
    half = 0.5 * (1.0 + th)
    slope = half + 0.5 * u * (1.0 - th * th) * cst * (1.0 + 3.0 * cubic * u * u)
    return u * half, slope


class Sizes:
    def __init__(self, mesh_shape, width, rows, targets, shard, ff_shard, hidden):
        self.Z = ZDIM
        self.X = mesh_shape["dp"] // 2
        self.Y = mesh_shape["fsdp"] // self.Z
        self.D = width
        self.R = rows
        self.T = targets
        self.r = shard
        self.rb = up16(2 * shard)
        self.nh = width // 2
        self.rff = ff_shard
        self.rbf = up16(2 * ff_shard)
        self.rfi = up16(shard)
        self.inside = shard % 8 == 0
        self.hid = hidden


def sems(sz):
    return 13 * sz.Y * sz.Z + 20 * (sz.X + sz.Y + sz.Z) + 8 * sz.X * sz.Y


def layout(sz):
    X, Y, Z, D, T, R = sz.X, sz.Y, sz.Z, sz.D, sz.T, sz.R
    rb, nh, rbf, rfi, hid = sz.rb, sz.nh, sz.rbf, sz.rfi, sz.hid
    half = PIECES // 2
    V = pltpu.VMEM
    sums = dict(
        rc=V((PIECES, X, Y, Z, rb, nh), BF),
        r1a=V((half, X - 1, Y, Z, rb, nh), BF),
        r1b=V((half, Y - 1, X, Z, rb, nh), BF),
        r2a=V((half, Y - 1, Z, rb, nh), BF),
        r2b=V((half, X - 1, Z, rb, nh), BF),
        rz=V((PIECES, Z - 1, rb, nh), BF),
    )
    return dict(
        **(sums if sz.inside else {}),
        gw=V((PIECES, 2, X, Y, Z, rb, nh), BF),
        w=V((PIECES, D, D), BF),
        acc=V((D, D), F32),
        lift=V((Y * Z * sz.r if sz.r % 8 else 8, D), F32),
        cell=V((max(rb, rbf, rfi), max(nh, hid)), F32),
        smb=V((2, X, Y, Z, 16, 128), BF),
        gain=V((16, D), F32),
        bias=V((HEADS // QUAD, WIDE, T), F32),
        spread=V((128, D), F32),
        mask=V((WIDE, WIDE), BF),
        pas=V((Y * Z, R, D), BF),
        kv=V((Y * Z, R, 2 * D), BF),
        h1=V((T, D), BF),
        qs=V((T, D), BF),
        ks=V((T, D), BF),
        vs=V((T, D), BF),
        os=V((T, D), BF),
        ps=V((HEADS // QUAD, WIDE, T), F32),
        x1=V((T, D), F32),
        h2=V((T, D), BF),
        x2=V((T, D), F32),
        oc=V((T, D), BF),
        dx=V((T, D), F32),
        qc=V((Z, Y, T, D), BF),
        h3=V((Z, Y, T, D), BF),
        g3=V((Z, Y, T, D), BF),
        do=V((Z, Y, T, D), BF),
        dr=V((Z, Y, 8, D), F32),
        po=V((Y, Z, T, D), BF),
        pst=V((Y, Z, T, 128), F32),
        ryo=V((Y - 1, Z, T, D), BF),
        ryst=V((Y - 1, Z, T, 128), F32),
        rzo=V((Z - 1, T, D), BF),
        rzst=V((Z - 1, T, 128), F32),
        py=V((Y, Z, T, D), BF),
        ryy=V((Y - 1, Z, T, D), BF),
        rzy=V((Z - 1, T, D), BF),
        fog=V((2, X, rbf, nh), BF),
        fo=V((hid, D), BF),
        fz=V((Z, Y, rfi, hid), BF),
        fig=V((2, X, Y, Z, rfi, hid), BF),
        fi=V((D, hid), BF),
        gl=V((Y, Z * T, hid), BF),
        du=V((Y, Z * T, hid), BF),
        gfo=V((2, X, rbf, nh), BF),
        rfo1=V((X, rbf, nh), BF),
        rfo2=V((X - 1, rbf, nh), BF),
        gfi=V((2, X, Y, Z, rfi, hid), BF),
        rfi1=V((X, Y, Z, rfi, hid), BF),
        rfi2=V((X - 1, Y, Z, rfi, hid), BF),
        rfi3=V((Y - 1, Z, rfi, hid), BF),
        rfi4=V((Z - 1, Y, rfi, hid), BF),
        sm=V((8, D), F32),
        rsm=V((1 + (X - 1) + (Y - 1) + (Z - 1), 8, D), F32),
        ssem=pltpu.SemaphoreType.DMA((sems(sz),)),
        rsem=pltpu.SemaphoreType.DMA((sems(sz),)),
        lsem=pltpu.SemaphoreType.DMA((1 + Y * Z,)),
    )


INPUTS = ("tok", "pas_in", "live", "og", "small", "sq", "skv", "so", "cq", "ckv", "co", "fi_in", "fo_in")
OUTPUTS = (
    "bo", "tg", "pg", "g_ls", "g_rb", "g_sq", "g_skv", "g_so",
    "g_lc", "g_cq", "g_ckv", "g_co", "g_lf", "g_fi", "g_fo",
)


def block_kernel(sz, names, *refs):
    n_in, n_out = len(INPUTS), len(OUTPUTS)
    m = dict(zip(INPUTS, refs[:n_in]))
    m.update(zip(OUTPUTS, refs[n_in : n_in + n_out]))
    m.update(zip(names, refs[n_in + n_out :]))
    X, Y, Z, D, T, R = sz.X, sz.Y, sz.Z, sz.D, sz.T, sz.R
    r, rb, nh, rff, rbf, rfi, hid = sz.r, sz.rb, sz.nh, sz.rff, sz.rbf, sz.rfi, sz.hid
    NQ = HEADS // QUAD
    YZ = Y * Z
    dp = lax.axis_index("dp")
    fs = lax.axis_index("fsdp")
    x, c = dp // 2, dp % 2
    z, y = fs // Y, fs % Y
    oth = 1 - c

    def xs(b):
        return (x + b) % X

    def ys(b):
        return (y + b) % Y

    def zs(b):
        return (z + b) % Z

    def dev(x_=None, c_=None, y_=None, z_=None):
        x_ = x if x_ is None else x_
        c_ = c if c_ is None else c_
        y_ = y if y_ is None else y_
        z_ = z if z_ is None else z_
        return (x_ * 2 + c_, z_ * Y + y_)

    ssem, rsem, lsem = m["ssem"], m["rsem"], m["lsem"]
    n_sems = sems(sz)
    used = [0]
    pending = []

    def take(n=1):
        at = used[0]
        used[0] += n
        assert used[0] <= n_sems
        return at

    def copy_at(i, src, dst, to):
        return pltpu.make_async_remote_copy(
            src_ref=src, dst_ref=dst, send_sem=ssem.at[i], recv_sem=rsem.at[i],
            device_id=to, device_id_type=pl.DeviceIdType.MESH,
        )

    def send(src, dst, to):
        cp = copy_at(take(), src, dst, to)
        cp.start()
        pending.append(cp)
        return cp

    def got(cps):
        for cp in cps:
            cp.wait_recv()

    def sent(cps):
        for cp in cps:
            cp.wait_send()
        pending[:] = [cp for cp in pending if all(cp is not done for done in cps)]

    def drain():
        sent(list(pending))

    partners = [dev(c_=oth)]
    partners += [dev(x_=xs(b)) for b in range(1, X)]
    partners += [dev(y_=ys(b)) for b in range(1, Y)]
    partners += [dev(z_=zs(b)) for b in range(1, Z)]
    bar = pltpu.get_barrier_semaphore()
    for p in partners:
        pl.semaphore_signal(bar, inc=1, device_id=p, device_id_type=pl.DeviceIdType.MESH)
    load_pas = pltpu.make_async_copy(m["pas_in"], m["pas"], lsem.at[0])
    load_pas.start()
    pl.semaphore_wait(bar, len(partners))

    mask = m["mask"]
    mask[...] = (iota((WIDE, WIDE), 0) // DK == iota((WIDE, WIDE), 1) // DK).astype(F32).astype(BF)

    def stack4(v):
        return jnp.concatenate([v, v, v, v], axis=0) * mask[...]

    def fold4(u):
        lane = iota((T, WIDE), 1)
        out = u[0:T]
        for h in range(1, QUAD):
            out = jnp.where(lane >= h * DK, u[h * T : (h + 1) * T], out)
        return out

    def quad(t):
        return slice(t * WIDE, (t + 1) * WIDE)

    cell, lift = m["cell"], m["lift"]

    def put_halves(dst, left, right, rows, total):
        if rows % 8 == 0 and 2 * rows == total:
            dst[...] = jnp.concatenate([left, right], axis=0).astype(BF)
        else:
            cols = left.shape[1]
            cell[0:total, 0:cols] = jnp.zeros((total, cols), F32)
            cell[0:rows, 0:cols] = left
            cell[rows : 2 * rows, 0:cols] = right
            dst[...] = cell[0:total, 0:cols].astype(BF)

    def get_halves(v, rows):
        if rows % 8 == 0:
            return v[0:rows], v[rows : 2 * rows]
        cell[0 : v.shape[0], 0 : v.shape[1]] = v
        return cell[0:rows, 0 : v.shape[1]], cell[rows : 2 * rows, 0 : v.shape[1]]

    def ag_z(buf):
        return [
            send(buf.at[c, x, y, z], buf.at[c, x, y, z], dev(z_=zs(a))) for a in range(1, Z)
        ]

    def line_to(buf, y_first):
        if y_first:
            return [send(buf.at[c, x, y], buf.at[c, x, y], dev(y_=ys(b))) for b in range(1, Y)]
        return [send(buf.at[c, x, y], buf.at[c, x, y], dev(x_=xs(b))) for b in range(1, X)]

    def ag_t2(buf, y_first):
        out = []
        if y_first:
            for b in range(1, Y):
                for d in range(1, X):
                    out.append(send(buf.at[c, x, ys(b)], buf.at[c, x, ys(b)], dev(x_=xs(d))))
        else:
            for b in range(1, X):
                for d in range(1, Y):
                    out.append(send(buf.at[c, xs(b), y], buf.at[c, xs(b), y], dev(y_=ys(d))))
        return out

    def ag_core(buf):
        return [send(buf.at[c], buf.at[c], dev(c_=oth))]

    gw, w, smb = m["gw"], m["w"], m["smb"]
    smb[c, x, y, z] = m["small"][...]
    sources = (
        (m["sq"], 0), (m["skv"], 0), (m["skv"], D), (m["so"], 0),
        (m["cq"], 0), (m["ckv"], 0), (m["ckv"], D), (m["co"], 0),
    )
    for p, (ref, off) in enumerate(sources):
        v = ref[:, off : off + D].astype(F32)
        put_halves(gw.at[p, c, x, y, z], v[:, 0:nh], v[:, nh:D], r, rb)
    steps = [[(smb, True), (gw.at[0], True)]]
    steps += [[(gw.at[p], p % 2 == 0)] for p in range(1, PIECES)]
    zc = [[ag_z(buf) for buf, _ in group] for group in steps]

    g3 = m["g3"]
    live = m["live"][:, 0:1]
    g3[z, y] = (live * m["og"][...]).astype(BF)

    def act_start(base, bufs):
        for n, buf in enumerate(bufs):
            for a in range(1, Z):
                copy_at(base + n * YZ + a, buf.at[z, y], buf.at[z, y], dev(z_=zs(a))).start()

    def act_forward(base, bufs, a):
        zi = zs(a)
        for n, buf in enumerate(bufs):
            for b in range(1, Y):
                copy_at(
                    base + n * YZ + b * Z + (Z - a) % Z, buf.at[zi, y], buf.at[zi, y], dev(y_=ys(b))
                ).start()

    def act_wait(base, bufs, t):
        at = base + (Y - t // Z) % Y * Z + (Z - t % Z) % Z
        for n, buf in enumerate(bufs):
            copy_at(at + n * YZ, buf.at[z, y], buf.at[z, y], dev(z_=zs(1))).wait_recv()

    def act_done(base, bufs):
        for n, buf in enumerate(bufs):
            for t in range(1, YZ):
                copy_at(base + n * YZ + t, buf.at[z, y], buf.at[z, y], dev(z_=zs(1))).wait_send()

    g3_base = take(YZ)
    act_start(g3_base, [g3])
    fog, fo, fz, fig, fi = m["fog"], m["fo"], m["fz"], m["fig"], m["fi"]
    fz[z] = m["fi_in"][pl.ds(z * Y, Y)]
    fi_z = [
        send(m["fi_in"].at[pl.ds(zs(a) * Y, Y)], fz.at[z], dev(z_=zs(a))) for a in range(1, Z)
    ]
    vfo = m["fo_in"][...].astype(F32)
    put_halves(fog.at[c, x], vfo[:, 0:nh], vfo[:, nh:D], rff, rbf)
    fo_x = [send(fog.at[c, x], fog.at[c, x], dev(x_=xs(b))) for b in range(1, X)]

    spread = m["spread"]
    lane = iota((128, D), 1)
    row = iota((128, D), 0)
    spread[...] = ((lane >= row * DK) & (lane < row * DK + DK)).astype(F32)
    tlane = iota((T, 128), 1)

    def unpack(p):
        group = 2 * Y * r

        def body(g, carry):
            x_ = g // (2 * (Z // 2))
            c_ = (g // (Z // 2)) % 2
            zp = g % (Z // 2)
            lefts, rights = [], []
            at = 0
            for dz in range(2):
                for yy in range(Y):
                    lo, hi = get_halves(gw[p, c_, x_, yy, 2 * zp + dz].astype(F32), r)
                    if r % 8 == 0:
                        lefts.append(lo)
                        rights.append(hi)
                    else:
                        lift[at : at + r, 0:nh] = lo
                        lift[at : at + r, nh:D] = hi
                    at += r
            rows = pl.ds(pl.multiple_of(g * group, 16), group)
            if r % 8 == 0:
                w[p, rows, 0:nh] = jnp.concatenate(lefts, axis=0).astype(BF)
                w[p, rows, nh:D] = jnp.concatenate(rights, axis=0).astype(BF)
            else:
                w[p, rows, :] = lift[0:group, :].astype(BF)
            return carry

        lax.fori_loop(0, X * 2 * (Z // 2), body, 0)

    gain = m["gain"]
    bias = m["bias"]
    rbs = HEADS * BUCKETS // (2 * X * YZ)

    def read_small():
        gain[...] = jnp.zeros_like(gain)
        flat = HEADS * BUCKETS

        def body(k, tot):
            c_ = (k // YZ) % 2
            x_ = k // (2 * YZ)
            z_ = (k % YZ) // Y
            y_ = k % Y
            b = smb[c_, x_, y_, z_]
            l0, n0 = iota((128, D), 0), iota((128, D), 1)
            place = ((n0 - l0 == k * r) & (l0 < r)).astype(F32).astype(BF)
            gain[...] += nn(b, place)
            l1, n1 = iota((128, flat), 0), iota((128, flat), 1)
            place1 = ((n1 - l1 == k * rbs) & (l1 < rbs)).astype(F32).astype(BF)
            return tot + nn(b, place1)

        tot = lax.fori_loop(0, 2 * X * YZ, body, jnp.zeros((16, flat), F32))
        per = jnp.broadcast_to(tot[3:4, :], (16, flat))
        h0, n0 = iota((16, flat), 0), iota((16, flat), 1)
        per = jnp.where((n0 >= h0 * BUCKETS) & (n0 < h0 * BUCKETS + BUCKETS), per, 0.0)
        nb, mb = iota((flat, 128), 0), iota((flat, 128), 1)
        dist = jnp.where(mb == 0, 0, 128 - mb)
        hot = ((nb & (BUCKETS - 1)) == bucket_of(dist)).astype(F32).astype(BF)
        table = nn(per.astype(BF), hot)
        for h in range(HEADS):
            wide = jnp.broadcast_to(table[h : h + 1, :], (T, 128))
            rolled = pltpu.roll(wide, 0, 1, stride=1, stride_axis=0)
            bias[h // QUAD, (h % QUAD) * T : (h % QUAD + 1) * T, :] = rolled[:, 0:T]

    tok = m["tok"]

    def self_forward():
        m["h1"][...] = normed(tok[...], gain[0:1, :]).astype(BF)
        h1 = m["h1"][...]
        m["qs"][...] = nn(h1, w[SQ]).astype(BF)
        m["ks"][...] = nn(h1, w[SK]).astype(BF)
        m["vs"][...] = nn(h1, w[SV]).astype(BF)
        allowed = iota((WIDE, T), 1) <= (iota((WIDE, T), 0) & (T - 1))
        for t in range(NQ):
            s = nt(stack4(m["qs"][:, quad(t)]), m["ks"][:, quad(t)]) + bias[t]
            s = jnp.where(allowed, s, NEG)
            e = jnp.exp(s - jnp.max(s, axis=1, keepdims=True))
            pr = e / jnp.sum(e, axis=1, keepdims=True)
            m["ps"][t] = pr
            m["os"][:, quad(t)] = fold4(nn(pr.astype(BF), m["vs"][:, quad(t)])).astype(BF)

    qc = m["qc"]
    qc_base = take(YZ)

    def self_out():
        x1 = tok[...] + nn(m["os"][...], w[SO])
        m["x1"][...] = x1
        m["h2"][...] = normed(x1, gain[1:2, :]).astype(BF)

    def cross_query():
        qc[z, y] = nn(m["h2"][...], w[CQ]).astype(BF)
        act_start(qc_base, [qc])

    kv, pas = m["kv"], m["pas"]

    def project(p, off):
        def body(q, carry):
            kv[q, :, off : off + D] = nn(pas[q], w[p]).astype(BF)
            return carry

        lax.fori_loop(0, YZ, body, 0)

    def g3_forward():
        for a in range(Z):
            if a:
                act_wait(g3_base, [g3], a)
            act_forward(g3_base, [g3], a)

    def ff_unpack():
        for x_ in range(X):
            for c_ in range(2):
                lo, hi = get_halves(fog[c_, x_].astype(F32), rff)
                rows = slice((x_ * 2 + c_) * rff, (x_ * 2 + c_ + 1) * rff)
                if rff % 16 == 0:
                    fo[rows, 0:nh] = lo.astype(BF)
                    fo[rows, nh:D] = hi.astype(BF)
                else:
                    m["acc"][rows, 0:nh] = lo
                    m["acc"][rows, nh:D] = hi
        if rff % 16:
            fo[...] = m["acc"][0:hid, 0:D].astype(BF)
        group = 2 * Y * r

        def body(g, carry):
            x_ = g // (2 * (Z // 2))
            c_ = (g // (Z // 2)) % 2
            zp = g % (Z // 2)
            parts = []
            at = 0
            for dz in range(2):
                for yy in range(Y):
                    v = fig[c_, x_, yy, 2 * zp + dz].astype(F32)
                    if r % 8 == 0:
                        parts.append(v[0:r])
                    else:
                        cell[0:rfi, 0:hid] = v
                        lift[at : at + r, 0:hid] = cell[0:r, 0:hid]
                    at += r
            rows = pl.ds(pl.multiple_of(g * group, 16), group)
            if r % 8 == 0:
                fi[rows, :] = jnp.concatenate(parts, axis=0).astype(BF)
            else:
                fi[rows, :] = lift[0:group, 0:hid].astype(BF)
            return carry

        lax.fori_loop(0, X * 2 * (Z // 2), body, 0)

    ff_state = {}

    def ff_step(k):
        if k == 0:
            got(fi_z)
            fig[c, x, y] = fz[:, pl.ds(y, 1)].reshape(Z, rfi, hid)
            ff_state["y"] = [
                send(fz.at[:, ys(b)], fig.at[c, x, y], dev(y_=ys(b))) for b in range(1, Y)
            ]
            got(fo_x)
            ff_state["fo"] = [send(fog.at[c], fog.at[c], dev(c_=oth))]
        elif k == 1:
            got(ff_state["y"])
            ff_state["x"] = [
                send(fig.at[c, x], fig.at[c, x], dev(x_=xs(b))) for b in range(1, X)
            ]
        elif k == 2:
            got(ff_state["x"])
            ff_state["core"] = [send(fig.at[c], fig.at[c], dev(c_=oth))]
        elif k == 3:
            got(ff_state["core"])
            got(ff_state["fo"])
            ff_unpack()

    def after(p):
        if p == 0:
            read_small()
        elif p == SV:
            self_forward()
        elif p == SO:
            self_out()
        elif p == CQ:
            cross_query()
        elif p == CK:
            load_pas.wait()
            project(CK, 0)
        elif p == CV:
            project(CV, D)

    sc, tc, cc = {}, {}, {}
    n_steps = len(steps)
    for s in range(n_steps + 3):
        if s < n_steps:
            sc[s], tc[s] = [], []
            for cps, (buf, y_first) in zip(zc[s], steps[s]):
                got(cps)
                sc[s].append(line_to(buf, y_first))
                tc[s].append(line_to(buf, not y_first))
        if 0 <= s - 1 < n_steps:
            for n, (buf, y_first) in enumerate(steps[s - 1]):
                got(sc[s - 1][n])
                tc[s - 1][n] = tc[s - 1][n] + ag_t2(buf, y_first)
        if 0 <= s - 2 < n_steps:
            cc[s - 2] = []
            for n, (buf, y_first) in enumerate(steps[s - 2]):
                got(tc[s - 2][n])
                cc[s - 2].append(ag_core(buf))
        if s == 4:
            g3_forward()
            ff_step(0)
        elif s == 6:
            ff_step(1)
        elif s == 8:
            ff_step(2)
        if 0 <= s - 3 < n_steps:
            for cps in cc[s - 3]:
                got(cps)
            unpack(s - 3)
            after(s - 3)
    ff_step(3)
    drain()

    po, pst, ryo, ryst, rzo, rzst = (m[k] for k in ("po", "pst", "ryo", "ryst", "rzo", "rzst"))

    def rs_y_base():
        return take((Y - 1) * Z)

    def rs_y_send(base, src, dst, b, a):
        zi = zs(a)
        copy_at(base + (b - 1) * Z + a, src.at[b, zi], dst.at[b - 1, zi], dev(y_=ys(b))).start()

    def rs_y_wait(base, src, dst, b, a):
        copy_at(base + (b - 1) * Z + a, src.at[b, 0], dst.at[b - 1, 0], dev(y_=ys(1))).wait_recv()

    def rs_y_done(base, src, dst):
        for b in range(1, Y):
            for a in range(Z):
                copy_at(
                    base + (b - 1) * Z + a, src.at[b, 0], dst.at[b - 1, 0], dev(y_=ys(1))
                ).wait_send()

    yo_base, yst_base = rs_y_base(), rs_y_base()

    def attend(t, carry):
        a = t % Z
        b = t // Z
        zi = zs(a)
        yi = ys(b)
        qi = zi * Y + yi

        @pl.when(t > 0)
        def _():
            act_wait(qc_base, [qc], t)

        @pl.when(t < Z)
        def _():
            act_forward(qc_base, [qc], a)

        st = jnp.zeros((T, 128), F32)
        for k in range(NQ):
            qb = stack4(qc[zi, yi, :, quad(k)])
            s = nt(qb, kv[qi, :, quad(k)])
            top = jnp.max(s, axis=1, keepdims=True)
            e = jnp.exp(s - top)
            tot = jnp.sum(e, axis=1, keepdims=True)
            u = nn(e.astype(BF), kv[qi, :, D + k * WIDE : D + (k + 1) * WIDE])
            po[b, zi, :, quad(k)] = fold4(u * (1.0 / tot)).astype(BF)
            lse = top + jnp.log(tot)
            for h in range(QUAD):
                st = jnp.where(tlane == k * QUAD + h, lse[h * T : (h + 1) * T], st)
        pst[b, zi] = st

        @pl.when(t >= Z)
        def _():
            rs_y_send(yo_base, po, ryo, b, a)
            rs_y_send(yst_base, pst, ryst, b, a)

        return carry

    lax.fori_loop(0, YZ, attend, 0)

    def merge(parts):
        top = parts[0][1]
        for _, st in parts[1:]:
            top = jnp.maximum(top, st)
        ws = [jnp.exp(st - top) for _, st in parts]
        tot = ws[0]
        for v in ws[1:]:
            tot = tot + v
        out = jnp.zeros((T, D), F32)
        for (o, _), v in zip(parts, ws):
            out = out + nn_high(v / tot, spread[...]) * o.astype(F32)
        return out, top + jnp.log(tot)

    zo = []
    for a in range(1, Z):
        zi = zs(a)
        for b in range(1, Y):
            rs_y_wait(yo_base, po, ryo, b, a)
            rs_y_wait(yst_base, pst, ryst, b, a)
        o, st = merge([(po[0, zi], pst[0, zi])] + [(ryo[b - 1, zi], ryst[b - 1, zi]) for b in range(1, Y)])
        po[0, zi] = o.astype(BF)
        pst[0, zi] = st
        zo.append(send(po.at[0, zi], rzo.at[a - 1], dev(z_=zi)))
        zo.append(send(pst.at[0, zi], rzst.at[a - 1], dev(z_=zi)))
    for b in range(1, Y):
        rs_y_wait(yo_base, po, ryo, b, 0)
        rs_y_wait(yst_base, pst, ryst, b, 0)
    got(zo)
    o, lse = merge(
        [(po[0, z], pst[0, z])]
        + [(ryo[b - 1, z], ryst[b - 1, z]) for b in range(1, Y)]
        + [(rzo[a - 1], rzst[a - 1]) for a in range(1, Z)]
    )
    m["oc"][...] = o.astype(BF)
    m["pst"][0, z] = lse
    x2 = m["x1"][...] + nn(m["oc"][...], w[CO])
    m["x2"][...] = x2
    h3 = m["h3"]
    h3[z, y] = normed(x2, gain[2:3, :]).astype(BF)
    h3_base = take(YZ)
    act_start(h3_base, [h3])
    act_done(qc_base, [qc])
    rs_y_done(yo_base, po, ryo)
    rs_y_done(yst_base, pst, ryst)

    ph, ryh, rzh = po, ryo, rzo
    py, ryy, rzy = (m[k] for k in ("py", "ryy", "rzy"))
    sent(zo)
    gl, du = m["gl"], m["du"]
    yh = []
    for b in range(Y):
        yi = ys(b)
        for a in range(Z):
            if b or a:
                act_wait(h3_base, [h3], b * Z + a)
            if b == 0:
                act_forward(h3_base, [h3], a)
            else:
                act_wait(g3_base, [g3], b * Z + a)
        hb = h3[:, pl.ds(yi, 1)].reshape(Z * T, D)
        gb = g3[:, pl.ds(yi, 1)].reshape(Z * T, D)
        u = nn(hb, fi[...])
        act, slope = gelu_pair(u)
        gl[b] = act.astype(BF)
        du[b] = (nt(gb, fo[...]) * slope).astype(BF)
        ph[b] = nt(du[b], fi[...]).astype(BF).reshape(Z, T, D)
        if b:
            yh.append(send(ph.at[b], ryh.at[b - 1], dev(y_=yi)))
    yy = []
    for b in range(Y):
        py[b] = nn(gl[b], fo[...]).astype(BF).reshape(Z, T, D)
        if b:
            yy.append(send(py.at[b], ryy.at[b - 1], dev(y_=ys(b))))
    act_done(h3_base, [h3])
    act_done(g3_base, [g3])

    def rs_z_stage(part, ry, rzb):
        cps = []
        for a in range(1, Z):
            zi = zs(a)
            tot = part[0, zi].astype(F32)
            for b in range(1, Y):
                tot = tot + ry[b - 1, zi].astype(F32)
            part[0, zi] = tot.astype(BF)
            cps.append(send(part.at[0, zi], rzb.at[a - 1], dev(z_=zi)))
        return cps

    def rs_total(part, ry, rzb):
        tot = part[0, z].astype(F32)
        for b in range(1, Y):
            tot = tot + ry[b - 1, z].astype(F32)
        for a in range(1, Z):
            tot = tot + rzb[a - 1].astype(F32)
        return tot

    got(yh)
    zh = rs_z_stage(ph, ryh, rzh)

    acc = m["acc"]
    gfo, rfo1, rfo2 = m["gfo"], m["rfo1"], m["rfo2"]
    gfi, rfi1, rfi2, rfi3, rfi4 = (m[k] for k in ("gfi", "rfi1", "rfi2", "rfi3", "rfi4"))

    def add_to(dst, src):
        dst[...] = (dst[...].astype(F32) + src[...].astype(F32)).astype(BF)

    def ff_out_grad():
        for b in range(Y):
            v = tn(gl[b], g3[:, pl.ds(ys(b), 1)].reshape(Z * T, D))
            if b == 0:
                acc[0:hid, 0:D] = v
            else:
                acc[0:hid, 0:D] += v
        for x_ in range(X):
            for c_ in range(2):
                lo = (x_ * 2 + c_) * rff
                put_halves(
                    gfo.at[c_, x_], acc[lo : lo + rff, 0:nh], acc[lo : lo + rff, nh:D], rff, rbf
                )
        return [send(gfo.at[oth], rfo1, dev(c_=oth))]

    def ff_in_grad():
        for b in range(Y):
            v = tn(h3[:, pl.ds(ys(b), 1)].reshape(Z * T, D), du[b])
            if b == 0:
                acc[:, 0:hid] = v
            else:
                acc[:, 0:hid] += v
        group = YZ * r

        def body(k, carry):
            x_ = k // 2
            c_ = k % 2
            if r % 8:
                lift[0:group, 0:hid] = acc[pl.ds(pl.multiple_of(k * group, 8), group), 0:hid]
            for z_ in range(Z):
                for y_ in range(Y):
                    at = (z_ * Y + y_) * r
                    if r % 8 == 0:
                        v = acc[pl.ds(pl.multiple_of(k * group + at, 8), r), 0:hid]
                        pad = jnp.zeros((rfi - r, hid), F32)
                        gfi[c_, x_, y_, z_] = jnp.concatenate([v, pad], axis=0).astype(BF)
                    else:
                        cell[0:rfi, 0:hid] = jnp.zeros((rfi, hid), F32)
                        cell[0:r, 0:hid] = lift[at : at + r, 0:hid]
                        gfi[c_, x_, y_, z_] = cell[0:rfi, 0:hid].astype(BF)
            return carry

        lax.fori_loop(0, 2 * X, body, 0)
        return [send(gfi.at[oth], rfi1, dev(c_=oth))]

    def ff_out_x(cps):
        got(cps)
        for x_ in range(X):
            add_to(gfo.at[c, x_], rfo1.at[x_])
        return [send(gfo.at[c, xs(b)], rfo2.at[b - 1], dev(x_=xs(b))) for b in range(1, X)]

    def ff_out_end(cps):
        got(cps)
        v = gfo[c, x].astype(F32)
        for b in range(1, X):
            v = v + rfo2[b - 1].astype(F32)
        lo, hi = get_halves(v, rff)
        m["g_fo"][:, 0:nh] = lo
        m["g_fo"][:, nh:D] = hi

    def ff_in_x(cps):
        got(cps)
        for x_ in range(X):
            for y_ in range(Y):
                add_to(gfi.at[c, x_, y_], rfi1.at[x_, y_])
        return [send(gfi.at[c, xs(b)], rfi2.at[b - 1], dev(x_=xs(b))) for b in range(1, X)]

    def ff_in_y(cps):
        got(cps)
        for b in range(1, X):
            for y_ in range(Y):
                add_to(gfi.at[c, x, y_], rfi2.at[b - 1, y_])
        return [send(gfi.at[c, x, ys(b)], rfi3.at[b - 1], dev(y_=ys(b))) for b in range(1, Y)]

    def ff_in_z(cps):
        got(cps)
        out = []
        for a in range(1, Z):
            zi = zs(a)
            out.append(send(gfi.at[c, x, y, zi], rfi4.at[a - 1, 0], dev(z_=zi)))
            for b in range(1, Y):
                out.append(send(rfi3.at[b - 1, zi], rfi4.at[a - 1, b], dev(z_=zi)))
        return out

    def ff_in_end(cps):
        got(cps)
        for a in range(Z):
            for b in range(Y):
                j = zs(Z - a) * Y + ys(Y - b)
                if a:
                    v = rfi4[a - 1, b]
                elif b:
                    v = rfi3[b - 1, z]
                else:
                    v = gfi[c, x, y, z]
                v = v.astype(F32)
                if r % 8 == 0:
                    m["g_fi"][j] = v[0:r]
                else:
                    cell[0:rfi, 0:hid] = v
                    m["g_fi"][j] = cell[0:r, 0:hid]

    rc, r1a, r1b, r2a, r2b, rz = (m.get(k) for k in ("rc", "r1a", "r1b", "r2a", "r2b", "rz"))

    def pack_grad(p):
        group = YZ * r
        if not sz.inside:
            name, off = targets[p]
            out = m[name].at[:, off : off + D]
            cp = pltpu.make_async_copy(acc, out, lsem.at[0])
            cp.start()
            cp.wait()
            return None

        def body(k, carry):
            x_ = k // 2
            c_ = k % 2
            for z_ in range(Z):
                for y_ in range(Y):
                    rows = pl.ds(pl.multiple_of(k * group + (z_ * Y + y_) * r, 8), r)
                    left, right = acc[rows, 0:nh], acc[rows, nh:D]
                    put_halves(gw.at[p, c_, x_, y_, z_], left, right, r, rb)
            return carry

        lax.fori_loop(0, 2 * X, body, 0)
        return [send(gw.at[p, oth], rc.at[p], dev(c_=oth))]

    def rs_first(p, cps):
        got(cps)

        def body(k, carry):
            x_ = k // Y
            y_ = k % Y
            add_to(gw.at[p, c, x_, y_], rc.at[p, x_, y_])
            return carry

        lax.fori_loop(0, X * Y, body, 0)
        if p % 2 == 0:
            return [
                send(gw.at[p, c, xs(b)], r1a.at[p // 2, b - 1], dev(x_=xs(b))) for b in range(1, X)
            ]
        return [
            send(gw.at[p, c, :, ys(b)], r1b.at[p // 2, b - 1], dev(y_=ys(b))) for b in range(1, Y)
        ]

    def rs_second(p, cps):
        got(cps)
        if p % 2 == 0:
            for b in range(1, X):
                for y_ in range(Y):
                    add_to(gw.at[p, c, x, y_], r1a.at[p // 2, b - 1, y_])
            return [
                send(gw.at[p, c, x, ys(b)], r2a.at[p // 2, b - 1], dev(y_=ys(b)))
                for b in range(1, Y)
            ]
        for b in range(1, Y):
            for x_ in range(X):
                add_to(gw.at[p, c, x_, y], r1b.at[p // 2, b - 1, x_])
        return [
            send(gw.at[p, c, xs(b), y], r2b.at[p // 2, b - 1], dev(x_=xs(b))) for b in range(1, X)
        ]

    def rs_third(p, cps):
        got(cps)
        if p % 2 == 0:
            for b in range(1, Y):
                add_to(gw.at[p, c, x, y], r2a.at[p // 2, b - 1])
        else:
            for b in range(1, X):
                add_to(gw.at[p, c, x, y], r2b.at[p // 2, b - 1])
        return [
            send(gw.at[p, c, x, y, zs(a)], rz.at[p, a - 1], dev(z_=zs(a))) for a in range(1, Z)
        ]

    targets = {
        SQ: ("g_sq", 0), SK: ("g_skv", 0), SV: ("g_skv", D), SO: ("g_so", 0),
        CQ: ("g_cq", 0), CK: ("g_ckv", 0), CV: ("g_ckv", D), CO: ("g_co", 0),
    }

    def rs_last(p, cps):
        got(cps)
        v = gw[p, c, x, y, z].astype(F32)
        for a in range(1, Z):
            v = v + rz[p, a - 1].astype(F32)
        lo, hi = get_halves(v, r)
        name, off = targets[p]
        m[name][:, off : off + nh] = lo
        m[name][:, off + nh : off + D] = hi

    stages = (rs_first, rs_second, rs_third, rs_last) if sz.inside else ()
    moving = {}

    def grad_of(p, lhs, rhs):
        acc[...] = tn(lhs, rhs)
        grad_out(p)

    def grad_out(p):
        moving[p] = (0, pack_grad(p))

    def push(p):
        k, cps = moving[p]
        if k < len(stages):
            moving[p] = (k + 1, stages[k](p, cps))

    def push_all(ps):
        for p in ps:
            push(p)

    fo_c = ff_out_grad()
    fi_c = ff_in_grad()
    got(zh)
    sm = m["sm"]
    sm[...] = jnp.zeros_like(sm)
    dh3 = rs_total(ph, ryh, rzh)
    dv, gg = norm_back(m["x2"][...], gain[2:3, :], dh3)
    sm[2:3, :] = gg
    dx2 = live * m["og"][...] + dv
    m["dx"][...] = dx2
    dx2l = dx2.astype(BF)
    doc = nt(dx2l, w[CO]).astype(BF)
    do, dr = m["do"], m["dr"]
    do[z, y] = doc
    pick = iota((T, D), 0) == (iota((T, D), 1) & (T - 1))

    def as_row(st):
        return jnp.sum(jnp.where(pick, nn_high(st, spread[...]), 0.0), axis=0, keepdims=True)

    prod = doc.astype(F32) * m["oc"][...].astype(F32)
    delta = lax.dot_general(
        prod, spread[...], (((1,), (1,)), ((), ())), preferred_element_type=F32, precision=HIGH
    )
    dr[z, y] = jnp.zeros((8, D), F32)
    dr[z, y, 0:1, :] = as_row(m["pst"][0, z])
    dr[z, y, 1:2, :] = as_row(delta)
    do_base = take(2 * YZ)
    act_start(do_base, [do, dr])
    grad_of(CO, m["oc"][...], dx2l)
    fo_x2 = ff_out_x(fo_c)
    fi_x2 = ff_in_x(fi_c)
    got(yy)
    zy = rs_z_stage(py, ryy, rzy)

    pq, ryq, rzq = po, ryo, rzo
    sent(yh + zh)
    yq_base = rs_y_base()

    def attend_back(t, carry):
        a = t % Z
        b = t // Z
        zi = zs(a)
        yi = ys(b)
        qi = zi * Y + yi

        @pl.when(t > 0)
        def _():
            act_wait(do_base, [do, dr], t)

        @pl.when(t < Z)
        def _():
            act_forward(do_base, [do, dr], a)

        for k in range(NQ):
            qb = stack4(qc[zi, yi, :, quad(k)])
            db = stack4(do[zi, yi, :, quad(k)])
            kt = kv[qi, :, quad(k)]
            vt = kv[qi, :, D + k * WIDE : D + (k + 1) * WIDE]
            pt = jnp.exp(nt(kt, qb) - dr[zi, yi, 0:1, quad(k)])
            ds = (pt * (nt(vt, db) - dr[zi, yi, 1:2, quad(k)])).astype(BF)
            pq[b, zi, :, quad(k)] = fold4(tn(ds, kt)).astype(BF)
            kv[qi, :, quad(k)] = nn(ds, qb).astype(BF)
            kv[qi, :, D + k * WIDE : D + (k + 1) * WIDE] = nn(pt.astype(BF), db).astype(BF)

        @pl.when(t >= Z)
        def _():
            rs_y_send(yq_base, pq, ryq, b, a)

        return carry

    lax.fori_loop(0, YZ, attend_back, 0)
    fi_y2 = ff_in_y(fi_x2)
    push(CO)
    for a in range(Z):
        for b in range(1, Y):
            rs_y_wait(yq_base, pq, ryq, b, a)
    zq = rs_z_stage(pq, ryq, rzq)

    for p, off in ((CK, 0), (CV, D)):
        if R % 16 == 0:
            acc[...] = tn(pas[...].reshape(YZ * R, D), kv[:, :, off : off + D].reshape(YZ * R, D))
        else:
            acc[...] = jnp.zeros_like(acc)

            def kv_grad(q, carry):
                acc[...] += tn(pas[q], kv[q, :, off : off + D])
                return carry

            lax.fori_loop(0, YZ, kv_grad, 0)
        grad_out(p)
        push(CO)

    def row_grad(q, carry):
        pas[q] = (nt(kv[q, :, 0:D], w[CK]) + nt(kv[q, :, D : 2 * D], w[CV])).astype(BF)
        pltpu.make_async_copy(pas.at[q], m["pg"].at[q], lsem.at[1 + q]).start()
        return carry

    lax.fori_loop(0, YZ, row_grad, 0)
    fi_z2 = ff_in_z(fi_y2)
    ff_out_end(fo_x2)

    got(zq)
    dqc = rs_total(pq, ryq, rzq).astype(BF)
    dh2 = nt(dqc, w[CQ])
    dv, gg = norm_back(m["x1"][...], gain[1:2, :], dh2)
    sm[1:2, :] = gg
    dx1 = m["dx"][...] + dv
    m["dx"][...] = dx1
    dx1l = dx1.astype(BF)
    grad_of(CQ, m["h2"][...], dqc)
    push_all([CK, CV, CO])
    grad_of(SO, m["os"][...], dx1l)
    push_all([CQ, CK, CV, CO])
    ff_in_end(fi_z2)
    got(zy)
    yt = rs_total(py, ryy, rzy)
    m["bo"][...] = live * (m["x2"][...] + yt)

    m["oc"][...] = nt(dx1l, w[SO]).astype(BF)
    grads = [[], [], []]
    tail = []
    for t in range(NQ):
        db = stack4(m["oc"][:, quad(t)])
        qb = stack4(m["qs"][:, quad(t)])
        pr = m["ps"][t]
        dps = nt(db, m["vs"][:, quad(t)])
        dss = (pr * (dps - jnp.sum(pr * dps, axis=1, keepdims=True))).astype(BF)
        grads[0].append(fold4(nn(dss, m["ks"][:, quad(t)])).astype(BF))
        grads[1].append(tn(dss, qb).astype(BF))
        grads[2].append(tn(pr.astype(BF), db).astype(BF))
        back = (iota((T, 128), 1) == T - 1 - iota((T, 128), 0)).astype(F32).astype(BF)
        turned = nn(dss, back)
        for h in range(QUAD):
            part = pltpu.roll(turned[h * T : (h + 1) * T], 0, 1, stride=1, stride_axis=0)
            tail.append(jnp.sum(part, axis=0, keepdims=True))
    dqs, dks, dvs = (jnp.concatenate(g, axis=1) for g in grads)
    h1 = m["h1"][...]
    push_all([SO, CQ, CK, CV, CO])
    grad_of(SV, h1, dvs)
    push_all([SO, CQ, CK, CV, CO])
    grad_of(SQ, h1, dqs)
    push_all([SV, SO, CQ, CK, CV, CO])
    grad_of(SK, h1, dks)
    push_all([SQ, SV, SO, CQ, CK, CV, CO])
    dh1 = nt(dqs, w[SQ]) + nt(dks, w[SK]) + nt(dvs, w[SV])
    dv, gg = norm_back(tok[...], gain[0:1, :], dh1)
    sm[0:1, :] = gg
    m["tg"][...] = m["dx"][...] + dv
    flat = HEADS * BUCKETS
    diag = jnp.concatenate(tail + [jnp.zeros((16 - HEADS, 128), F32)], axis=0)
    mi, bi = iota((128, 128), 0), iota((128, 128), 1)
    hot = ((mi >= T - 1) & (bucket_of(mi - (T - 1)) == bi) & (bi < BUCKETS)).astype(F32)
    table = nn_high(diag, hot)
    bb, nb = iota((128, flat), 0), iota((128, flat), 1)
    wide = nn_high(table, ((nb & (BUCKETS - 1)) == bb).astype(F32))
    h0, n0 = iota((16, flat), 0), iota((16, flat), 1)
    own = (n0 >= h0 * BUCKETS) & (n0 < h0 * BUCKETS + BUCKETS)
    sm[3:4, 0:flat] = jnp.sum(jnp.where(own, wide, 0.0), axis=0, keepdims=True)

    rsm = m["rsm"]
    slot = [0]

    def small_sum(devs):
        first = slot[0]
        cps = []
        for to in devs:
            cps.append(send(sm, rsm.at[slot[0]], to))
            slot[0] += 1
        got(cps)
        sent(cps)
        for k in range(first, slot[0]):
            sm[...] += rsm[k]

    small_sum([dev(c_=oth)])
    push_all([SK, SQ, SV, SO, CQ, CK, CV, CO])
    small_sum([dev(x_=xs(b)) for b in range(1, X)])
    push_all([SK, SQ, SV, SO, CQ, CK, CV, CO])
    small_sum([dev(y_=ys(b)) for b in range(1, Y)])
    push_all([SK, SQ, SV, SO, CQ, CK, CV, CO])
    small_sum([dev(z_=zs(a)) for a in range(1, Z)])
    while any(k < len(stages) for k, _ in moving.values()):
        push_all([SK, SQ, SV, SO, CQ, CK, CV, CO])
    me = dp * YZ + fs
    nd, ld = iota((D, 128), 0), iota((D, 128), 1)
    mine = nn_high(sm[...], ((nd == me * r + ld) & (ld < r)).astype(F32))
    mine_b = nn_high(sm[...], ((nd == me * rbs + ld) & (ld < rbs)).astype(F32))
    m["g_ls"][...] = mine[0:1, 0:r]
    m["g_lc"][...] = mine[1:2, 0:r]
    m["g_lf"][...] = mine[2:3, 0:r]
    m["g_rb"][...] = mine_b[3:4, 0:rbs]

    act_done(do_base, [do, dr])
    rs_y_done(yq_base, pq, ryq)
    drain()

    def pg_wait(q, carry):
        pltpu.make_async_copy(pas.at[q], m["pg"].at[q], lsem.at[1 + q]).wait()
        return carry

    lax.fori_loop(0, YZ, pg_wait, 0)


def per_device(
    sz,
    targets, passages, tgt_len, out_grad, ln_self, rel_bias, self_q, self_kv, self_out,
    ln_cross, cross_q, cross_kv, cross_out, ln_ff, ff_in, ff_out,
):
    T, D, r, hid, rfi, rff = sz.T, sz.D, sz.r, sz.hid, sz.rfi, sz.rff
    nfs = sz.Y * sz.Z
    ndp = 2 * sz.X
    live = (jnp.arange(T) < tgt_len[0]).astype(F32)
    live = jnp.broadcast_to(live[:, None], (T, 128))

    def line(v):
        return jnp.pad(v, (0, 128 - v.shape[0]))

    small = jnp.stack([line(ln_self), line(ln_cross), line(ln_ff), line(rel_bias)])
    small = jnp.pad(small, ((0, 12), (0, 0)))
    fi_in = ff_in.reshape(r, ndp, nfs, rff).transpose(2, 0, 1, 3).reshape(nfs, r, hid)
    fi_in = jnp.pad(fi_in, ((0, 0), (0, rfi - r), (0, 0)))
    scratch = layout(sz)
    names = tuple(scratch)
    gr = r if sz.inside else D
    vm = pl.BlockSpec(memory_space=pltpu.VMEM)
    hbm = pl.BlockSpec(memory_space=pl.ANY)
    shape = jax.ShapeDtypeStruct
    rbs = rel_bias.shape[0]
    out_shape = (
        shape((T, D), F32), shape((T, D), F32), shape(passages.shape, BF),
        shape((1, r), F32), shape((1, rbs), F32),
        shape((gr, D), F32), shape((gr, 2 * D), F32), shape((gr, D), F32),
        shape((1, r), F32), shape((gr, D), F32), shape((gr, 2 * D), F32), shape((gr, D), F32),
        shape((1, r), F32), shape((nfs, r, hid), F32), shape((rff, D), F32),
    )
    weight_outs = ("g_sq", "g_skv", "g_so", "g_cq", "g_ckv", "g_co")
    apart = ("pg",) if sz.inside else ("pg",) + weight_outs
    outs = pl.pallas_call(
        functools.partial(block_kernel, sz, names),
        out_shape=out_shape,
        in_specs=[hbm if n == "pas_in" else vm for n in INPUTS],
        out_specs=tuple(hbm if n in apart else vm for n in OUTPUTS),
        scratch_shapes=tuple(scratch.values()),
        compiler_params=pltpu.CompilerParams(
            collective_id=0, has_side_effects=True, vmem_limit_bytes=63 * 2**20
        ),
        cost_estimate=pl.CostEstimate(
            flops=20 * 10**9, bytes_accessed=2 * 10**7, transcendentals=4 * 10**6
        ),
    )(
        targets[0], passages, live, out_grad[0], small, self_q, self_kv, self_out,
        cross_q, cross_kv, cross_out, fi_in, ff_out,
    )
    (bo, tg, pg, g_ls, g_rb, g_sq, g_skv, g_so, g_lc, g_cq, g_ckv, g_co, g_lf, g_fi, g_fo) = outs
    if not sz.inside:
        g_sq, g_skv, g_so, g_cq, g_ckv, g_co = (
            lax.psum_scatter(g, ("dp", "fsdp"), scatter_dimension=0, tiled=True)
            for g in (g_sq, g_skv, g_so, g_cq, g_ckv, g_co)
        )
    g_fi = g_fi.reshape(nfs, r, ndp, rff).transpose(1, 2, 0, 3).reshape(r, ndp * nfs * rff)
    return (
        bo[None], tg[None], pg, g_ls[0], g_rb[0], g_sq, g_skv, g_so,
        g_lc[0], g_cq, g_ckv, g_co, g_lf[0], g_fi, g_fo,
    )


def solution(mesh):
    both = ("dp", "fsdp")
    rows3, rows2, rows1 = P(both, None, None), P(both, None), P(both)
    placed = (
        rows3, P("dp", "fsdp", None), rows1, rows3, rows1, rows1, rows2, rows2, rows2,
        rows1, rows2, rows2, rows2, rows1, rows2, rows2,
    )
    outs = (
        rows3, rows3, P("dp", "fsdp", None), rows1, rows1, rows2, rows2, rows2,
        rows1, rows2, rows2, rows2, rows1, rows2, rows2,
    )

    def run(*args):
        targets, passages, self_q, ff_out = args[0], args[1], args[6], args[15]
        sz = Sizes(
            mesh.shape,
            targets.shape[2], passages.shape[1], targets.shape[1],
            self_q.shape[0], ff_out.shape[0],
            ff_out.shape[0] * mesh.shape["dp"],
        )
        return per_device(sz, *args)

    return jax.shard_map(run, mesh=mesh, in_specs=placed, out_specs=outs, check_vma=False)
```

```python
import functools
import math

import jax
import jax.numpy as jnp
from jax import lax
from jax.experimental import pallas as pl
from jax.experimental.pallas import tpu as pltpu
from jax.sharding import PartitionSpec as P

HEADS = 12
DK = 64
BUCKETS = 32
QUAD = 4
WIDE = QUAD * DK
EPS = 1e-06
NEG = -1e30
HIGH = lax.Precision.HIGHEST
BF = jnp.bfloat16
F32 = jnp.float32
PIECES = 10
SQ, SK, SV, SO, CQ, CK, CV, CO, FI, FO = range(PIECES)
X_LAST = (SQ, SV, CQ, CV, CO, FI, FO)
Y_LAST = (SK, SO, CK)
Y_GATHERED_LAST = (SK, CK)
ZDIM = 4


def up16(n):
    return (n + 15) // 16 * 16


def bucket_limits():
    limits = []
    for target_bucket in range(1, 16):
        distance = 16
        while int(math.log(distance / 16.0) / math.log(8.0) * 16.0) < target_bucket:
            distance = distance + 1
        limits.append(distance)
    return limits


def bucket_of(distance):
    larger = jnp.full_like(distance, 16)
    for limit_value in bucket_limits():
        larger = larger + (distance >= limit_value).astype(jnp.int32)
    return jnp.where(distance < 16, distance, jnp.minimum(larger, 31))


def iota(shape, axis):
    return lax.broadcasted_iota(jnp.int32, shape, axis)


def nn(a, b):
    return lax.dot_general(a, b, (((1,), (0,)), ((), ())), preferred_element_type=F32)


def nt(a, b):
    return lax.dot_general(a, b, (((1,), (1,)), ((), ())), preferred_element_type=F32)


def tn(a, b):
    return lax.dot_general(a, b, (((0,), (0,)), ((), ())), preferred_element_type=F32)


def nn_high(a, b):
    return lax.dot_general(
        a, b, (((1,), (0,)), ((), ())), preferred_element_type=F32, precision=HIGH
    )


def normed(v, gain):
    return v * lax.rsqrt(jnp.mean(v * v, axis=-1, keepdims=True) + EPS) * gain


def norm_back(v, gain, dy):
    s = lax.rsqrt(jnp.mean(v * v, axis=-1, keepdims=True) + EPS)
    dyg = dy * gain
    gain_grad = jnp.sum(dy * v * s, axis=0, keepdims=True)
    dv = s * dyg - v * (s * s * s) * jnp.mean(dyg * v, axis=-1, keepdims=True)
    return dv, gain_grad


def gelu_pair(u):
    cst = 0.7978845608028654
    cubic = 0.044715
    th = jnp.tanh(cst * (u + cubic * u * u * u))
    half = 0.5 * (1.0 + th)
    slope = half + 0.5 * u * (1.0 - th * th) * cst * (1.0 + 3.0 * cubic * u * u)
    return u * half, slope


class Sizes:
    def __init__(self, mesh_shape, width, rows, targets, shard, ff_shard, hidden):
        self.Z = ZDIM
        self.X = mesh_shape["dp"] // 2
        self.Y = mesh_shape["fsdp"] // self.Z
        self.D = width
        self.R = rows
        self.T = targets
        self.r = shard
        self.rb = up16(2 * shard)
        self.nh = width // 2
        self.inside = shard % 8 == 0
        self.rff = ff_shard
        self.hid = hidden
        assert ff_shard == self.Z * shard and hidden == width


def sems(sz):
    return 264 if sz.inside else 900


def layout(sz):
    X, Y, Z, D, T, R = sz.X, sz.Y, sz.Z, sz.D, sz.T, sz.R
    rb, nh, hid = sz.rb, sz.nh, sz.hid
    na, nb = len(X_LAST), len(Y_LAST)
    NQ = HEADS // QUAD
    V = pltpu.VMEM
    sums = dict(
        rc=V((PIECES, X, Y, Z, rb, nh), BF),
        r1a=V((na, X - 1, Y, Z, rb, nh), BF),
        r1b=V((nb, Y - 1, X, Z, rb, nh), BF),
        r2a=V((na, Y - 1, Z, rb, nh), BF),
        r2b=V((nb, X - 1, Z, rb, nh), BF),
        rz=V((PIECES, Z - 1, rb, nh), BF),
    )
    return dict(
        **(sums if sz.inside else {}),
        gw=V((PIECES, 2, X, Y, Z, rb, nh), BF),
        w=V((PIECES, D, D), BF),
        fip=V((Z, rb, nh), BF),
        acc=V((D, D), F32),
        lift=V((max(Y * Z * sz.r, sz.rff) if sz.r % 8 else 8, D), F32),
        even=V((sz.r, D), F32),
        gfi=V((Z, sz.r, D), F32),
        cell=V((rb, nh), F32),
        smb=V((2, X, Y, Z, 16, 128), BF),
        hot_gain=V((128, D), BF),
        hot_bias=V((128, HEADS * BUCKETS), BF),
        gain=V((16, D), F32),
        bias=V((NQ, WIDE, T), F32),
        spread=V((16, D), F32),
        mask=V((WIDE, WIDE), BF),
        pas=V((Y * Z, R, D), BF),
        kv=V((Y * Z, R, 2 * D), BF),
        h1=V((T, D), BF),
        qs=V((T, D), BF),
        ks=V((T, D), BF),
        vs=V((T, D), BF),
        os=V((T, D), BF),
        ps=V((NQ, WIDE, T), F32),
        x1=V((T, D), F32),
        h2=V((T, D), BF),
        x2=V((T, D), F32),
        oc=V((T, D), BF),
        dx=V((T, D), F32),
        lse=V((16, T), F32),
        qc=V((Z, Y, T, D), BF),
        h3=V((Z, T, D), BF),
        g3=V((Z, T, D), BF),
        do=V((Z, Y, T, D), BF),
        dr=V((Z, Y, 16, 128), F32),
        po=V((Y, Z, T, D), BF),
        pst=V((Y, Z, 16, T), F32),
        ryo=V((Y - 1, Z, T, D), BF),
        ryst=V((Y - 1, Z, 16, T), F32),
        rzo=V((Z - 1, T, D), BF),
        rzst=V((Z - 1, 16, T), F32),
        py=V((Z, T, D), BF),
        rzy=V((Z - 1, T, D), BF),
        da=V((Z * T, hid), F32),
        gl=V((Z * T, hid), BF),
        du=V((Z * T, hid), BF),
        sm=V((8, D), F32),
        rsm=V((1 + (X - 1) + (Y - 1) + (Z - 1), 8, D), F32),
        ssem=pltpu.SemaphoreType.DMA((sems(sz),)),
        rsem=pltpu.SemaphoreType.DMA((sems(sz),)),
        lsem=pltpu.SemaphoreType.DMA((1 + Y * Z,)),
    )


INPUTS = (
    "tok", "pas_in", "len", "og", "ls", "rel", "sq", "skv", "so",
    "lc", "cq", "ckv", "co", "lf", "fi_in", "fo_in",
)
OUTPUTS = (
    "bo", "tg", "pg", "g_ls", "g_rb", "g_sq", "g_skv", "g_so",
    "g_lc", "g_cq", "g_ckv", "g_co", "g_lf", "g_fi", "g_fo",
)


def block_kernel(sz, names, *refs):
    n_in, n_out = len(INPUTS), len(OUTPUTS)
    m = dict(zip(INPUTS, refs[:n_in]))
    m.update(zip(OUTPUTS, refs[n_in : n_in + n_out]))
    m.update(zip(names, refs[n_in + n_out :]))
    X, Y, Z, D, T, R = sz.X, sz.Y, sz.Z, sz.D, sz.T, sz.R
    r, rb, nh, hid = sz.r, sz.rb, sz.nh, sz.hid
    NQ = HEADS // QUAD
    YZ = Y * Z
    dp = lax.axis_index("dp")
    fs = lax.axis_index("fsdp")
    x, c = dp // 2, dp % 2
    z, y = fs // Y, fs % Y
    oth = 1 - c

    def xs(b):
        return (x + b) % X

    def ys(b):
        return (y + b) % Y

    def zs(b):
        return (z + b) % Z

    def dev(x_=None, c_=None, y_=None, z_=None):
        x_ = x if x_ is None else x_
        c_ = c if c_ is None else c_
        y_ = y if y_ is None else y_
        z_ = z if z_ is None else z_
        return (x_ * 2 + c_, z_ * Y + y_)

    ssem, rsem, lsem = m["ssem"], m["rsem"], m["lsem"]
    n_sems = sems(sz)
    used = [0]
    pending = []

    def take(n=1):
        at = used[0]
        used[0] += n
        assert used[0] <= n_sems
        return at

    def copy_at(i, src, dst, to):
        return pltpu.make_async_remote_copy(
            src_ref=src, dst_ref=dst, send_sem=ssem.at[i], recv_sem=rsem.at[i],
            device_id=to, device_id_type=pl.DeviceIdType.MESH,
        )

    def send(src, dst, to):
        cp = copy_at(take(), src, dst, to)
        cp.start()
        pending.append(cp)
        return cp

    def got(cps):
        for cp in cps:
            cp.wait_recv()

    def sent(cps):
        for cp in cps:
            cp.wait_send()
        pending[:] = [cp for cp in pending if all(cp is not done for done in cps)]

    def drain():
        sent(list(pending))

    partners = [dev(c_=oth)]
    partners += [dev(x_=xs(b)) for b in range(1, X)]
    partners += [dev(y_=ys(b)) for b in range(1, Y)]
    partners += [dev(z_=zs(b)) for b in range(1, Z)]
    bar = pltpu.get_barrier_semaphore()
    for p in partners:
        pl.semaphore_signal(bar, inc=1, device_id=p, device_id_type=pl.DeviceIdType.MESH)
    load_pas = pltpu.make_async_copy(m["pas_in"], m["pas"], lsem.at[0])
    load_pas.start()
    pl.semaphore_wait(bar, len(partners))

    mask = m["mask"]
    mask[...] = (iota((WIDE, WIDE), 0) // DK == iota((WIDE, WIDE), 1) // DK).astype(F32).astype(BF)

    def stack4(v):
        return jnp.concatenate([v, v, v, v], axis=0) * mask[...]

    def fold4(u):
        lane = iota((T, WIDE), 1)
        out = u[0:T]
        for h in range(1, QUAD):
            out = jnp.where(lane >= h * DK, u[h * T : (h + 1) * T], out)
        return out

    def quad(t):
        return slice(t * WIDE, (t + 1) * WIDE)

    cell, lift = m["cell"], m["lift"]

    def put_halves(dst, left, right, rows, total):
        if rows % 8 == 0 and 2 * rows == total:
            dst[...] = jnp.concatenate([left, right], axis=0).astype(BF)
        else:
            cols = left.shape[1]
            cell[0:total, 0:cols] = jnp.zeros((total, cols), F32)
            cell[0:rows, 0:cols] = left
            cell[rows : 2 * rows, 0:cols] = right
            dst[...] = cell[0:total, 0:cols].astype(BF)

    def get_halves(v, rows):
        if rows % 8 == 0:
            return v[0:rows], v[rows : 2 * rows]
        cell[0 : v.shape[0], 0 : v.shape[1]] = v
        return cell[0:rows, 0 : v.shape[1]], cell[rows : 2 * rows, 0 : v.shape[1]]

    gw, w, smb = m["gw"], m["w"], m["smb"]

    def line_to(buf, over_y, blocks):
        out = []
        for k in blocks:
            block = buf.at[c, x, y, k]
            if over_y:
                out += [send(block, block, dev(y_=ys(b))) for b in range(1, Y)]
            else:
                out += [send(block, block, dev(x_=xs(b))) for b in range(1, X)]
        return out

    class Gather:
        def __init__(self, buf, y_first, feed="gather"):
            self.buf, self.y_first, self.feed = buf, y_first, feed
            own = buf.at[c, x, y, z]
            self.z = []
            for a in range(1, Z):
                if feed == "gather":
                    self.z.append(send(own, own, dev(z_=zs(a))))
                elif feed == "exchange":
                    self.z.append(send(m["fip"].at[zs(a)], own, dev(z_=zs(a))))

        def own_out(self):
            blocks = range(Z) if self.feed == "local" else [z]
            self.second = line_to(self.buf, self.y_first, blocks)
            self.third = line_to(self.buf, not self.y_first, blocks)

        def line_out(self):
            got(self.z)
            if self.feed != "local":
                blocks = [zs(Z - a) for a in range(1, Z)]
                self.second += line_to(self.buf, self.y_first, blocks)
                self.third += line_to(self.buf, not self.y_first, blocks)

        def plane_out(self):
            got(self.second)
            buf = self.buf
            if self.y_first:
                for b in range(1, Y):
                    line = buf.at[c, x, ys(b)]
                    self.third += [send(line, line, dev(x_=xs(d))) for d in range(1, X)]
            else:
                for b in range(1, X):
                    line = buf.at[c, xs(b), y]
                    self.third += [send(line, line, dev(y_=ys(d))) for d in range(1, Y)]

        def core_out(self):
            got(self.third)
            self.core = [send(self.buf.at[c], self.buf.at[c], dev(c_=oth))]

        def end(self):
            got(self.core)

    own_small = [jnp.zeros((16, 128), F32)]
    for at, key in enumerate(("ls", "lc", "lf", "rel")):
        v = m[key][...].astype(F32)
        v = jnp.concatenate([v, jnp.zeros((1, 128 - v.shape[1]), F32)], axis=1)
        own_small[0] = jnp.where(iota((16, 128), 0) == at, v, own_small[0])
    smb[c, x, y, z] = own_small[0].astype(BF)
    moves = {}

    def begin(p, feed="gather"):
        moves[p] = Gather(gw.at[p], p not in Y_GATHERED_LAST, feed)

    moves["small"] = Gather(smb, True)
    moves["small"].own_out()
    sources = (
        (m["sq"], 0), (m["skv"], 0), (m["skv"], D), (m["so"], 0),
        (m["cq"], 0), (m["ckv"], 0), (m["ckv"], D), (m["co"], 0),
    )

    def pack(p):
        ref, off = sources[p]
        v = ref[:, off : off + D].astype(F32)
        put_halves(gw.at[p, c, x, y, z], v[:, 0:nh], v[:, nh:D], r, rb)
        begin(p)
        moves[p].own_out()

    for p in (SQ, SK, SV, SO, CQ, CK, CV):
        pack(p)

    g3 = m["g3"]
    live = (iota((T, 1), 0) < m["len"][0]).astype(F32)
    g3[z] = (live * m["og"][...]).astype(BF)

    def line_start(base, buf):
        for a in range(1, Z):
            copy_at(base + a, buf.at[z], buf.at[z], dev(z_=zs(a))).start()

    def line_wait(base, buf):
        for a in range(1, Z):
            copy_at(base + a, buf.at[z], buf.at[z], dev(z_=zs(a))).wait_recv()

    def line_done(base, buf):
        for a in range(1, Z):
            copy_at(base + a, buf.at[z], buf.at[z], dev(z_=zs(a))).wait_send()

    def act_start(base, bufs):
        for n, buf in enumerate(bufs):
            for a in range(1, Z):
                copy_at(base + n * YZ + a, buf.at[z, y], buf.at[z, y], dev(z_=zs(a))).start()

    def act_forward(base, bufs, a):
        zi = zs(a)
        for n, buf in enumerate(bufs):
            for b in range(1, Y):
                copy_at(
                    base + n * YZ + b * Z + (Z - a) % Z, buf.at[zi, y], buf.at[zi, y], dev(y_=ys(b))
                ).start()

    def act_wait(base, bufs, t):
        at = base + (Y - t // Z) % Y * Z + (Z - t % Z) % Z
        for n, buf in enumerate(bufs):
            copy_at(at + n * YZ, buf.at[z, y], buf.at[z, y], dev(z_=zs(1))).wait_recv()

    def act_done(base, bufs):
        for n, buf in enumerate(bufs):
            for t in range(1, YZ):
                copy_at(base + n * YZ + t, buf.at[z, y], buf.at[z, y], dev(z_=zs(1))).wait_send()

    fip = m["fip"]
    ndp = 2 * X
    per = D // ndp

    def pack_ff():
        even = m["even"]
        for k in range(Z):
            for i in range(ndp):
                at = (i * Z + k) * per
                even[:, i * per : (i + 1) * per] = m["fi_in"][:, at : at + per].astype(F32)
            put_halves(fip.at[k], even[:, 0:nh], even[:, nh:D], r, rb)
        vo = m["fo_in"][...].astype(F32)
        if r % 8:
            lift[0 : Z * r, :] = vo
        for k in range(Z):
            part = lift[k * r : k * r + r, :] if r % 8 else vo[k * r : k * r + r]
            put_halves(gw.at[FO, c, x, y, k], part[:, 0:nh], part[:, nh:D], r, rb)
        gw[FI, c, x, y, z] = fip[z]

    g3_base = take(Z)
    line_start(g3_base, g3)

    spread = m["spread"]
    lane = iota((16, D), 1)
    row = iota((16, D), 0)
    spread[...] = ((lane >= row * DK) & (lane < row * DK + DK)).astype(F32)
    tlane = iota((T, 128), 1)
    rbs = HEADS * BUCKETS // (2 * X * YZ)

    def repeat_of(width, step):
        l0, n0 = iota((128, width), 0), iota((128, width), 1)

        def body(k, tot):
            return tot + ((n0 - l0 == k * step) & (l0 < step)).astype(F32)

        return lax.fori_loop(0, width // step, body, jnp.zeros((128, width), F32)).astype(BF)

    m["hot_gain"][...] = repeat_of(D, r)
    m["hot_bias"][...] = repeat_of(HEADS * BUCKETS, rbs)

    def unpack(p):
        group = 2 * Y * r

        if p == FO:
            group = YZ * r
            parts = [(yy, zz) for yy in range(Y) for zz in range(Z)]
        else:
            parts = [(yy, zz) for zz in range(2) for yy in range(Y)]
        per = YZ // len(parts)

        def body(g, carry):
            x_ = g // (2 * per)
            c_ = (g // per) % 2
            zp = 0 if per == 1 else g % per
            lefts, rights = [], []
            at = 0
            for yy, zz in parts:
                lo, hi = get_halves(gw[p, c_, x_, yy, 2 * zp + zz].astype(F32), r)
                if r % 8 == 0:
                    lefts.append(lo)
                    rights.append(hi)
                else:
                    lift[at : at + r, 0:nh] = lo
                    lift[at : at + r, nh:D] = hi
                at += r
            rows = pl.ds(pl.multiple_of(g * group, 16), group)
            if r % 8 == 0:
                w[p, rows, 0:nh] = jnp.concatenate(lefts, axis=0).astype(BF)
                w[p, rows, nh:D] = jnp.concatenate(rights, axis=0).astype(BF)
            else:
                w[p, rows, :] = lift[0:group, :].astype(BF)
            return carry

        lax.fori_loop(0, X * 2 * per, body, 0)

    gain = m["gain"]
    bias = m["bias"]
    def read_small():
        flat = HEADS * BUCKETS
        every = smb[...].reshape(2 * X * YZ * 16, 128)
        wide_g, wide_b = nn(every, m["hot_gain"][...]), nn(every, m["hot_bias"][...])
        ng, nb = iota((16, D), 1), iota((16, flat), 1)
        gains, tot = jnp.zeros((16, D), F32), jnp.zeros((16, flat), F32)
        at = 0
        for c_ in range(2):
            for x_ in range(X):
                for y_ in range(Y):
                    for z_ in range(Z):
                        k = (x_ * 2 + c_) * YZ + z_ * Y + y_
                        mine = (ng >= k * r) & (ng < k * r + r)
                        gains = jnp.where(mine, wide_g[at : at + 16], gains)
                        mine = (nb >= k * rbs) & (nb < k * rbs + rbs)
                        tot = jnp.where(mine, wide_b[at : at + 16], tot)
                        at += 16
        gain[...] = gains
        per = jnp.broadcast_to(tot[3:4, :], (16, flat))
        h0, n0 = iota((16, flat), 0), iota((16, flat), 1)
        per = jnp.where((n0 >= h0 * BUCKETS) & (n0 < h0 * BUCKETS + BUCKETS), per, 0.0)
        nb, mb = iota((flat, 128), 0), iota((flat, 128), 1)
        dist = jnp.where(mb == 0, 0, 128 - mb)
        hot = ((nb & (BUCKETS - 1)) == bucket_of(dist)).astype(F32).astype(BF)
        table = nn(per.astype(BF), hot)
        for h in range(HEADS):
            wide = jnp.broadcast_to(table[h : h + 1, :], (T, 128))
            rolled = pltpu.roll(wide, 0, 1, stride=1, stride_axis=0)
            bias[h // QUAD, (h % QUAD) * T : (h % QUAD + 1) * T, :] = rolled[:, 0:T]

    tok = m["tok"]

    def self_forward():
        m["h1"][...] = normed(tok[...], gain[0:1, :]).astype(BF)
        h1 = m["h1"][...]
        m["qs"][...] = nn(h1, w[SQ]).astype(BF)
        m["ks"][...] = nn(h1, w[SK]).astype(BF)
        m["vs"][...] = nn(h1, w[SV]).astype(BF)
        allowed = iota((WIDE, T), 1) <= (iota((WIDE, T), 0) & (T - 1))
        for t in range(NQ):
            s = nt(stack4(m["qs"][:, quad(t)]), m["ks"][:, quad(t)]) + bias[t]
            s = jnp.where(allowed, s, NEG)
            e = jnp.exp(s - jnp.max(s, axis=1, keepdims=True))
            pr = e / jnp.sum(e, axis=1, keepdims=True)
            m["ps"][t] = pr
            m["os"][:, quad(t)] = fold4(nn(pr.astype(BF), m["vs"][:, quad(t)])).astype(BF)

    qc = m["qc"]
    qc_base = take(YZ)

    def self_out():
        x1 = tok[...] + nn(m["os"][...], w[SO])
        m["x1"][...] = x1
        m["h2"][...] = normed(x1, gain[1:2, :]).astype(BF)

    def cross_query():
        qc[z, y] = nn(m["h2"][...], w[CQ]).astype(BF)
        act_start(qc_base, [qc])

    kv, pas = m["kv"], m["pas"]

    chunk = 4 if R % 16 == 0 else 1

    def project(p, off):
        def body(k, carry):
            if chunk == 1:
                kv[k, :, off : off + D] = nn(pas[k], w[p]).astype(BF)
            else:
                rows = pl.ds(k * chunk, chunk)
                v = nn(pas[rows].reshape(chunk * R, D), w[p])
                kv[rows, :, off : off + D] = v.astype(BF).reshape(chunk, R, D)
            return carry

        lax.fori_loop(0, YZ // chunk, body, 0)

    def query_forward():
        for a in range(Z):
            if a:
                act_wait(qc_base, [qc], a)
            act_forward(qc_base, [qc], a)

    def after(p):
        unpack(p)
        if p == SQ:
            moves["small"].end()
            read_small()
        elif p == SV:
            self_forward()
        elif p == SO:
            self_out()
        elif p == CQ:
            cross_query()
        elif p == CK:
            load_pas.wait()
            project(CK, 0)
        elif p == CV:
            query_forward()
            project(CV, D)

    order = (SQ, SK, SV, SO, CQ, CK, CV, CO, FI, FO)

    def line_out(k):
        if k == 0:
            moves["small"].line_out()
        moves[order[k]].line_out()

    def plane_out(k):
        if k == 0:
            moves["small"].plane_out()
        moves[order[k]].plane_out()

    def core_out(k):
        if k == 0:
            moves["small"].core_out()
        moves[order[k]].core_out()

    def arrive(k):
        moves[order[k]].end()
        after(order[k])

    for k in range(7):
        line_out(k)
        if k == 1:
            pack_ff()
        if k >= 1:
            plane_out(k - 1)
        if k >= 2:
            core_out(k - 2)
        if k >= 3:
            arrive(k - 3)
    plane_out(6)
    pack(CO)
    begin(FI, "exchange")
    core_out(5)
    arrive(4)
    core_out(6)
    arrive(5)
    line_out(7)
    moves[FI].own_out()
    begin(FO, "local")
    moves[FO].own_out()
    arrive(6)

    po, pst, ryo, ryst, rzo, rzst = (m[k] for k in ("po", "pst", "ryo", "ryst", "rzo", "rzst"))

    def rs_y_base():
        return take((Y - 1) * Z)

    def rs_y_send(base, src, dst, b, a):
        zi = zs(a)
        copy_at(base + (b - 1) * Z + a, src.at[b, zi], dst.at[b - 1, zi], dev(y_=ys(b))).start()

    def rs_y_wait(base, src, dst, b, a):
        copy_at(base + (b - 1) * Z + a, src.at[b, 0], dst.at[b - 1, 0], dev(y_=ys(1))).wait_recv()

    def rs_y_done(base, src, dst):
        for b in range(1, Y):
            for a in range(Z):
                copy_at(
                    base + (b - 1) * Z + a, src.at[b, 0], dst.at[b - 1, 0], dev(y_=ys(1))
                ).wait_send()

    yo_base, yst_base = rs_y_base(), rs_y_base()
    zo_base, zst_base = take(Z), take(Z)

    def attend(a, b):
        zi = zs(a)
        yi = ys(b)
        qi = zi * Y + yi
        st = jnp.zeros((T, 128), F32)
        for k in range(NQ):
            qb = stack4(qc[zi, yi, :, quad(k)])
            s = nt(qb, kv[qi, :, quad(k)])
            top = jnp.max(s, axis=1, keepdims=True)
            e = jnp.exp(s - top)
            tot = jnp.sum(e, axis=1, keepdims=True)
            u = nn(e.astype(BF), kv[qi, :, D + k * WIDE : D + (k + 1) * WIDE])
            po[b, zi, :, quad(k)] = fold4(u * (1.0 / tot)).astype(BF)
            lse = top + jnp.log(tot)
            for h in range(QUAD):
                st = jnp.where(tlane == k * QUAD + h, lse[h * T : (h + 1) * T], st)
        pst[b, zi] = st.T[0:16]

    def expand(st):
        return lax.dot_general(
            st, spread[...], (((0,), (0,)), ((), ())), preferred_element_type=F32, precision=HIGH
        )

    def merge(parts):
        top = parts[0][1]
        for _, st in parts[1:]:
            top = jnp.maximum(top, st)
        ws = [jnp.exp(st - top) for _, st in parts]
        tot = ws[0]
        for v in ws[1:]:
            tot = tot + v
        out = jnp.zeros((T, D), F32)
        for (o, _), v in zip(parts, ws):
            out = out + expand(v / tot) * o.astype(F32)
        return out, top + jnp.log(tot)

    def z_send(base, src, dst, a):
        zi = zs(a)
        copy_at(base + a, src.at[0, zi], dst.at[a - 1], dev(z_=zi)).start()

    def z_each(base, src, dst, wait):
        for a in range(1, Z):
            cp = copy_at(base + a, src.at[0, 0], dst.at[a - 1], dev(z_=zs(a)))
            if wait == "recv":
                cp.wait_recv()
            else:
                cp.wait_send()

    def attend_other(t, carry):
        a = (1 + t % Z) % Z
        b = 1 + t // Z
        act_wait(qc_base, [qc], b * Z + a)
        attend(a, b)
        rs_y_send(yo_base, po, ryo, b, a)
        rs_y_send(yst_base, pst, ryst, b, a)
        return carry

    def attend_own(t, carry):
        a = (1 + t) % Z
        zi = zs(a)
        attend(a, 0)

        @pl.when(t < Z - 1)
        def _():
            for b in range(1, Y):
                rs_y_wait(yo_base, po, ryo, b, a)
                rs_y_wait(yst_base, pst, ryst, b, a)
            o, st = merge(
                [(po[0, zi], pst[0, zi])]
                + [(ryo[b - 1, zi], ryst[b - 1, zi]) for b in range(1, Y)]
            )
            po[0, zi] = o.astype(BF)
            pst[0, zi] = st
            z_send(zo_base, po, rzo, a)
            z_send(zst_base, pst, rzst, a)

        return carry

    lax.fori_loop(0, (Y - 1) * Z, attend_other, 0)
    plane_out(7)
    line_out(8)
    line_out(9)
    lax.fori_loop(0, Z, attend_own, 0)
    core_out(7)
    plane_out(8)
    plane_out(9)
    arrive(7)
    for b in range(1, Y):
        rs_y_wait(yo_base, po, ryo, b, 0)
        rs_y_wait(yst_base, pst, ryst, b, 0)
    z_each(zo_base, po, rzo, "recv")
    z_each(zst_base, pst, rzst, "recv")
    o, lse = merge(
        [(po[0, z], pst[0, z])]
        + [(ryo[b - 1, z], ryst[b - 1, z]) for b in range(1, Y)]
        + [(rzo[a - 1], rzst[a - 1]) for a in range(1, Z)]
    )
    m["oc"][...] = o.astype(BF)
    m["lse"][...] = lse
    x2 = m["x1"][...] + nn(m["oc"][...], w[CO])
    m["x2"][...] = x2
    h3 = m["h3"]
    h3[z] = normed(x2, gain[2:3, :]).astype(BF)
    h3_base = take(Z)
    line_start(h3_base, h3)

    core_out(8)
    core_out(9)
    arrive(8)
    line_wait(g3_base, g3)
    arrive(9)
    gb = g3[...].reshape(Z * T, D)
    m["da"][...] = nt(gb, w[FO])
    act_done(qc_base, [qc])
    rs_y_done(yo_base, po, ryo)
    rs_y_done(yst_base, pst, ryst)
    z_each(zo_base, po, rzo, "send")
    z_each(zst_base, pst, rzst, "send")
    drain()
    py, rzy = m["py"], m["rzy"]
    gl, du = m["gl"], m["du"]
    line_wait(h3_base, h3)
    hb = h3[...].reshape(Z * T, D)
    act, slope = gelu_pair(nn(hb, w[FI]))
    du[...] = (m["da"][...] * slope).astype(BF)
    gl[...] = act.astype(BF)
    po[0] = nt(du[...], w[FI]).astype(BF).reshape(Z, T, D)

    def rs_z(part, rzb):
        return [send(part.at[zs(a)], rzb.at[a - 1], dev(z_=zs(a))) for a in range(1, Z)]

    def rs_total(part, rzb):
        tot = part[z].astype(F32)
        for a in range(1, Z):
            tot = tot + rzb[a - 1].astype(F32)
        return tot

    zh = rs_z(po.at[0], rzo)
    py[...] = nn(gl[...], w[FO]).astype(BF).reshape(Z, T, D)
    line_done(h3_base, h3)
    line_done(g3_base, g3)

    acc = m["acc"]

    def add_to(dst, src):
        dst[...] = (dst[...].astype(F32) + src[...].astype(F32)).astype(BF)

    rc, r1a, r1b, r2a, r2b, rz = (m.get(k) for k in ("rc", "r1a", "r1b", "r2a", "r2b", "rz"))

    def pack_grad(p):
        group = YZ * r
        if not sz.inside:
            name, off = targets[p]
            out = m[name] if p in (FI, FO) else m[name].at[:, off : off + D]
            cp = pltpu.make_async_copy(acc, out, lsem.at[0])
            cp.start()
            cp.wait()
            return None

        def body(k, carry):
            x_ = k // 2
            c_ = k % 2
            for z_ in range(Z):
                for y_ in range(Y):
                    at = (y_ * Z + z_) * r if p == FO else (z_ * Y + y_) * r
                    rows = pl.ds(pl.multiple_of(k * group + at, 8), r)
                    left, right = acc[rows, 0:nh], acc[rows, nh:D]
                    put_halves(gw.at[p, c_, x_, y_, z_], left, right, r, rb)
            return carry

        lax.fori_loop(0, 2 * X, body, 0)
        return [send(gw.at[p, oth], rc.at[p], dev(c_=oth))]

    def rs_first(p, cps):
        got(cps)

        def body(k, carry):
            x_ = k // Y
            y_ = k % Y
            add_to(gw.at[p, c, x_, y_], rc.at[p, x_, y_])
            return carry

        lax.fori_loop(0, X * Y, body, 0)
        if p in X_LAST:
            return [
                send(gw.at[p, c, xs(b)], r1a.at[X_LAST.index(p), b - 1], dev(x_=xs(b))) for b in range(1, X)
            ]
        return [
            send(gw.at[p, c, :, ys(b)], r1b.at[Y_LAST.index(p), b - 1], dev(y_=ys(b))) for b in range(1, Y)
        ]

    def rs_second(p, cps):
        got(cps)
        if p in X_LAST:
            for b in range(1, X):
                for y_ in range(Y):
                    add_to(gw.at[p, c, x, y_], r1a.at[X_LAST.index(p), b - 1, y_])
            return [
                send(gw.at[p, c, x, ys(b)], r2a.at[X_LAST.index(p), b - 1], dev(y_=ys(b)))
                for b in range(1, Y)
            ]
        for b in range(1, Y):
            for x_ in range(X):
                add_to(gw.at[p, c, x_, y], r1b.at[Y_LAST.index(p), b - 1, x_])
        return [
            send(gw.at[p, c, xs(b), y], r2b.at[Y_LAST.index(p), b - 1], dev(x_=xs(b))) for b in range(1, X)
        ]

    def rs_third(p, cps):
        got(cps)
        if p in X_LAST:
            for b in range(1, Y):
                add_to(gw.at[p, c, x, y], r2a.at[X_LAST.index(p), b - 1])
        else:
            for b in range(1, X):
                add_to(gw.at[p, c, x, y], r2b.at[Y_LAST.index(p), b - 1])
        if p == FO:
            return []
        return [
            send(gw.at[p, c, x, y, zs(a)], rz.at[p, a - 1], dev(z_=zs(a))) for a in range(1, Z)
        ]

    targets = {
        SQ: ("g_sq", 0), SK: ("g_skv", 0), SV: ("g_skv", D), SO: ("g_so", 0),
        CQ: ("g_cq", 0), CK: ("g_ckv", 0), CV: ("g_ckv", D), CO: ("g_co", 0),
        FI: ("g_fi", 0), FO: ("g_fo", 0),
    }

    def rs_last(p, cps):
        got(cps)
        name, off = targets[p]
        if p in (FI, FO):
            for a in range(Z):
                k = a if p == FO else zs(Z - a)
                if p == FO:
                    v = gw[p, c, x, y, a]
                else:
                    v = rz[p, a - 1] if a else gw[p, c, x, y, z]
                lo, hi = get_halves(v.astype(F32), r)
                if p == FI:
                    m["gfi"][k, :, 0:nh] = lo
                    m["gfi"][k, :, nh:D] = hi
                else:
                    m[name][k * r : k * r + r, 0:nh] = lo
                    m[name][k * r : k * r + r, nh:D] = hi
            if p == FI:
                for k in range(Z):
                    for i in range(ndp):
                        at = (i * Z + k) * per
                        m[name][:, at : at + per] = m["gfi"][k, :, i * per : (i + 1) * per]
            return None
        v = gw[p, c, x, y, z].astype(F32)
        for a in range(1, Z):
            v = v + rz[p, a - 1].astype(F32)
        lo, hi = get_halves(v, r)
        m[name][:, off : off + nh] = lo
        m[name][:, off + nh : off + D] = hi

    stages = (rs_first, rs_second, rs_third, rs_last) if sz.inside else ()
    moving = {}

    def grad_of(p, lhs, rhs):
        acc[...] = tn(lhs, rhs)
        grad_out(p)

    def grad_out(p):
        moving[p] = (0, pack_grad(p))

    def push(p):
        k, cps = moving[p]
        if k < len(stages):
            moving[p] = (k + 1, stages[k](p, cps))

    def push_all(ps):
        for p in ps:
            push(p)

    grad_of(FO, gl[...], gb)
    grad_of(FI, hb, du[...])
    got(zh)
    sm = m["sm"]
    sm[...] = jnp.zeros_like(sm)
    dh3 = rs_total(po.at[0], rzo)
    dv, gg = norm_back(m["x2"][...], gain[2:3, :], dh3)
    sm[2:3, :] = gg
    dx2 = live * m["og"][...] + dv
    m["dx"][...] = dx2
    dx2l = dx2.astype(BF)
    doc = nt(dx2l, w[CO]).astype(BF)
    do, dr = m["do"], m["dr"]
    do[z, y] = doc
    pick = iota((T, D), 0) == (iota((T, D), 1) & (T - 1))

    def as_rows(st):
        v = jnp.sum(jnp.where(pick, expand(st), 0.0), axis=0, keepdims=True)
        parts = [v[:, k * 128 : (k + 1) * 128] for k in range(D // 128)]
        return jnp.concatenate(parts + [jnp.zeros((8 - D // 128, 128), F32)], axis=0)

    prod = doc.astype(F32) * m["oc"][...].astype(F32)
    delta = lax.dot_general(
        spread[...], prod, (((1,), (1,)), ((), ())), preferred_element_type=F32, precision=HIGH
    )
    dr[z, y, 0:8] = as_rows(m["lse"][...])
    dr[z, y, 8:16] = as_rows(delta)
    do_base = take(2 * YZ)
    act_start(do_base, [do, dr])
    act_forward(do_base, [do, dr], 0)
    zy = rs_z(py, rzy)
    grad_of(CO, m["oc"][...], dx2l)

    sent(zh)
    yq_base = rs_y_base()

    def row_of(ref, k):
        return jnp.concatenate([ref[2 * k : 2 * k + 1, :], ref[2 * k + 1 : 2 * k + 2, :]], axis=1)

    def attend_back(t, carry):
        a = t % Z
        b = t // Z
        zi = zs(a)
        yi = ys(b)
        qi = zi * Y + yi

        @pl.when(t > 0)
        def _():
            act_wait(do_base, [do, dr], t)

        @pl.when((t > 0) & (t < Z))
        def _():
            act_forward(do_base, [do, dr], a)

        lse_rows = dr[zi, yi, 0:8]
        delta_rows = dr[zi, yi, 8:16]
        for k in range(NQ):
            qb = stack4(qc[zi, yi, :, quad(k)])
            db = stack4(do[zi, yi, :, quad(k)])
            kt = kv[qi, :, quad(k)]
            vt = kv[qi, :, D + k * WIDE : D + (k + 1) * WIDE]
            pt = jnp.exp(nt(kt, qb) - row_of(lse_rows, k))
            ds = (pt * (nt(vt, db) - row_of(delta_rows, k))).astype(BF)
            po[b, zi, :, quad(k)] = fold4(tn(ds, kt)).astype(BF)
            kv[qi, :, quad(k)] = nn(ds, qb).astype(BF)
            kv[qi, :, D + k * WIDE : D + (k + 1) * WIDE] = nn(pt.astype(BF), db).astype(BF)

        @pl.when(t >= Z)
        def _():
            rs_y_send(yq_base, po, ryo, b, a)

        return carry

    lax.fori_loop(0, 2, attend_back, 0)
    push_all([FO, FI])
    lax.fori_loop(2, Z, attend_back, 0)
    push_all([CO])
    lax.fori_loop(Z, YZ, attend_back, 0)

    def kv_grad(p, off):
        if R % 16 == 0:
            acc[...] = tn(pas[...].reshape(YZ * R, D), kv[:, :, off : off + D].reshape(YZ * R, D))
        else:
            acc[...] = jnp.zeros_like(acc)

            def body(q, carry):
                acc[...] += tn(pas[q], kv[q, :, off : off + D])
                return carry

            lax.fori_loop(0, YZ, body, 0)
        grad_out(p)

    def row_grads(k0, k1):
        def body(k, carry):
            if chunk == 1:
                pas[k] = (nt(kv[k, :, 0:D], w[CK]) + nt(kv[k, :, D : 2 * D], w[CV])).astype(BF)
            else:
                rows = pl.ds(k * chunk, chunk)
                v = nt(kv[rows, :, 0:D].reshape(chunk * R, D), w[CK])
                v = v + nt(kv[rows, :, D : 2 * D].reshape(chunk * R, D), w[CV])
                pas[rows] = v.astype(BF).reshape(chunk, R, D)
            for q in range(chunk):
                at = k * chunk + q
                pltpu.make_async_copy(pas.at[at], m["pg"].at[at], lsem.at[1 + at]).start()
            return carry

        lax.fori_loop(k0, k1, body, 0)

    kv_grad(CK, 0)
    zq = []
    for a in list(range(1, Z)) + [0]:
        zi = zs(a)
        for b in range(1, Y):
            rs_y_wait(yq_base, po, ryo, b, a)
        tot = po[0, zi].astype(F32)
        for b in range(1, Y):
            tot = tot + ryo[b - 1, zi].astype(F32)
        po[0, zi] = tot.astype(BF)
        if a:
            zq.append(send(po.at[0, zi], rzo.at[a - 1], dev(z_=zi)))
    kv_grad(CV, D)
    push_all([CK, FO, FI])
    half = YZ // chunk // 2
    row_grads(0, half)
    push_all([CV, CO])
    got(zq)
    dqc = rs_total(po.at[0], rzo).astype(BF)
    dh2 = nt(dqc, w[CQ])
    dv, gg = norm_back(m["x1"][...], gain[1:2, :], dh2)
    sm[1:2, :] = gg
    dx1 = m["dx"][...] + dv
    m["dx"][...] = dx1
    dx1l = dx1.astype(BF)
    grad_of(CQ, m["h2"][...], dqc)
    grad_of(SO, m["os"][...], dx1l)
    push_all([CQ])

    m["oc"][...] = nt(dx1l, w[SO]).astype(BF)
    grads = [[], [], []]
    tail = []
    for t in range(NQ):
        db = stack4(m["oc"][:, quad(t)])
        qb = stack4(m["qs"][:, quad(t)])
        pr = m["ps"][t]
        dps = nt(db, m["vs"][:, quad(t)])
        dss = (pr * (dps - jnp.sum(pr * dps, axis=1, keepdims=True))).astype(BF)
        grads[0].append(fold4(nn(dss, m["ks"][:, quad(t)])).astype(BF))
        grads[1].append(tn(dss, qb).astype(BF))
        grads[2].append(tn(pr.astype(BF), db).astype(BF))
        back = (iota((T, 128), 1) == T - 1 - iota((T, 128), 0)).astype(F32).astype(BF)
        turned = nn(dss, back)
        for h in range(QUAD):
            part = pltpu.roll(turned[h * T : (h + 1) * T], 0, 1, stride=1, stride_axis=0)
            tail.append(jnp.sum(part, axis=0, keepdims=True))
    dqs, dks, dvs = (jnp.concatenate(g, axis=1) for g in grads)
    h1 = m["h1"][...]
    grad_of(SV, h1, dvs)
    push(SO)
    grad_of(SQ, h1, dqs)
    push(SV)
    grad_of(SK, h1, dks)
    push(SQ)
    dh1 = nt(dqs, w[SQ]) + nt(dks, w[SK]) + nt(dvs, w[SV])
    dv, gg = norm_back(tok[...], gain[0:1, :], dh1)
    sm[0:1, :] = gg
    m["tg"][...] = m["dx"][...] + dv
    flat = HEADS * BUCKETS
    diag = jnp.concatenate(tail + [jnp.zeros((16 - HEADS, 128), F32)], axis=0)
    mi, bi = iota((128, 128), 0), iota((128, 128), 1)
    hot = ((mi >= T - 1) & (bucket_of(mi - (T - 1)) == bi) & (bi < BUCKETS)).astype(F32)
    table = nn_high(diag, hot)
    bb, nb = iota((128, flat), 0), iota((128, flat), 1)
    wide = nn_high(table, ((nb & (BUCKETS - 1)) == bb).astype(F32))
    h0, n0 = iota((16, flat), 0), iota((16, flat), 1)
    own = (n0 >= h0 * BUCKETS) & (n0 < h0 * BUCKETS + BUCKETS)
    sm[3:4, 0:flat] = jnp.sum(jnp.where(own, wide, 0.0), axis=0, keepdims=True)

    rsm = m["rsm"]
    slot = [0]

    def small_send(devs):
        cps = []
        for to in devs:
            cps.append((slot[0], send(sm, rsm.at[slot[0]], to)))
            slot[0] += 1
        return cps

    def small_end(cps):
        got([cp for _, cp in cps])
        sent([cp for _, cp in cps])
        for k, _ in cps:
            sm[...] += rsm[k]

    def small_sum(devs):
        small_end(small_send(devs))

    small_sum([dev(c_=oth)])
    push(SK)
    small_x = small_send([dev(x_=xs(b)) for b in range(1, X)])
    push(CK)
    push(CV)
    push_all([FO, FI, CO])
    row_grads(half, YZ // chunk)
    push(CQ)
    push(CK)
    push(SO)
    push(CV)
    push(SV)
    push_all([FO, FI, CO])
    small_end(small_x)
    small_y = small_send([dev(y_=ys(b)) for b in range(1, Y)])
    got(zy)
    m["bo"][...] = live * (m["x2"][...] + rs_total(py, rzy))
    push(SQ)
    push(CQ)
    push(SK)
    push(SO)
    push_all([CK, CV])
    small_end(small_y)
    small_z = small_send([dev(z_=zs(a)) for a in range(1, Z)])
    push(SV)
    push(SQ)
    push(SK)
    push_all([CQ, SO])
    small_end(small_z)
    push_all([SV, SQ, SK])
    assert all(k == len(stages) for k, _ in moving.values())
    me = dp * YZ + fs
    nd, ld = iota((D, 128), 0), iota((D, 128), 1)
    mine = nn_high(sm[...], ((nd == me * r + ld) & (ld < r)).astype(F32))
    mine_b = nn_high(sm[...], ((nd == me * rbs + ld) & (ld < rbs)).astype(F32))
    m["g_ls"][...] = mine[0:1, 0:r]
    m["g_lc"][...] = mine[1:2, 0:r]
    m["g_lf"][...] = mine[2:3, 0:r]
    m["g_rb"][...] = mine_b[3:4, 0:rbs]

    act_done(do_base, [do, dr])
    rs_y_done(yq_base, po, ryo)
    drain()

    def pg_wait(q, carry):
        pltpu.make_async_copy(pas.at[q], m["pg"].at[q], lsem.at[1 + q]).wait()
        return carry

    lax.fori_loop(0, YZ, pg_wait, 0)


def place_kernel(*refs):
    n = len(OUTPUTS)
    copies = [
        pltpu.make_async_copy(refs[k], refs[n + k], refs[2 * n].at[k]) for k in range(n)
    ]
    for cp in copies:
        cp.start()
    for cp in copies:
        cp.wait()


def per_device(
    sz,
    targets, passages, tgt_len, out_grad, ln_self, rel_bias, self_q, self_kv, self_out,
    ln_cross, cross_q, cross_kv, cross_out, ln_ff, ff_in, ff_out,
):
    T, D, r, Z = sz.T, sz.D, sz.r, sz.Z
    ndp = 2 * sz.X
    per = sz.Y * sz.rff
    scratch = layout(sz)
    names = tuple(scratch)
    gr = r if sz.inside else D
    vm = pl.BlockSpec(memory_space=pltpu.VMEM)
    hbm = pl.BlockSpec(memory_space=pltpu.HBM)
    smem = pl.BlockSpec(memory_space=pltpu.SMEM)
    shape = jax.ShapeDtypeStruct
    rbs = rel_bias.shape[0]
    out_shape = (
        shape((T, D), F32), shape((T, D), F32), shape(passages.shape, BF),
        shape((1, r), F32), shape((1, rbs), F32),
        shape((gr, D), F32), shape((gr, 2 * D), F32), shape((gr, D), F32),
        shape((1, r), F32), shape((gr, D), F32), shape((gr, 2 * D), F32), shape((gr, D), F32),
        shape((1, r), F32),
        shape((r, Z * D) if sz.inside else (D, D), F32),
        shape((Z * r, D) if sz.inside else (D, D), F32),
    )
    weight_outs = ("g_sq", "g_skv", "g_so", "g_cq", "g_ckv", "g_co", "g_fi", "g_fo")
    apart = ("pg",) if sz.inside else ("pg",) + weight_outs
    outs = pl.pallas_call(
        functools.partial(block_kernel, sz, names),
        out_shape=out_shape,
        in_specs=[{"pas_in": hbm, "len": smem}.get(n, vm) for n in INPUTS],
        out_specs=tuple(hbm if n in apart else vm for n in OUTPUTS),
        scratch_shapes=tuple(scratch.values()),
        compiler_params=pltpu.CompilerParams(
            collective_id=0, has_side_effects=True, vmem_limit_bytes=63 * 2**20
        ),
        cost_estimate=pl.CostEstimate(
            flops=20 * 10**9, bytes_accessed=2 * 10**7, transcendentals=4 * 10**6
        ),
    )(
        targets[0], passages, tgt_len, out_grad[0], ln_self[None], rel_bias[None],
        self_q, self_kv, self_out, ln_cross[None], cross_q, cross_kv, cross_out,
        ln_ff[None], ff_in, ff_out,
    )
    (bo, tg, pg, g_ls, g_rb, g_sq, g_skv, g_so, g_lc, g_cq, g_ckv, g_co, g_lf, g_fi, g_fo) = outs
    if not sz.inside:
        at = lax.axis_index("fsdp") // sz.Y
        rows = jnp.zeros((ndp, Z, per, D), F32).at[:, at].set(g_fo.reshape(ndp, per, D))
        cols = jnp.zeros((D, ndp, Z, per), F32).at[:, :, at].set(g_fi.reshape(D, ndp, per))
        g_sq, g_skv, g_so, g_cq, g_ckv, g_co, g_fi, g_fo = (
            lax.psum_scatter(g, ("dp", "fsdp"), scatter_dimension=0, tiled=True)
            for g in (
                g_sq, g_skv, g_so, g_cq, g_ckv, g_co,
                cols.reshape(D, Z * D), rows.reshape(Z * D, D),
            )
        )
    outs = (bo, tg, pg, g_ls, g_rb, g_sq, g_skv, g_so, g_lc, g_cq, g_ckv, g_co, g_lf, g_fi, g_fo)
    if sz.inside:
        outs = pl.pallas_call(
            place_kernel,
            out_shape=tuple(shape(o.shape, o.dtype) for o in outs),
            in_specs=[vm] * len(outs),
            out_specs=(hbm,) * len(outs),
            scratch_shapes=(pltpu.SemaphoreType.DMA((len(outs),)),),
            compiler_params=pltpu.CompilerParams(vmem_limit_bytes=63 * 2**20),
        )(*outs)
    (bo, tg, pg, g_ls, g_rb, g_sq, g_skv, g_so, g_lc, g_cq, g_ckv, g_co, g_lf, g_fi, g_fo) = outs
    return (
        bo[None], tg[None], pg, g_ls[0], g_rb[0], g_sq, g_skv, g_so,
        g_lc[0], g_cq, g_ckv, g_co, g_lf[0], g_fi, g_fo,
    )


def solution(mesh):
    both = ("dp", "fsdp")
    rows3, rows2, rows1 = P(both, None, None), P(both, None), P(both)
    placed = (
        rows3, P("dp", "fsdp", None), rows1, rows3, rows1, rows1, rows2, rows2, rows2,
        rows1, rows2, rows2, rows2, rows1, rows2, rows2,
    )
    outs = (
        rows3, rows3, P("dp", "fsdp", None), rows1, rows1, rows2, rows2, rows2,
        rows1, rows2, rows2, rows2, rows1, rows2, rows2,
    )

    def run(*args):
        targets, passages, self_q, ff_out = args[0], args[1], args[6], args[15]
        sz = Sizes(
            mesh.shape,
            targets.shape[2], passages.shape[1], targets.shape[1],
            self_q.shape[0], ff_out.shape[0],
            ff_out.shape[0] * mesh.shape["dp"] * mesh.shape["fsdp"] // ZDIM,
        )
        return per_device(sz, *args)

    return jax.shard_map(run, mesh=mesh, in_specs=placed, out_specs=outs, check_vma=False)
```

```python
import functools
import math

import jax
import jax.numpy as jnp
from jax import lax
from jax.experimental import pallas as pl
from jax.experimental.pallas import tpu as pltpu
from jax.sharding import PartitionSpec as P

HEADS = 12
DK = 64
BUCKETS = 32
QUAD = 4
WIDE = QUAD * DK
EPS = 1e-06
NEG = -1e30
HIGH = lax.Precision.HIGHEST
BF = jnp.bfloat16
F32 = jnp.float32
PIECES = 10
SQ, SK, SV, SO, CQ, CK, CV, CO, FI, FO = range(PIECES)
X_LAST = (CK, CV, CQ, SO, SQ, SK, CO, FI, FO)
Y_LAST = (SV,)
Y_GATHERED_LAST = (SQ, SV, CQ)
ZDIM = 4


def up16(n):
    return (n + 15) // 16 * 16


def bucket_limits():
    limits = []
    for target_bucket in range(1, 16):
        distance = 16
        while int(math.log(distance / 16.0) / math.log(8.0) * 16.0) < target_bucket:
            distance = distance + 1
        limits.append(distance)
    return limits


def bucket_of(distance):
    larger = jnp.full_like(distance, 16)
    for limit_value in bucket_limits():
        larger = larger + (distance >= limit_value).astype(jnp.int32)
    return jnp.where(distance < 16, distance, jnp.minimum(larger, 31))


def iota(shape, axis):
    return lax.broadcasted_iota(jnp.int32, shape, axis)


def nn(a, b):
    return lax.dot_general(a, b, (((1,), (0,)), ((), ())), preferred_element_type=F32)


def nt(a, b):
    return lax.dot_general(a, b, (((1,), (1,)), ((), ())), preferred_element_type=F32)


def tn(a, b):
    return lax.dot_general(a, b, (((0,), (0,)), ((), ())), preferred_element_type=F32)


def nn_high(a, b):
    return lax.dot_general(
        a, b, (((1,), (0,)), ((), ())), preferred_element_type=F32, precision=HIGH
    )


def normed(v, gain):
    return v * lax.rsqrt(jnp.mean(v * v, axis=-1, keepdims=True) + EPS) * gain


def norm_back(v, gain, dy):
    s = lax.rsqrt(jnp.mean(v * v, axis=-1, keepdims=True) + EPS)
    dyg = dy * gain
    gain_grad = jnp.sum(dy * v * s, axis=0, keepdims=True)
    dv = s * dyg - v * (s * s * s) * jnp.mean(dyg * v, axis=-1, keepdims=True)
    return dv, gain_grad


def gelu_pair(u):
    cst = 0.7978845608028654
    cubic = 0.044715
    th = jnp.tanh(cst * (u + cubic * u * u * u))
    half = 0.5 * (1.0 + th)
    slope = half + 0.5 * u * (1.0 - th * th) * cst * (1.0 + 3.0 * cubic * u * u)
    return u * half, slope


class Spot:
    def __init__(self, base, steps=()):
        self.base, self.steps = base, steps

    @property
    def at(self):
        return Steps(self)

    def ref(self):
        out = self.base
        for step in self.steps:
            out = out.at[step]
        return out

    def __getitem__(self, key):
        return self.ref()[key]

    def __setitem__(self, key, value):
        self.ref()[key] = value


class Steps:
    def __init__(self, spot):
        self.spot = spot

    def __getitem__(self, key):
        return Spot(self.spot.base, self.spot.steps + (key,))


class Sent:
    def __init__(self, make):
        self.make = make

    def wait_recv(self):
        self.make().wait_recv()

    def wait_send(self):
        self.make().wait_send()


class Sizes:
    def __init__(self, mesh_shape, width, rows, targets, shard, ff_shard, hidden):
        self.Z = ZDIM
        self.X = mesh_shape["dp"] // 2
        self.Y = mesh_shape["fsdp"] // self.Z
        self.D = width
        self.R = rows
        self.T = targets
        self.r = shard
        self.rb = up16(2 * shard)
        self.nh = width // 2
        self.inside = shard % 8 == 0
        self.rff = ff_shard
        self.hid = hidden
        assert ff_shard == self.Z * shard and hidden == width


def sems(sz):
    return 199 if sz.inside else 900


def layout(sz):
    X, Y, Z, D, T, R = sz.X, sz.Y, sz.Z, sz.D, sz.T, sz.R
    rb, nh, hid = sz.rb, sz.nh, sz.hid
    na, nb = len(X_LAST), len(Y_LAST)
    NQ = HEADS // QUAD
    V = pltpu.VMEM
    sums = dict(
        rc=V((PIECES, X, Y, Z, rb, nh), BF),
        r1a=V((na, X - 1, Y, Z, rb, nh), BF),
        r1b=V((nb, Y - 1, X, Z, rb, nh), BF),
        r2a=V((na, Y - 1, Z, rb, nh), BF),
        r2b=V((nb, X - 1, Z, rb, nh), BF),
        rz=V((PIECES, Z - 1, rb, nh), BF),
    )
    return dict(
        **(sums if sz.inside else {}),
        gw=V((PIECES, 2, X, Y, Z, rb, nh), BF),
        w=V((PIECES, D, D), BF),
        fip=V((Z, rb, nh), BF),
        kvacc=V((D, 2 * D), F32),
        lift=V((max(Y * Z * sz.r, sz.rff) if sz.r % 8 else 8, D), F32),
        even=V((sz.r, D), F32),
        cell=V((rb, nh), F32),
        smb=V((2, X, Y, Z, 16, 128), BF),
        hot_gain=V((128, D), BF),
        hot_bias=V((128, HEADS * BUCKETS), BF),
        gain=V((16, D), F32),
        bias=V((NQ, WIDE, T), F32),
        spread=V((16, D), F32),
        spread2=V((32, D), BF),
        mask=V((WIDE, WIDE), BF),
        pas=V((Y * Z, R, D), BF),
        kv=V((Y * Z, R, 2 * D), BF),
        h1=V((T, D), BF),
        qs=V((T, D), BF),
        ks=V((T, D), BF),
        vs=V((T, D), BF),
        os=V((T, D), BF),
        ps=V((NQ, WIDE, T), F32),
        x1=V((T, D), F32),
        h2=V((T, D), BF),
        x2=V((T, D), F32),
        oc=V((T, D), BF),
        dx=V((T, D), F32),
        lse=V((16, T), F32),
        qc=V((Z, Y, T, D), BF),
        h3=V((Z, T, D), BF),
        g3=V((Z, T, D), BF),
        do=V((Z, Y, T, D), BF),
        dr=V((Z, Y, 16, 128), F32),
        po=V((Y, Z, T, D), BF),
        pst=V((Y, Z, 16, T), F32),
        ryo=V((Y - 1, Z, T, D), BF),
        ryst=V((Y - 1, Z, 16, T), F32),
        rzo=V((Z - 1, T, D), BF),
        rzst=V((Z - 1, 16, T), F32),
        py=V((Z, T, D), BF),
        rzy=V((Z - 1, T, D), BF),
        gl=V((Z * T, hid), BF),
        du=V((Z * T, hid), BF),
        sm=V((8, D), F32),
        rsm=V((1 + (X - 1) + (Y - 1) + (Z - 1), 8, D), F32),
        ssem=pltpu.SemaphoreType.DMA((sems(sz),)),
        rsem=pltpu.SemaphoreType.DMA((sems(sz),)),
        lsem=pltpu.SemaphoreType.DMA((1 + Y * Z,)),
    )


TAIL = (
    "ck",
    "cv",
    "CO",
    "FI",
    "FO",
    "pass",
    "CK",
    "CV",
    "rows1",
    "CO",
    "dq",
    "FI",
    "cq",
    "so",
    "CK",
    "FO",
    "selfback",
    "CQ",
    "FO",
    "CO",
    "sv",
    "SO",
    "sq",
    "FI",
    "sk",
    "CV",
    "SV",
    "CK",
    "dh1",
    "small",
    "SQ",
    "SK",
    "rows2",
    "small",
    "CQ",
    "CV",
    "bo",
    "CK",
    "SO",
    "SV",
    "CV",
    "CQ",
    "SQ",
    "SO",
    "CQ",
    "SQ",
    "SK",
    "small",
    "SO",
    "SV",
    "SQ",
    "SK",
    "small",
    "SV",
    "SK",
    "small",
)

INPUTS = (
    "tok", "pas_in", "len", "og", "ls", "rel", "sq", "skv", "so",
    "lc", "cq", "ckv", "co", "lf", "fi_in", "fo_in",
)
OUTPUTS = (
    "bo", "tg", "pg", "g_ls", "g_rb", "g_sq", "g_skv", "g_so",
    "g_lc", "g_cq", "g_ckv", "g_co", "g_lf", "g_fi", "g_fo",
)


def block_kernel(sz, names, *refs):
    n_in, n_out = len(INPUTS), len(OUTPUTS)
    m = dict(zip(INPUTS, refs[:n_in]))
    m.update(zip(OUTPUTS, refs[n_in : n_in + n_out]))
    m.update(zip(names, refs[n_in + n_out :]))
    for name in ("gw", "smb", "fip", "rc", "r1a", "r1b", "r2a", "r2b", "rz"):
        if name in m:
            m[name] = Spot(m[name])
    X, Y, Z, D, T, R = sz.X, sz.Y, sz.Z, sz.D, sz.T, sz.R
    r, rb, nh, hid = sz.r, sz.rb, sz.nh, sz.hid
    NQ = HEADS // QUAD
    YZ = Y * Z
    dp = lax.axis_index("dp")
    fs = lax.axis_index("fsdp")
    x, c = dp // 2, dp % 2
    z, y = fs // Y, fs % Y
    oth = 1 - c

    ring_x = [(x + b) % X for b in range(X)]
    ring_y = [(y + b) % Y for b in range(Y)]
    ring_z = [(z + b) % Z for b in range(Z)]

    def around(ring, at, b):
        return ring[b] if isinstance(b, int) else (at + b) % len(ring)

    def xs(b):
        return around(ring_x, x, b)

    def ys(b):
        return around(ring_y, y, b)

    def zs(b):
        return around(ring_z, z, b)

    def any_dev(x_=None, c_=None, y_=None, z_=None):
        x_ = x if x_ is None else x_
        c_ = c if c_ is None else c_
        y_ = y if y_ is None else y_
        z_ = z if z_ is None else z_
        return (x_ * 2 + c_, z_ * Y + y_)

    near = {}

    def dev(x_=None, c_=None, y_=None, z_=None):
        key = (id(x_), id(c_), id(y_), id(z_))
        if key not in near:
            return any_dev(x_, c_, y_, z_)
        return near[key]

    none = id(None)
    near[(none, id(oth), none, none)] = any_dev(c_=oth)
    for v in ring_x:
        near[(id(v), none, none, none)] = any_dev(x_=v)
    for v in ring_y:
        near[(none, none, id(v), none)] = any_dev(y_=v)
    for v in ring_z:
        near[(none, none, none, id(v))] = any_dev(z_=v)

    ssem, rsem, lsem = m["ssem"], m["rsem"], m["lsem"]
    n_sems = sems(sz)
    used = [0]
    pending = []

    spare = []
    early = [False, []]

    def take(n=1):
        if n == 1 and spare:
            return spare.pop(0)
        at = used[0]
        used[0] += n
        assert used[0] <= n_sems
        return at

    def copy_at(i, src, dst, to):
        src = src.ref() if isinstance(src, Spot) else src
        dst = dst.ref() if isinstance(dst, Spot) else dst
        return pltpu.make_async_remote_copy(
            src_ref=src, dst_ref=dst, send_sem=ssem.at[i], recv_sem=rsem.at[i],
            device_id=to, device_id_type=pl.DeviceIdType.MESH,
        )

    def send(src, dst, to):
        i = take()
        if early[0]:
            early[1].append(i)
        cp = Sent(lambda: copy_at(i, src, dst, to))
        cp.make().start()
        pending.append(cp)
        return cp

    def got(cps):
        for cp in cps:
            cp.wait_recv()

    def sent(cps):
        for cp in cps:
            cp.wait_send()
        pending[:] = [cp for cp in pending if all(cp is not done for done in cps)]

    def drain():
        sent(list(pending))

    partners = [dev(c_=oth)]
    partners += [dev(x_=xs(b)) for b in range(1, X)]
    partners += [dev(y_=ys(b)) for b in range(1, Y)]
    partners += [dev(z_=zs(b)) for b in range(1, Z)]
    bar = pltpu.get_barrier_semaphore()
    for p in partners:
        pl.semaphore_signal(bar, inc=1, device_id=p, device_id_type=pl.DeviceIdType.MESH)
    load_pas = pltpu.make_async_copy(m["pas_in"], m["pas"], lsem.at[0])
    load_pas.start()
    pl.semaphore_wait(bar, len(partners))

    mask = m["mask"]
    mask[...] = (iota((WIDE, WIDE), 0) // DK == iota((WIDE, WIDE), 1) // DK).astype(F32).astype(BF)

    def stack4(v):
        return jnp.concatenate([v, v, v, v], axis=0) * mask[...]

    def fold4(u):
        lane = iota((T, WIDE), 1)
        out = u[0:T]
        for h in range(1, QUAD):
            out = jnp.where(lane >= h * DK, u[h * T : (h + 1) * T], out)
        return out

    def quad(t):
        return slice(t * WIDE, (t + 1) * WIDE)

    cell, lift = m["cell"], m["lift"]

    def put_halves(dst, left, right, rows, total):
        if rows % 8 == 0 and 2 * rows == total:
            dst[...] = jnp.concatenate([left, right], axis=0).astype(BF)
        else:
            cols = left.shape[1]
            cell[0:total, 0:cols] = jnp.zeros((total, cols), F32)
            cell[0:rows, 0:cols] = left
            cell[rows : 2 * rows, 0:cols] = right
            dst[...] = cell[0:total, 0:cols].astype(BF)

    def get_halves(v, rows):
        if rows % 8 == 0:
            return v[0:rows], v[rows : 2 * rows]
        cell[0 : v.shape[0], 0 : v.shape[1]] = v
        return cell[0:rows, 0 : v.shape[1]], cell[rows : 2 * rows, 0 : v.shape[1]]

    gw, w, smb = m["gw"], m["w"], m["smb"]

    def line_to(buf, over_y, blocks):
        out = []
        for k in blocks:
            block = buf.at[c, x, y, k]
            if over_y:
                out += [send(block, block, dev(y_=ys(b))) for b in range(1, Y)]
            else:
                out += [send(block, block, dev(x_=xs(b))) for b in range(1, X)]
        return out

    class Gather:
        def __init__(self, buf, y_first, feed="gather", first=False):
            self.first = first
            early[0] = first
            self.buf, self.y_first, self.feed = buf, y_first, feed
            own = buf.at[c, x, y, z]
            self.z = []
            for a in range(1, Z):
                if feed == "gather":
                    self.z.append(send(own, own, dev(z_=zs(a))))
                elif feed == "exchange":
                    self.z.append(send(m["fip"].at[zs(a)], own, dev(z_=zs(a))))
            early[0] = False

        def own_out(self):
            early[0] = self.first
            blocks = range(Z) if self.feed == "local" else [z]
            self.second = line_to(self.buf, self.y_first, blocks)
            self.third = line_to(self.buf, not self.y_first, blocks)
            early[0] = False

        def line_out(self):
            early[0] = self.first
            got(self.z)
            if self.feed != "local":
                blocks = [zs((Z - a) % Z) for a in range(1, Z)]
                self.second += line_to(self.buf, self.y_first, blocks)
                self.third += line_to(self.buf, not self.y_first, blocks)
            early[0] = False

        def plane_out(self):
            early[0] = self.first
            got(self.second)
            buf = self.buf
            if self.y_first:
                for b in range(1, Y):
                    line = buf.at[c, x, ys(b)]
                    self.third += [send(line, line, dev(x_=xs(d))) for d in range(1, X)]
            else:
                for b in range(1, X):
                    line = buf.at[c, xs(b), y]
                    self.third += [send(line, line, dev(y_=ys(d))) for d in range(1, Y)]
            early[0] = False

        def core_out(self):
            early[0] = self.first
            got(self.third)
            self.core = [send(self.buf.at[c], self.buf.at[c], dev(c_=oth))]
            early[0] = False

        def end(self):
            got(self.core)

    own_small = [jnp.zeros((16, 128), F32)]
    for at, key in enumerate(("ls", "lc", "lf", "rel")):
        v = m[key][...].astype(F32)
        v = jnp.concatenate([v, jnp.zeros((1, 128 - v.shape[1]), F32)], axis=1)
        own_small[0] = jnp.where(iota((16, 128), 0) == at, v, own_small[0])
    smb[c, x, y, z] = own_small[0].astype(BF)
    moves = {}

    def begin(p, feed="gather"):
        moves[p] = Gather(gw.at[p], p not in Y_GATHERED_LAST, feed, p < CO)

    moves["small"] = Gather(smb, True, first=True)
    moves["small"].own_out()
    sources = (
        (m["sq"], 0), (m["skv"], 0), (m["skv"], D), (m["so"], 0),
        (m["cq"], 0), (m["ckv"], 0), (m["ckv"], D), (m["co"], 0),
    )

    def pack(p):
        ref, off = sources[p]
        v = ref[:, off : off + D].astype(F32)
        put_halves(gw.at[p, c, x, y, z], v[:, 0:nh], v[:, nh:D], r, rb)
        begin(p)
        moves[p].own_out()

    for p in (SQ, SK, SV, SO, CQ, CK, CV, CO):
        pack(p)

    g3 = m["g3"]
    live = (iota((T, 1), 0) < m["len"][0]).astype(F32)
    g3[z] = (live * m["og"][...]).astype(BF)

    def line_start(base, buf):
        for a in range(1, Z):
            copy_at(base + a, buf.at[z], buf.at[z], dev(z_=zs(a))).start()

    def line_wait(base, buf):
        for a in range(1, Z):
            copy_at(base + a, buf.at[z], buf.at[z], dev(z_=zs(a))).wait_recv()

    def line_done(base, buf):
        for a in range(1, Z):
            copy_at(base + a, buf.at[z], buf.at[z], dev(z_=zs(a))).wait_send()

    def act_start(base, bufs):
        for n, buf in enumerate(bufs):
            for a in range(1, Z):
                copy_at(base + n * YZ + a, buf.at[z, y], buf.at[z, y], dev(z_=zs(a))).start()

    def act_forward(base, bufs, a):
        zi = zs(a)
        for n, buf in enumerate(bufs):
            for b in range(1, Y):
                copy_at(
                    base + n * YZ + b * Z + (Z - a) % Z, buf.at[zi, y], buf.at[zi, y], dev(y_=ys(b))
                ).start()

    def act_wait(base, bufs, t):
        at = base + (Y - t // Z) % Y * Z + (Z - t % Z) % Z
        for n, buf in enumerate(bufs):
            copy_at(at + n * YZ, buf.at[z, y], buf.at[z, y], dev(z_=zs(1))).wait_recv()

    def act_done(base, bufs):
        for n, buf in enumerate(bufs):
            for t in range(1, YZ):
                copy_at(base + n * YZ + t, buf.at[z, y], buf.at[z, y], dev(z_=zs(1))).wait_send()

    fip = m["fip"]
    ndp = 2 * X
    per = D // ndp

    def pack_ff():
        even = m["even"]
        for k in range(Z):
            for i in range(ndp):
                at = (i * Z + k) * per
                even[:, i * per : (i + 1) * per] = m["fi_in"][:, at : at + per].astype(F32)
            put_halves(fip.at[k], even[:, 0:nh], even[:, nh:D], r, rb)
        vo = m["fo_in"][...].astype(F32)
        if r % 8:
            lift[0 : Z * r, :] = vo
        for k in range(Z):
            part = lift[k * r : k * r + r, :] if r % 8 else vo[k * r : k * r + r]
            put_halves(gw.at[FO, c, x, y, k], part[:, 0:nh], part[:, nh:D], r, rb)
        gw[FI, c, x, y, z] = fip[z]

    g3_base = take(Z)

    spread = m["spread"]
    lane = iota((16, D), 1)
    row = iota((16, D), 0)
    spread[...] = ((lane >= row * DK) & (lane < row * DK + DK)).astype(F32)
    m["spread2"][...] = jnp.concatenate([spread[...], spread[...]], axis=0).astype(BF)
    tlane = iota((T, 128), 1)
    rbs = HEADS * BUCKETS // (2 * X * YZ)

    def repeat_of(width, step):
        l0, n0 = iota((128, width), 0), iota((128, width), 1)

        def body(k, tot):
            return tot + ((n0 - l0 == k * step) & (l0 < step)).astype(F32)

        return lax.fori_loop(0, width // step, body, jnp.zeros((128, width), F32)).astype(BF)

    m["hot_gain"][...] = repeat_of(D, r)
    m["hot_bias"][...] = repeat_of(HEADS * BUCKETS, rbs)

    def unpack(p):
        group = 2 * Y * r

        if p == FO:
            group = YZ * r
            parts = [(yy, zz) for yy in range(Y) for zz in range(Z)]
        else:
            parts = [(yy, zz) for zz in range(2) for yy in range(Y)]
        per = YZ // len(parts)

        def body(g, carry):
            x_ = g // (2 * per)
            c_ = (g // per) % 2
            zp = 0 if per == 1 else g % per
            lefts, rights = [], []
            at = 0
            for yy, zz in parts:
                lo, hi = get_halves(gw[p, c_, x_, yy, 2 * zp + zz].astype(F32), r)
                if r % 8 == 0:
                    lefts.append(lo)
                    rights.append(hi)
                else:
                    lift[at : at + r, 0:nh] = lo
                    lift[at : at + r, nh:D] = hi
                at += r
            rows = pl.ds(pl.multiple_of(g * group, 16), group)
            if r % 8 == 0:
                w[p, rows, 0:nh] = jnp.concatenate(lefts, axis=0).astype(BF)
                w[p, rows, nh:D] = jnp.concatenate(rights, axis=0).astype(BF)
            else:
                w[p, rows, :] = lift[0:group, :].astype(BF)
            return carry

        lax.fori_loop(0, X * 2 * per, body, 0)

    gain = m["gain"]
    bias = m["bias"]
    def read_small():
        flat = HEADS * BUCKETS
        every = smb[...].reshape(2 * X * YZ * 16, 128)
        wide_g, wide_b = nn(every, m["hot_gain"][...]), nn(every, m["hot_bias"][...])
        ng, nb = iota((16, D), 1), iota((16, flat), 1)
        gains, tot = jnp.zeros((16, D), F32), jnp.zeros((16, flat), F32)
        at = 0
        for c_ in range(2):
            for x_ in range(X):
                for y_ in range(Y):
                    for z_ in range(Z):
                        k = (x_ * 2 + c_) * YZ + z_ * Y + y_
                        mine = (ng >= k * r) & (ng < k * r + r)
                        gains = jnp.where(mine, wide_g[at : at + 16], gains)
                        mine = (nb >= k * rbs) & (nb < k * rbs + rbs)
                        tot = jnp.where(mine, wide_b[at : at + 16], tot)
                        at += 16
        gain[...] = gains
        per = jnp.broadcast_to(tot[3:4, :], (16, flat))
        h0, n0 = iota((16, flat), 0), iota((16, flat), 1)
        per = jnp.where((n0 >= h0 * BUCKETS) & (n0 < h0 * BUCKETS + BUCKETS), per, 0.0)
        nb, mb = iota((flat, 128), 0), iota((flat, 128), 1)
        dist = jnp.where(mb == 0, 0, 128 - mb)
        hot = ((nb & (BUCKETS - 1)) == bucket_of(dist)).astype(F32).astype(BF)
        table = nn(per.astype(BF), hot)
        for h in range(HEADS):
            wide = jnp.broadcast_to(table[h : h + 1, :], (T, 128))
            rolled = pltpu.roll(wide, 0, 1, stride=1, stride_axis=0)
            bias[h // QUAD, (h % QUAD) * T : (h % QUAD + 1) * T, :] = rolled[:, 0:T]

    tok = m["tok"]

    def self_forward():
        m["h1"][...] = normed(tok[...], gain[0:1, :]).astype(BF)
        h1 = m["h1"][...]
        m["qs"][...] = nn(h1, w[SQ]).astype(BF)
        m["ks"][...] = nn(h1, w[SK]).astype(BF)
        m["vs"][...] = nn(h1, w[SV]).astype(BF)
        allowed = iota((WIDE, T), 1) <= (iota((WIDE, T), 0) & (T - 1))
        for t in range(NQ):
            s = nt(stack4(m["qs"][:, quad(t)]), m["ks"][:, quad(t)]) + bias[t]
            s = jnp.where(allowed, s, NEG)
            e = jnp.exp(s - jnp.max(s, axis=1, keepdims=True))
            pr = e / jnp.sum(e, axis=1, keepdims=True)
            m["ps"][t] = pr
            m["os"][:, quad(t)] = fold4(nn(pr.astype(BF), m["vs"][:, quad(t)])).astype(BF)

    qc = m["qc"]
    qc_base = take(YZ)

    def self_out():
        x1 = tok[...] + nn(m["os"][...], w[SO])
        m["x1"][...] = x1
        m["h2"][...] = normed(x1, gain[1:2, :]).astype(BF)

    def cross_query():
        qc[z, y] = nn(m["h2"][...], w[CQ]).astype(BF)
        act_start(qc_base, [qc])
        act_forward(qc_base, [qc], 0)

    kv, pas = m["kv"], m["pas"]

    chunk = 4 if R % 16 == 0 else 1

    def project(p, off):
        def part(k, carry):
            rows = pl.ds(k // NQ * chunk, chunk)
            at = k % NQ * WIDE
            cols = pl.ds(pl.multiple_of(at, WIDE), WIDE)
            v = nn(pas[rows].reshape(chunk * R, D), w[p, :, cols])
            cols = pl.ds(pl.multiple_of(off + at, WIDE), WIDE)
            kv[rows, :, cols] = v.astype(BF).reshape(chunk, R, WIDE)
            return carry

        lax.fori_loop(0, YZ // chunk * NQ, part, 0)

    def project_one(q, p, off):
        kv[q, :, off : off + D] = nn(pas[q], w[p]).astype(BF)

    def after(p):
        unpack(p)
        if p == SQ:
            moves["small"].end()
            read_small()
        elif p == SV:
            self_forward()
        elif p == SO:
            self_out()
        elif p == CQ:
            cross_query()
        elif p == CK:
            load_pas.wait()
            project(CK, 0)

    order = (SQ, SK, SV, SO, CQ, CK, CV, CO, FI, FO)

    def line_out(k):
        if k == 0:
            moves["small"].line_out()
        moves[order[k]].line_out()

    def plane_out(k):
        if k == 0:
            moves["small"].plane_out()
        moves[order[k]].plane_out()

    def core_out(k):
        if k == 0:
            moves["small"].core_out()
        moves[order[k]].core_out()

    def arrive(k):
        moves[order[k]].end()
        after(order[k])

    def query_out(a):
        act_wait(qc_base, [qc], a)
        act_forward(qc_base, [qc], a)

    line_out(0)
    line_out(1)
    pack_ff()
    begin(FI, "exchange")
    plane_out(0)
    line_out(2)
    plane_out(1)
    line_out(3)
    core_out(0)
    plane_out(2)
    arrive(0)
    line_out(4)
    core_out(1)
    plane_out(3)
    arrive(1)
    line_out(5)
    core_out(2)
    plane_out(4)
    arrive(2)
    line_out(6)
    core_out(3)
    plane_out(5)
    arrive(3)
    core_out(4)
    arrive(4)
    line_start(g3_base, g3)
    plane_out(6)
    core_out(5)
    line_out(7)
    begin(FO, "local")
    moves[FI].own_out()
    moves[FO].own_out()
    line_out(8)
    line_out(9)
    arrive(5)
    query_out(1)
    core_out(6)
    query_out(2)
    arrive(6)
    plane_out(7)
    query_out(3)

    po, pst, ryo, ryst, rzo, rzst = (m[k] for k in ("po", "pst", "ryo", "ryst", "rzo", "rzst"))

    def rs_y_base():
        return take((Y - 1) * Z)

    def rs_y_send(base, src, dst, b, a):
        zi = zs(a)
        copy_at(base + (b - 1) * Z + a, src.at[b, zi], dst.at[b - 1, zi], dev(y_=ys(b))).start()

    def rs_y_wait(base, src, dst, b, a):
        copy_at(base + (b - 1) * Z + a, src.at[b, 0], dst.at[b - 1, 0], dev(y_=ys(1))).wait_recv()

    def rs_y_done(base, src, dst):
        for b in range(1, Y):
            for a in range(Z):
                copy_at(
                    base + (b - 1) * Z + a, src.at[b, 0], dst.at[b - 1, 0], dev(y_=ys(1))
                ).wait_send()

    yo_base, yst_base = rs_y_base(), rs_y_base()
    zo_base, zst_base = take(Z), take(Z)

    def attend(a, b):
        zi = zs(a)
        yi = ys(b)
        qi = zi * Y + yi
        st = jnp.zeros((T, 128), F32)
        for k in range(NQ):
            qb = stack4(qc[zi, yi, :, quad(k)])
            s = nt(qb, kv[qi, :, quad(k)])
            top = jnp.max(s, axis=1, keepdims=True)
            e = jnp.exp(s - top)
            tot = jnp.sum(e, axis=1, keepdims=True)
            u = nn(e.astype(BF), kv[qi, :, D + k * WIDE : D + (k + 1) * WIDE])
            po[b, zi, :, quad(k)] = fold4(u * (1.0 / tot)).astype(BF)
            lse = top + jnp.log(tot)
            for h in range(QUAD):
                st = jnp.where(tlane == k * QUAD + h, lse[h * T : (h + 1) * T], st)
        pst[b, zi] = st.T[0:16]

    def expand(st):
        return lax.dot_general(
            st, spread[...], (((0,), (0,)), ((), ())), preferred_element_type=F32, precision=HIGH
        )

    def expand_low(v):
        hi = v.astype(BF)
        lo = (v - hi.astype(F32)).astype(BF)
        both = jnp.concatenate([hi, lo], axis=0)
        ones = m["spread2"][...]
        return tn(both, ones)

    def merge(parts):
        top = parts[0][1]
        for _, st in parts[1:]:
            top = jnp.maximum(top, st)
        ws = [jnp.exp(st - top) for _, st in parts]
        tot = ws[0]
        for v in ws[1:]:
            tot = tot + v
        out = jnp.zeros((T, D), F32)
        for (o, _), v in zip(parts, ws):
            out = out + expand_low(v / tot) * o.astype(F32)
        return out, top + jnp.log(tot)

    def z_send(base, src, dst, a):
        zi = zs(a)
        copy_at(base + a, src.at[0, zi], dst.at[a - 1], dev(z_=zi)).start()

    def z_each(base, src, dst, wait):
        for a in range(1, Z):
            cp = copy_at(base + a, src.at[0, 0], dst.at[a - 1], dev(z_=zs(a)))
            if wait == "recv":
                cp.wait_recv()
            else:
                cp.wait_send()

    def pass_on(a):
        zi = zs(a)
        for b in range(1, Y):
            rs_y_wait(yo_base, po, ryo, b, a)
            rs_y_wait(yst_base, pst, ryst, b, a)
        o, st = merge(
            [(po[0, zi], pst[0, zi])] + [(ryo[b - 1, zi], ryst[b - 1, zi]) for b in range(1, Y)]
        )
        po[0, zi] = o.astype(BF)
        pst[0, zi] = st
        z_send(zo_base, po, rzo, a)
        z_send(zst_base, pst, rzst, a)

    def attend_step(t, carry):
        a = (1 + t % Z) % Z
        b = (1 + t // Z) % Y

        project_one(zs(a) * Y + ys(b), CV, D)

        @pl.when(b > 0)
        def _():
            act_wait(qc_base, [qc], b * Z + a)

        attend(a, b)

        @pl.when(b > 0)
        def _():
            rs_y_send(yo_base, po, ryo, b, a)
            rs_y_send(yst_base, pst, ryst, b, a)

        @pl.when((b == 0) & (a > 0))
        def _():
            pass_on(a)

        @pl.when(t == YZ - Z - 1)
        def _():
            core_out(7)

        @pl.when(t == 1)
        def _():
            plane_out(8)
            plane_out(9)

        return carry

    lax.fori_loop(0, YZ, attend_step, 0)
    arrive(7)
    for b in range(1, Y):
        rs_y_wait(yo_base, po, ryo, b, 0)
        rs_y_wait(yst_base, pst, ryst, b, 0)
    z_each(zo_base, po, rzo, "recv")
    z_each(zst_base, pst, rzst, "recv")
    o, lse = merge(
        [(po[0, z], pst[0, z])]
        + [(ryo[b - 1, z], ryst[b - 1, z]) for b in range(1, Y)]
        + [(rzo[a - 1], rzst[a - 1]) for a in range(1, Z)]
    )
    m["oc"][...] = o.astype(BF)
    m["lse"][...] = lse
    x2 = m["x1"][...] + nn(m["oc"][...], w[CO])
    m["x2"][...] = x2
    h3 = m["h3"]
    h3[z] = normed(x2, gain[2:3, :]).astype(BF)
    h3_base = take(Z)
    line_start(h3_base, h3)

    core_out(8)
    core_out(9)
    arrive(8)
    line_wait(g3_base, g3)
    arrive(9)
    gb = g3[...].reshape(Z * T, D)
    m["kvacc"].at[0 : Z * T, 0:hid][...] = nt(gb, w[FO])
    act_done(qc_base, [qc])
    rs_y_done(yo_base, po, ryo)
    rs_y_done(yst_base, pst, ryst)
    z_each(zo_base, po, rzo, "send")
    z_each(zst_base, pst, rzst, "send")
    drain()
    py, rzy = m["py"], m["rzy"]
    gl, du = m["gl"], m["du"]
    line_wait(h3_base, h3)
    act, slope = gelu_pair(nn(h3[...].reshape(Z * T, D), w[FI]))
    du[...] = (m["kvacc"].at[0 : Z * T, 0:hid][...] * slope).astype(BF)
    gl[...] = act.astype(BF)
    po[0] = nt(du[...], w[FI]).astype(BF).reshape(Z, T, D)

    def rs_z(part, rzb):
        return [send(part.at[zs(a)], rzb.at[a - 1], dev(z_=zs(a))) for a in range(1, Z)]

    def rs_total(part, rzb):
        tot = part[z].astype(F32)
        for a in range(1, Z):
            tot = tot + rzb[a - 1].astype(F32)
        return tot

    zh = rs_z(po.at[0], rzo)
    py[...] = nn(gl[...], w[FO]).astype(BF).reshape(Z, T, D)
    line_done(h3_base, h3)
    line_done(g3_base, g3)

    acc = m["kvacc"].at[:, 0:D]

    def add_to(dst, src):
        dst[...] = (dst[...].astype(F32) + src[...].astype(F32)).astype(BF)

    def add_blocks(rows, dst, src):
        def body(i, carry):
            add_to(dst(i // Z, i % Z), src(i // Z, i % Z))
            return carry

        lax.fori_loop(0, rows * Z, body, 0)

    rc, r1a, r1b, r2a, r2b, rz = (m.get(k) for k in ("rc", "r1a", "r1b", "r2a", "r2b", "rz"))

    def pack_grad(p, acc, col):
        group = YZ * r
        if not sz.inside:
            name, off = targets[p]
            out = m[name] if p in (FI, FO) else m[name].at[:, off : off + D]
            cp = pltpu.make_async_copy(acc.at[:, col : col + D], out, lsem.at[0])
            cp.start()
            cp.wait()
            return None

        def body(k, carry):
            x_ = k // 2
            c_ = k % 2
            for z_ in range(Z):
                for y_ in range(Y):
                    at = (y_ * Z + z_) * r if p == FO else (z_ * Y + y_) * r
                    rows = pl.ds(pl.multiple_of(k * group + at, 8), r)
                    left, right = acc[rows, col : col + nh], acc[rows, col + nh : col + D]
                    put_halves(gw.at[p, c_, x_, y_, z_], left, right, r, rb)
            return carry

        lax.fori_loop(0, 2 * X, body, 0)
        return [send(gw.at[p, oth], rc.at[p], dev(c_=oth))]

    def rs_first(p, cps):
        got(cps)

        add_blocks(
            X * Y,
            lambda k, z_: gw.at[p, c, k // Y, k % Y, z_],
            lambda k, z_: rc.at[p, k // Y, k % Y, z_],
        )
        if p in X_LAST:
            return [
                send(gw.at[p, c, xs(b)], r1a.at[X_LAST.index(p), b - 1], dev(x_=xs(b))) for b in range(1, X)
            ]
        return [
            send(gw.at[p, c, :, ys(b)], r1b.at[Y_LAST.index(p), b - 1], dev(y_=ys(b))) for b in range(1, Y)
        ]

    def rs_second(p, cps):
        got(cps)
        if p in X_LAST:
            for b in range(1, X):
                add_blocks(
                    Y,
                    lambda k, z_: gw.at[p, c, x, k, z_],
                    lambda k, z_: r1a.at[X_LAST.index(p), b - 1, k, z_],
                )
            return [
                send(gw.at[p, c, x, ys(b)], r2a.at[X_LAST.index(p), b - 1], dev(y_=ys(b)))
                for b in range(1, Y)
            ]
        for b in range(1, Y):
            add_blocks(
                X,
                lambda k, z_: gw.at[p, c, k, y, z_],
                lambda k, z_: r1b.at[Y_LAST.index(p), b - 1, k, z_],
            )
        return [
            send(gw.at[p, c, xs(b), y], r2b.at[Y_LAST.index(p), b - 1], dev(x_=xs(b))) for b in range(1, X)
        ]

    def rs_third(p, cps):
        got(cps)
        if p in X_LAST:
            for b in range(1, Y):
                add_blocks(
                    1,
                    lambda k, z_: gw.at[p, c, x, y, z_],
                    lambda k, z_: r2a.at[X_LAST.index(p), b - 1, z_],
                )
        else:
            for b in range(1, X):
                add_blocks(
                    1,
                    lambda k, z_: gw.at[p, c, x, y, z_],
                    lambda k, z_: r2b.at[Y_LAST.index(p), b - 1, z_],
                )
        if p == FO:
            return []
        return [
            send(gw.at[p, c, x, y, zs(a)], rz.at[p, a - 1], dev(z_=zs(a))) for a in range(1, Z)
        ]

    targets = {
        SQ: ("g_sq", 0), SK: ("g_skv", 0), SV: ("g_skv", D), SO: ("g_so", 0),
        CQ: ("g_cq", 0), CK: ("g_ckv", 0), CV: ("g_ckv", D), CO: ("g_co", 0),
        FI: ("g_fi", 0), FO: ("g_fo", 0),
    }

    def rs_last(p, cps):
        got(cps)
        name, off = targets[p]
        if p in (FI, FO):
            for a in range(Z):
                k = a if p == FO else zs((Z - a) % Z)
                if p == FO:
                    v = gw[p, c, x, y, a]
                else:
                    v = rz[p, a - 1] if a else gw[p, c, x, y, z]
                lo, hi = get_halves(v.astype(F32), r)
                if p == FI:
                    m["kvacc"][pl.ds(pl.multiple_of(k * r, 8), r), 0:nh] = lo
                    m["kvacc"][pl.ds(pl.multiple_of(k * r, 8), r), nh:D] = hi
                else:
                    m[name][k * r : k * r + r, 0:nh] = lo
                    m[name][k * r : k * r + r, nh:D] = hi
            if p == FI:
                for k in range(Z):
                    for i in range(ndp):
                        at = (i * Z + k) * per
                        m[name][:, at : at + per] = m["kvacc"][k * r : k * r + r, i * per : (i + 1) * per]
            return None
        v = gw[p, c, x, y, z].astype(F32)
        for a in range(1, Z):
            v = v + rz[p, a - 1].astype(F32)
        lo, hi = get_halves(v, r)
        m[name][:, off : off + nh] = lo
        m[name][:, off + nh : off + D] = hi

    stages = (rs_first, rs_second, rs_third, rs_last) if sz.inside else ()
    moving = {}

    def grad_of(p, lhs, rhs):
        def part(k, carry):
            cols = pl.ds(pl.multiple_of(k * WIDE, WIDE), WIDE)
            left = lhs[:, :, cols].reshape(Z * T, WIDE) if len(lhs.shape) == 3 else lhs[:, cols]
            acc[cols, :] = tn(left, rhs[...])
            return carry

        lax.fori_loop(0, NQ, part, 0)
        grad_out(p)

    def grad_out(p, src=None, col=0):
        moving[p] = (0, pack_grad(p, acc if src is None else src, col))

    def push(p):
        k, cps = moving[p]
        if k < len(stages):
            moving[p] = (k + 1, stages[k](p, cps))

    def push_all(ps):
        for p in ps:
            push(p)

    spare.extend(early[1])
    grad_of(FO, gl, gb)
    grad_of(FI, h3, du)
    push_all([FO, FI])
    sm = m["sm"]
    sm[...] = jnp.zeros_like(sm)
    got(zh)
    dh3 = rs_total(po.at[0], rzo)
    dv, gg = norm_back(m["x2"][...], gain[2:3, :], dh3)
    sm[2:3, :] = gg
    dx2 = live * m["og"][...] + dv
    m["dx"][...] = dx2
    dx2l = dx2.astype(BF)
    doc = nt(dx2l, w[CO]).astype(BF)
    do, dr = m["do"], m["dr"]
    do[z, y] = doc
    pick = iota((T, D), 0) == (iota((T, D), 1) & (T - 1))

    def as_rows(st):
        v = jnp.sum(jnp.where(pick, expand(st), 0.0), axis=0, keepdims=True)
        parts = [v[:, k * 128 : (k + 1) * 128] for k in range(D // 128)]
        return jnp.concatenate(parts + [jnp.zeros((8 - D // 128, 128), F32)], axis=0)

    prod = doc.astype(F32) * m["oc"][...].astype(F32)
    delta = lax.dot_general(
        spread[...], prod, (((1,), (1,)), ((), ())), preferred_element_type=F32, precision=HIGH
    )
    dr[z, y, 0:8] = as_rows(m["lse"][...])
    dr[z, y, 8:16] = as_rows(delta)
    do_base = take(2 * YZ)
    act_start(do_base, [do, dr])
    act_forward(do_base, [do, dr], 0)
    zy = rs_z(py, rzy)
    grad_of(CO, m["oc"], dx2l)

    sent(zh)
    yq_base = rs_y_base()

    def row_of(ref, k):
        return jnp.concatenate([ref[2 * k : 2 * k + 1, :], ref[2 * k + 1 : 2 * k + 2, :]], axis=1)

    zq_base = take(Z)

    def pass_back(a):
        zi = zs(a)
        for b in range(1, Y):
            rs_y_wait(yq_base, po, ryo, b, a)
        tot = po[0, zi].astype(F32)
        for b in range(1, Y):
            tot = tot + ryo[b - 1, zi].astype(F32)
        po[0, zi] = tot.astype(BF)
        z_send(zq_base, po, rzo, a)

    def attend_back(a, b):
        zi = zs(a)
        yi = ys(b)
        qi = zi * Y + yi

        lse_rows = dr[zi, yi, 0:8]
        delta_rows = dr[zi, yi, 8:16]
        for k in range(NQ):
            qb = stack4(qc[zi, yi, :, quad(k)])
            db = stack4(do[zi, yi, :, quad(k)])
            kt = kv[qi, :, quad(k)]
            vt = kv[qi, :, D + k * WIDE : D + (k + 1) * WIDE]
            pt = jnp.exp(nt(kt, qb) - row_of(lse_rows, k))
            ds = (pt * (nt(vt, db) - row_of(delta_rows, k))).astype(BF)
            po[b, zi, :, quad(k)] = fold4(tn(ds, kt)).astype(BF)
            kv[qi, :, quad(k)] = nn(ds, qb).astype(BF)
            kv[qi, :, D + k * WIDE : D + (k + 1) * WIDE] = nn(pt.astype(BF), db).astype(BF)


    kvacc = m["kvacc"]

    def kv_grad(q):
        def part(k, carry):
            cols = pl.ds(pl.multiple_of(k * WIDE, WIDE), WIDE)
            kvacc[cols, :] += tn(pas[q, :, cols], kv[q])
            return carry

        lax.fori_loop(0, NQ, part, 0)

    def back_step(t, carry):
        a = t % Z
        b = t // Z

        @pl.when(t > 0)
        def _():
            act_wait(do_base, [do, dr], t)

        @pl.when((t > 0) & (t < Z))
        def _():
            act_forward(do_base, [do, dr], a)

        attend_back(a, b)

        @pl.when(t >= Z)
        def _():
            rs_y_send(yq_base, po, ryo, b, a)

        @pl.when(t == 1)
        def _():
            push(CO)

        kv_grad(zs(a) * Y + ys(b))

        return carry

    kvacc[...] = jnp.zeros_like(kvacc)
    lax.fori_loop(0, YZ, back_step, 0)
    def row_grads(k0, k1):
        def whole(k, carry):
            pas[k] = (nt(kv[k, :, 0:D], w[CK]) + nt(kv[k, :, D : 2 * D], w[CV])).astype(BF)
            pltpu.make_async_copy(pas.at[k], m["pg"].at[k], lsem.at[1 + k]).start()
            return carry

        def part(k, carry):
            rows = pl.ds(k // NQ * chunk, chunk)
            cols = pl.ds(pl.multiple_of(k % NQ * WIDE, WIDE), WIDE)
            v = nt(kv[rows, :, 0:D].reshape(chunk * R, D), w[CK, cols, :])
            v = v + nt(kv[rows, :, D : 2 * D].reshape(chunk * R, D), w[CV, cols, :])
            pas[rows, :, cols] = v.astype(BF).reshape(chunk, R, WIDE)

            @pl.when(k % NQ == NQ - 1)
            def _():
                for q in range(chunk):
                    at = k // NQ * chunk + q
                    pltpu.make_async_copy(pas.at[at], m["pg"].at[at], lsem.at[1 + at]).start()

            return carry

        if chunk == 1:
            lax.fori_loop(k0, k1, whole, 0)
        else:
            lax.fori_loop(k0 * NQ, k1 * NQ, part, 0)

    half = YZ // chunk // 2
    held = {}

    def take_dq():
        for b in range(1, Y):
            rs_y_wait(yq_base, po, ryo, b, 0)
        z_each(zq_base, po, rzo, "recv")
        dqc = rs_total(po.at[0], rzo)
        for b in range(1, Y):
            dqc = dqc + ryo[b - 1, z].astype(F32)
        held["dqc"] = dqc.astype(BF)
        dh2 = nt(held["dqc"], w[CQ])
        dv, gg = norm_back(m["x1"][...], gain[1:2, :], dh2)
        sm[1:2, :] = gg
        dx1 = m["dx"][...] + dv
        m["dx"][...] = dx1
        held["dx1l"] = dx1.astype(BF)

    def self_back():
        m["oc"][...] = nt(held["dx1l"], w[SO]).astype(BF)
        grads = [[], [], []]
        held["tail"] = []
        back = (iota((T, 128), 1) == T - 1 - iota((T, 128), 0)).astype(F32).astype(BF)
        for t in range(NQ):
            db = stack4(m["oc"][:, quad(t)])
            qb = stack4(m["qs"][:, quad(t)])
            pr = m["ps"][t]
            dps = nt(db, m["vs"][:, quad(t)])
            dss = (pr * (dps - jnp.sum(pr * dps, axis=1, keepdims=True))).astype(BF)
            grads[0].append(fold4(nn(dss, m["ks"][:, quad(t)])).astype(BF))
            grads[1].append(tn(dss, qb).astype(BF))
            grads[2].append(tn(pr.astype(BF), db).astype(BF))
            turned = nn(dss, back)
            for h in range(QUAD):
                part = pltpu.roll(turned[h * T : (h + 1) * T], 0, 1, stride=1, stride_axis=0)
                held["tail"].append(jnp.sum(part, axis=0, keepdims=True))
        held["dqs"], held["dks"], held["dvs"] = (jnp.concatenate(g, axis=1) for g in grads)

    def token_grad():
        dh1 = nt(held["dqs"], w[SQ]) + nt(held["dks"], w[SK]) + nt(held["dvs"], w[SV])
        dv, gg = norm_back(tok[...], gain[0:1, :], dh1)
        sm[0:1, :] = gg
        m["tg"][...] = m["dx"][...] + dv
        flat = HEADS * BUCKETS
        diag = jnp.concatenate(held["tail"] + [jnp.zeros((16 - HEADS, 128), F32)], axis=0)
        mi, bi = iota((128, 128), 0), iota((128, 128), 1)
        hot = ((mi >= T - 1) & (bucket_of(mi - (T - 1)) == bi) & (bi < BUCKETS)).astype(F32)
        table = nn_high(diag, hot)
        bb, nb = iota((128, flat), 0), iota((128, flat), 1)
        wide = nn_high(table, ((nb & (BUCKETS - 1)) == bb).astype(F32))
        h0, n0 = iota((16, flat), 0), iota((16, flat), 1)
        own = (n0 >= h0 * BUCKETS) & (n0 < h0 * BUCKETS + BUCKETS)
        sm[3:4, 0:flat] = jnp.sum(jnp.where(own, wide, 0.0), axis=0, keepdims=True)

    rsm = m["rsm"]
    slot = [0]

    def small_to(devs):
        held["small"] = []
        for to in devs:
            held["small"].append((slot[0], send(sm, rsm.at[slot[0]], to)))
            slot[0] += 1

    def small_got():
        got([cp for _, cp in held["small"]])
        sent([cp for _, cp in held["small"]])
        for k, _ in held["small"]:
            sm[...] += rsm[k]

    def small_step(k):
        if k:
            small_got()
        if k < 4:
            small_to(
                (
                    [dev(c_=oth)],
                    [dev(x_=xs(b)) for b in range(1, X)],
                    [dev(y_=ys(b)) for b in range(1, Y)],
                    [dev(z_=zs(a)) for a in range(1, Z)],
                )[k]
            )

    def block_out():
        got(zy)
        m["bo"][...] = live * (m["x2"][...] + rs_total(py, rzy))

    steps = {
        "ck": lambda: grad_out(CK, kvacc, 0),
        "cv": lambda: grad_out(CV, kvacc, D),
        "pass": lambda: [pass_back(a) for a in range(1, Z)],
        "rows1": lambda: row_grads(0, half),
        "rows2": lambda: row_grads(half, YZ // chunk),
        "dq": take_dq,
        "cq": lambda: grad_of(CQ, m["h2"], held["dqc"]),
        "so": lambda: grad_of(SO, m["os"], held["dx1l"]),
        "selfback": self_back,
        "sv": lambda: grad_of(SV, m["h1"], held["dvs"]),
        "sq": lambda: grad_of(SQ, m["h1"], held["dqs"]),
        "sk": lambda: grad_of(SK, m["h1"], held["dks"]),
        "dh1": token_grad,
        "bo": block_out,
    }
    pieces = dict(SQ=SQ, SK=SK, SV=SV, SO=SO, CQ=CQ, CK=CK, CV=CV, CO=CO, FI=FI, FO=FO)
    small_at = [0]

    def run(name):
        if name == "small":
            small_step(small_at[0])
            small_at[0] += 1
        elif name in pieces:
            push(pieces[name])
        else:
            steps[name]()

    for name in TAIL:
        run(name)
    assert all(k == len(stages) for k, _ in moving.values()), moving
    assert small_at[0] == 5
    me = dp * YZ + fs
    nd, ld = iota((D, 128), 0), iota((D, 128), 1)
    mine = nn_high(sm[...], ((nd == me * r + ld) & (ld < r)).astype(F32))
    mine_b = nn_high(sm[...], ((nd == me * rbs + ld) & (ld < rbs)).astype(F32))
    m["g_ls"][...] = mine[0:1, 0:r]
    m["g_lc"][...] = mine[1:2, 0:r]
    m["g_lf"][...] = mine[2:3, 0:r]
    m["g_rb"][...] = mine_b[3:4, 0:rbs]

    act_done(do_base, [do, dr])
    rs_y_done(yq_base, po, ryo)
    z_each(zq_base, po, rzo, "send")
    drain()

    def pg_wait(q, carry):
        pltpu.make_async_copy(pas.at[q], m["pg"].at[q], lsem.at[1 + q]).wait()
        return carry

    lax.fori_loop(0, YZ, pg_wait, 0)


def place_kernel(*refs):
    n = len(OUTPUTS)
    given, put, held, sem = refs[:n], refs[n : 2 * n], refs[2 * n : 3 * n], refs[3 * n]
    loads = [pltpu.make_async_copy(given[k], held[k], sem.at[k]) for k in range(n)]
    stores = [pltpu.make_async_copy(held[k], put[k], sem.at[n + k]) for k in range(n)]
    for cp in loads:
        cp.start()
    for load, store in zip(loads, stores):
        load.wait()
        store.start()
    for cp in stores:
        cp.wait()


def per_device(
    sz,
    targets, passages, tgt_len, out_grad, ln_self, rel_bias, self_q, self_kv, self_out,
    ln_cross, cross_q, cross_kv, cross_out, ln_ff, ff_in, ff_out,
):
    T, D, r, Z = sz.T, sz.D, sz.r, sz.Z
    ndp = 2 * sz.X
    per = sz.Y * sz.rff
    scratch = layout(sz)
    names = tuple(scratch)
    gr = r if sz.inside else D
    vm = pl.BlockSpec(memory_space=pltpu.VMEM)
    hbm = pl.BlockSpec(memory_space=pltpu.HBM)
    smem = pl.BlockSpec(memory_space=pltpu.SMEM)
    shape = jax.ShapeDtypeStruct
    rbs = rel_bias.shape[0]
    out_shape = (
        shape((T, D), F32), shape((T, D), F32), shape(passages.shape, BF),
        shape((1, r), F32), shape((1, rbs), F32),
        shape((gr, D), F32), shape((gr, 2 * D), F32), shape((gr, D), F32),
        shape((1, r), F32), shape((gr, D), F32), shape((gr, 2 * D), F32), shape((gr, D), F32),
        shape((1, r), F32),
        shape((r, Z * D) if sz.inside else (D, D), F32),
        shape((Z * r, D) if sz.inside else (D, D), F32),
    )
    weight_outs = ("g_sq", "g_skv", "g_so", "g_cq", "g_ckv", "g_co", "g_fi", "g_fo")
    apart = ("pg",) if sz.inside else ("pg",) + weight_outs
    outs = pl.pallas_call(
        functools.partial(block_kernel, sz, names),
        out_shape=out_shape,
        in_specs=[{"pas_in": hbm, "len": smem}.get(n, vm) for n in INPUTS],
        out_specs=tuple(hbm if n in apart else vm for n in OUTPUTS),
        scratch_shapes=tuple(scratch.values()),
        compiler_params=pltpu.CompilerParams(
            collective_id=0, has_side_effects=True, vmem_limit_bytes=63 * 2**20
        ),
        cost_estimate=pl.CostEstimate(
            flops=20 * 10**9, bytes_accessed=2 * 10**7, transcendentals=4 * 10**6
        ),
    )(
        targets[0], passages, tgt_len, out_grad[0], ln_self[None], rel_bias[None],
        self_q, self_kv, self_out, ln_cross[None], cross_q, cross_kv, cross_out,
        ln_ff[None], ff_in, ff_out,
    )
    (bo, tg, pg, g_ls, g_rb, g_sq, g_skv, g_so, g_lc, g_cq, g_ckv, g_co, g_lf, g_fi, g_fo) = outs
    if not sz.inside:
        at = lax.axis_index("fsdp") // sz.Y
        rows = jnp.zeros((ndp, Z, per, D), F32).at[:, at].set(g_fo.reshape(ndp, per, D))
        cols = jnp.zeros((D, ndp, Z, per), F32).at[:, :, at].set(g_fi.reshape(D, ndp, per))
        g_sq, g_skv, g_so, g_cq, g_ckv, g_co, g_fi, g_fo = (
            lax.psum_scatter(g, ("dp", "fsdp"), scatter_dimension=0, tiled=True)
            for g in (
                g_sq, g_skv, g_so, g_cq, g_ckv, g_co,
                cols.reshape(D, Z * D), rows.reshape(Z * D, D),
            )
        )
    outs = (bo, tg, pg, g_ls, g_rb, g_sq, g_skv, g_so, g_lc, g_cq, g_ckv, g_co, g_lf, g_fi, g_fo)
    if sz.inside:
        outs = pl.pallas_call(
            place_kernel,
            out_shape=tuple(shape(o.shape, o.dtype) for o in outs),
            in_specs=[hbm] * len(outs),
            out_specs=(hbm,) * len(outs),
            scratch_shapes=tuple(pltpu.VMEM(o.shape, o.dtype) for o in outs)
            + (pltpu.SemaphoreType.DMA((2 * len(outs),)),),
            compiler_params=pltpu.CompilerParams(vmem_limit_bytes=63 * 2**20),
        )(*outs)
    (bo, tg, pg, g_ls, g_rb, g_sq, g_skv, g_so, g_lc, g_cq, g_ckv, g_co, g_lf, g_fi, g_fo) = outs
    return (
        bo[None], tg[None], pg, g_ls[0], g_rb[0], g_sq, g_skv, g_so,
        g_lc[0], g_cq, g_ckv, g_co, g_lf[0], g_fi, g_fo,
    )


def solution(mesh):
    both = ("dp", "fsdp")
    rows3, rows2, rows1 = P(both, None, None), P(both, None), P(both)
    placed = (
        rows3, P("dp", "fsdp", None), rows1, rows3, rows1, rows1, rows2, rows2, rows2,
        rows1, rows2, rows2, rows2, rows1, rows2, rows2,
    )
    outs = (
        rows3, rows3, P("dp", "fsdp", None), rows1, rows1, rows2, rows2, rows2,
        rows1, rows2, rows2, rows2, rows1, rows2, rows2,
    )

    def run(*args):
        targets, passages, self_q, ff_out = args[0], args[1], args[6], args[15]
        sz = Sizes(
            mesh.shape,
            targets.shape[2], passages.shape[1], targets.shape[1],
            self_q.shape[0], ff_out.shape[0],
            ff_out.shape[0] * mesh.shape["dp"] * mesh.shape["fsdp"] // ZDIM,
        )
        return per_device(sz, *args)

    return jax.shard_map(run, mesh=mesh, in_specs=placed, out_specs=outs, check_vma=False)
```

```python
import functools
import math

import jax
import jax.numpy as jnp
from jax import lax
from jax.experimental import pallas as pl
from jax.experimental.pallas import tpu as pltpu
from jax.sharding import PartitionSpec as P

HEADS = 12
DK = 64
BUCKETS = 32
QUAD = 4
WIDE = QUAD * DK
EPS = 1e-06
NEG = -1e30
HIGH = lax.Precision.HIGHEST
BF = jnp.bfloat16
F32 = jnp.float32
PIECES = 10
SQ, SK, SV, SO, CQ, CK, CV, CO, FI, FO = range(PIECES)
WIDE_PIECES = (CK, CV, FI, FO)
Y_SUMMED_FIRST = (CK, CV)
FACTORS = {SQ: "h1", SK: "h1", SV: "h1", SO: "os", CQ: "h2", CO: "oc"}
ACTS = ("h1", "os", "h2", "oc")
Y_GATHERED_LAST = (SQ, SV, CQ)
ZDIM = 4


def up16(n):
    return (n + 15) // 16 * 16


def bucket_limits():
    limits = []
    for target_bucket in range(1, 16):
        distance = 16
        while int(math.log(distance / 16.0) / math.log(8.0) * 16.0) < target_bucket:
            distance = distance + 1
        limits.append(distance)
    return limits


def bucket_of(distance):
    larger = jnp.full_like(distance, 16)
    for limit_value in bucket_limits():
        larger = larger + (distance >= limit_value).astype(jnp.int32)
    return jnp.where(distance < 16, distance, jnp.minimum(larger, 31))


def iota(shape, axis):
    return lax.broadcasted_iota(jnp.int32, shape, axis)


def nn(a, b):
    return lax.dot_general(a, b, (((1,), (0,)), ((), ())), preferred_element_type=F32)


def nt(a, b):
    return lax.dot_general(a, b, (((1,), (1,)), ((), ())), preferred_element_type=F32)


def tn(a, b):
    return lax.dot_general(a, b, (((0,), (0,)), ((), ())), preferred_element_type=F32)


def nn_high(a, b):
    return lax.dot_general(
        a, b, (((1,), (0,)), ((), ())), preferred_element_type=F32, precision=HIGH
    )


def normed(v, gain):
    return v * lax.rsqrt(jnp.mean(v * v, axis=-1, keepdims=True) + EPS) * gain


def norm_back(v, gain, dy):
    s = lax.rsqrt(jnp.mean(v * v, axis=-1, keepdims=True) + EPS)
    dyg = dy * gain
    gain_grad = jnp.sum(dy * v * s, axis=0, keepdims=True)
    dv = s * dyg - v * (s * s * s) * jnp.mean(dyg * v, axis=-1, keepdims=True)
    return dv, gain_grad


def gelu_pair(u):
    cst = 0.7978845608028654
    cubic = 0.044715
    th = jnp.tanh(cst * (u + cubic * u * u * u))
    half = 0.5 * (1.0 + th)
    slope = half + 0.5 * u * (1.0 - th * th) * cst * (1.0 + 3.0 * cubic * u * u)
    return u * half, slope


class Buffers:
    pass


class Spot:
    def __init__(self, base, steps=()):
        self.base, self.steps = base, steps

    @property
    def at(self):
        return Steps(self)

    def ref(self):
        out = self.base
        for step in self.steps:
            out = out.at[step]
        return out

    def __getitem__(self, key):
        return self.ref()[key]

    def __setitem__(self, key, value):
        self.ref()[key] = value


class Steps:
    def __init__(self, spot):
        self.spot = spot

    def __getitem__(self, key):
        return Spot(self.spot.base, self.spot.steps + (key,))


class Sent:
    def __init__(self, make):
        self.make = make

    def wait_recv(self):
        self.make().wait_recv()

    def wait_send(self):
        self.make().wait_send()


class Sizes:
    def __init__(self, mesh_shape, width, rows, targets, shard, ff_shard, hidden):
        self.Z = ZDIM
        self.X = mesh_shape["dp"] // 2
        self.Y = mesh_shape["fsdp"] // self.Z
        self.D = width
        self.R = rows
        self.T = targets
        self.r = shard
        self.rb = up16(2 * shard)
        self.nh = width // 2
        self.inside = shard % 8 == 0
        self.rff = ff_shard
        self.hid = hidden
        assert ff_shard == self.Z * shard and hidden == width


def sems(sz):
    return 156 if sz.inside else 900


def layout(sz):
    X, Y, Z, D, T, R = sz.X, sz.Y, sz.Z, sz.D, sz.T, sz.R
    rb, nh, hid = sz.rb, sz.nh, sz.hid
    nw = len(WIDE_PIECES)
    NQ = HEADS // QUAD
    V = pltpu.VMEM
    sums = dict(
        rc=V((nw, X, Y, Z, rb, nh), BF),
        r1=V((nw, X - 1, Y, Z, rb, nh), BF),
        r1y=V((nw, Y - 1, X, Z, rb, nh), BF),
        r2x=V((nw, X - 1, Z, rb, nh), BF),
        r2=V((PIECES, Y - 1, Z, rb, nh), BF),
        rz=V((PIECES, 3, rb, nh), BF),
        act=V((len(ACTS), X, 2, T, D), BF),
        cot=V((PIECES, X, 2, T, D), BF),
    )
    return dict(
        **(sums if sz.inside else {}),
        gw=V((PIECES, 2, X, Y, Z, rb, nh), BF),
        w=V((PIECES, D, D), BF),
        fip=V((Z, rb, nh), BF),
        kvacc=V((D, 2 * D), F32),
        lift=V((max(Y * Z * sz.r, sz.rff) if sz.r % 8 else 8, D), F32),
        even=V((sz.r, D), F32),
        cell=V((rb, nh), F32),
        smb=V((2, X, Y, Z, 16, 128), BF),
        hot_gain=V((128, D), BF),
        hot_bias=V((128, HEADS * BUCKETS), BF),
        gain=V((16, D), F32),
        bias=V((NQ, WIDE, T), F32),
        spread=V((16, D), F32),
        spread2=V((32, D), BF),
        mask=V((WIDE, WIDE), BF),
        pas=V((Y * Z, R, D), BF),
        kv=V((Y * Z, R, 2 * D), BF),
        h1=V((T, D), BF),
        qs=V((T, D), BF),
        ks=V((T, D), BF),
        vs=V((T, D), BF),
        os=V((T, D), BF),
        ps=V((NQ, WIDE, T), F32),
        x1=V((T, D), F32),
        h2=V((T, D), BF),
        x2=V((T, D), F32),
        oc=V((T, D), BF),
        dx=V((T, D), F32),
        lse=V((16, T), F32),
        qc=V((Z, Y, T, D), BF),
        h3=V((Z, T, D), BF),
        g3=V((Z, T, D), BF),
        do=V((Z, Y, T, D), BF),
        dr=V((Z, Y, 16, 128), F32),
        po=V((Y, Z, T, D), BF),
        pst=V((Y, Z, 16, T), F32),
        ryo=V((Y - 1, Z, T, D), BF),
        ryst=V((Y - 1, Z, 16, T), F32),
        rzo=V((Z - 1, T, D), BF),
        rzst=V((Z - 1, 16, T), F32),
        py=V((Z, T, D), BF),
        rzy=V((Z - 1, T, D), BF),
        gl=V((Z * T, hid), BF),
        du=V((Z * T, hid), BF),
        sm=V((8, D), F32),
        rsm=V((1 + (X - 1) + (Y - 1) + (Z - 1), 8, D), F32),
        ssem=pltpu.SemaphoreType.DMA((sems(sz),)),
        rsem=pltpu.SemaphoreType.DMA((sems(sz),)),
        lsem=pltpu.SemaphoreType.DMA((1 + Y * Z,)),
    )


(
    DO_CK, DO_CV, DO_PASS, DO_ROWS1, DO_ROWS2, DO_ROWS3,
    DO_ROWS4, DO_DQ, DO_CQ, DO_SO, DO_SELFBACK, DO_SV,
    DO_SQ, DO_SK, DO_DH1, DO_BO, DO_SMALL,
) = range(PIECES, PIECES + 17)
TAIL = (
    FO, DO_CK, DO_CV, CO, FO, FO, DO_PASS, CK,
    CV, DO_ROWS1, FI, CO, DO_DQ, DO_CQ, DO_SO, DO_SELFBACK,
    DO_SV, DO_SQ, DO_SK, DO_DH1, DO_SMALL, CK, DO_BO, FI,
    CQ, FI, DO_SMALL, CO, SO, CQ, DO_ROWS2, SV,
    SO, CV, CO, SQ, SV, SK, CQ, SQ,
    DO_ROWS3, SK, CK, SO, DO_SMALL, CQ, DO_ROWS4, SV,
    CV, CK, SQ, SO, CQ, SV, SK, DO_SMALL,
    CV, CK, SQ, SO, SV, SK, DO_SMALL, CV,
    SQ, SK,
)

SPOTS = ("gw", "smb", "fip", "rc", "r1", "r1y", "r2", "r2x", "rz", "act", "cot")
INPUTS = (
    "tok", "pas_in", "len", "og", "ls", "rel", "sq", "skv", "so",
    "lc", "cq", "ckv", "co", "lf", "fi_in", "fo_in",
)
OUTPUTS = (
    "bo", "tg", "pg", "g_ls", "g_rb", "g_sq", "g_skv", "g_so",
    "g_lc", "g_cq", "g_ckv", "g_co", "g_lf", "g_fi", "g_fo",
)


def block_kernel(sz, names, *refs):
    m = Buffers()
    vars(m).update(zip(INPUTS + OUTPUTS + names, refs))
    for name in SPOTS:
        if hasattr(m, name):
            setattr(m, name, Spot(getattr(m, name)))
    X, Y, Z, D, T, R = sz.X, sz.Y, sz.Z, sz.D, sz.T, sz.R
    r, rb, nh, hid = sz.r, sz.rb, sz.nh, sz.hid
    NQ = HEADS // QUAD
    YZ = Y * Z
    dp = lax.axis_index("dp")
    fs = lax.axis_index("fsdp")
    x, c = dp // 2, dp % 2
    z, y = fs // Y, fs % Y
    oth = 1 - c

    ring_x = [(x + b) % X for b in range(X)]
    ring_y = [(y + b) % Y for b in range(Y)]
    ring_z = [(z + b) % Z for b in range(Z)]

    def around(ring, at, b):
        return ring[b] if isinstance(b, int) else (at + b) % len(ring)

    def xs(b):
        return around(ring_x, x, b)

    def ys(b):
        return around(ring_y, y, b)

    def zs(b):
        return around(ring_z, z, b)

    def any_dev(x_=None, c_=None, y_=None, z_=None):
        x_ = x if x_ is None else x_
        c_ = c if c_ is None else c_
        y_ = y if y_ is None else y_
        z_ = z if z_ is None else z_
        return (x_ * 2 + c_, z_ * Y + y_)

    near = {}

    def dev(x_=None, c_=None, y_=None, z_=None):
        key = (id(x_), id(c_), id(y_), id(z_))
        if key not in near:
            return any_dev(x_, c_, y_, z_)
        return near[key]

    none = id(None)
    near[(none, id(oth), none, none)] = any_dev(c_=oth)
    for v in ring_x:
        near[(id(v), none, none, none)] = any_dev(x_=v)
    for v in ring_y:
        near[(none, none, id(v), none)] = any_dev(y_=v)
    for v in ring_z:
        near[(none, none, none, id(v))] = any_dev(z_=v)

    z_near = z + 1 - 2 * (z % 2)
    z_far = ring_z[2]
    z_cross = (z_near + 2) % Z
    near[(none, none, none, id(z_near))] = any_dev(z_=z_near)

    ssem, rsem, lsem = m.ssem, m.rsem, m.lsem
    n_sems = sems(sz)
    used = [0]
    pending = []

    spare = []
    early = [False, []]

    def take(n=1):
        if n == 1 and spare:
            return spare.pop(0)
        if n == 0:
            return 0
        at = used[0]
        used[0] += n
        assert used[0] <= n_sems
        return at

    def copy_at(i, src, dst, to):
        src = src.ref() if isinstance(src, Spot) else src
        dst = dst.ref() if isinstance(dst, Spot) else dst
        return pltpu.make_async_remote_copy(
            src_ref=src, dst_ref=dst, send_sem=ssem.at[i], recv_sem=rsem.at[i],
            device_id=to, device_id_type=pl.DeviceIdType.MESH,
        )

    def send(src, dst, to):
        i = take()
        cp = Sent(lambda: copy_at(i, src, dst, to))
        cp.make().start()
        pending.append(cp)
        return cp

    def got(cps):
        for cp in cps:
            cp.wait_recv()

    def sent(cps):
        for cp in cps:
            cp.wait_send()
        pending[:] = [cp for cp in pending if all(cp is not done for done in cps)]

    def drain():
        sent(list(pending))

    partners = [dev(c_=oth)]
    partners += [dev(x_=xs(b)) for b in range(1, X)]
    partners += [dev(y_=ys(b)) for b in range(1, Y)]
    partners += [dev(z_=zs(b)) for b in range(1, Z)]
    bar = pltpu.get_barrier_semaphore()
    for p in partners:
        pl.semaphore_signal(bar, inc=1, device_id=p, device_id_type=pl.DeviceIdType.MESH)
    load_pas = pltpu.make_async_copy(m.pas_in, m.pas, lsem.at[0])
    load_pas.start()
    pl.semaphore_wait(bar, len(partners))

    mask = m.mask
    mask[...] = (iota((WIDE, WIDE), 0) // DK == iota((WIDE, WIDE), 1) // DK).astype(F32).astype(BF)

    def stack4(v):
        return jnp.concatenate([v, v, v, v], axis=0) * mask[...]

    def fold4(u):
        lane = iota((T, WIDE), 1)
        out = u[0:T]
        for h in range(1, QUAD):
            out = jnp.where(lane >= h * DK, u[h * T : (h + 1) * T], out)
        return out

    def quad(t):
        return slice(t * WIDE, (t + 1) * WIDE)

    cell, lift = m.cell, m.lift

    def put_halves(dst, left, right, rows, total):
        if rows % 8 == 0 and 2 * rows == total:
            dst[...] = jnp.concatenate([left, right], axis=0).astype(BF)
        else:
            cols = left.shape[1]
            cell[0:total, 0:cols] = jnp.zeros((total, cols), F32)
            cell[0:rows, 0:cols] = left
            cell[rows : 2 * rows, 0:cols] = right
            dst[...] = cell[0:total, 0:cols].astype(BF)

    def get_halves(v, rows):
        if rows % 8 == 0:
            return v[0:rows], v[rows : 2 * rows]
        cell[0 : v.shape[0], 0 : v.shape[1]] = v
        return cell[0:rows, 0 : v.shape[1]], cell[rows : 2 * rows, 0 : v.shape[1]]

    gw, w, smb = m.gw, m.w, m.smb

    class Gather:

        def __init__(self, buf, y_first, feed="gather", first=False):
            self.buf, self.y_first, self.feed = buf, y_first, feed
            self.iz, self.iy, self.ix, self.ic = take(), take(Y - 1), take(X - 1), take()
            self.far = take() if feed == "gather" else 0
            if first:
                early[1].extend([self.iz, self.ic, self.far])
                early[1].extend(range(self.iy, self.iy + Y - 1))
                early[1].extend(range(self.ix, self.ix + X - 1))
            if feed == "exchange":
                own = buf.at[c, x, y, z]
                for a in range(1, Z):
                    copy_at(self.iz, m.fip.at[zs(a)], own, dev(z_=zs(a))).start()
                some = buf.at[c, x, y, 0 : Z - 1]
                pending.append(Sent(lambda: copy_at(self.iz, some, some, dev(z_=z_near))))

        def z_out(self):
            own = self.buf.at[c, x, y, z]
            copy_at(self.far, own, own, dev(z_=z_far)).start()
            copy_at(self.iz, own, own, dev(z_=z_near)).start()

        def pair_out(self):
            block = self.buf.at[c, x, y, z_far]
            far = Sent(lambda: copy_at(self.far, block, block, dev(z_=z_far)))
            far.wait_recv()
            copy_at(self.iz, block, block, dev(z_=z_near)).start()
            pair = self.buf.at[c, x, y, 0:2]
            pending.extend([far, Sent(lambda: copy_at(self.iz, pair, pair, dev(z_=z_near)))])
            self.over(self.y_first, block)
            self.over(not self.y_first, block)

        def over(self, is_y, block):
            if is_y:
                for b in range(1, Y):
                    copy_at(self.iy + b - 1, block, block, dev(y_=ys(b))).start()
            else:
                for b in range(1, X):
                    copy_at(self.ix + b - 1, block, block, dev(x_=xs(b))).start()

        def own_out(self):
            at = (c, x, y) if self.feed == "local" else (c, x, y, z)
            self.over(self.y_first, self.buf.at[at])
            self.over(not self.y_first, self.buf.at[at])

        def line_out(self):
            if self.feed == "local":
                return
            if self.feed == "gather":
                some = self.buf.at[c, x, y, 0:2]
                blocks = (z_near, z_cross)
            else:
                some = self.buf.at[c, x, y, 0 : Z - 1]
                blocks = ring_z[1:]
            copy_at(self.iz, some, some, dev(z_=z_near)).wait_recv()
            for k in blocks:
                block = self.buf.at[c, x, y, k]
                self.over(self.y_first, block)
                self.over(not self.y_first, block)

        def arrived(self, is_y, all_of_it):
            buf = self.buf
            if is_y:
                ref = buf.at[c, 0 : X, y] if all_of_it else buf.at[c, x, y]
                for b in range(1, Y):
                    yield Sent(
                        lambda b=b: copy_at(self.iy + b - 1, ref, ref, dev(y_=ys(b)))
                    )
            else:
                ref = buf.at[c, x] if all_of_it else buf.at[c, x, y]
                for b in range(1, X):
                    yield Sent(
                        lambda b=b: copy_at(self.ix + b - 1, ref, ref, dev(x_=xs(b)))
                    )

        def plane_out(self):
            second = list(self.arrived(self.y_first, False))
            got(second)
            pending.extend(second)
            if self.y_first:
                for b in range(1, Y):
                    self.over(False, self.buf.at[c, x, ys(b)])
            else:
                for b in range(1, X):
                    self.over(True, self.buf.at[c, xs(b), y])

        def core_out(self):
            third = list(self.arrived(not self.y_first, True))
            got(third)
            pending.extend(third)
            plane = self.buf.at[c]
            self.core = [Sent(lambda: copy_at(self.ic, plane, plane, dev(c_=oth)))]
            self.core[0].make().start()
            pending.extend(self.core)
            self.last = third + self.core

        def end(self):
            got(self.core)

    own_small = [jnp.zeros((16, 128), F32)]
    for at, key in enumerate(("ls", "lc", "lf", "rel")):
        v = getattr(m, key)[...].astype(F32)
        v = jnp.concatenate([v, jnp.zeros((1, 128 - v.shape[1]), F32)], axis=1)
        own_small[0] = jnp.where(iota((16, 128), 0) == at, v, own_small[0])
    smb[c, x, y, z] = own_small[0].astype(BF)
    moves = {}

    def begin(p, feed="gather"):
        moves[p] = Gather(gw.at[p], p not in Y_GATHERED_LAST, feed, p < CO)

    moves["small"] = Gather(smb, True, first=True)
    moves["small"].z_out()
    moves["small"].own_out()
    sources = (
        (m.sq, 0), (m.skv, 0), (m.skv, D), (m.so, 0),
        (m.cq, 0), (m.ckv, 0), (m.ckv, D), (m.co, 0),
    )

    def pack(p):
        ref, off = sources[p]
        v = ref[:, off : off + D].astype(F32)
        put_halves(gw.at[p, c, x, y, z], v[:, 0:nh], v[:, nh:D], r, rb)
        begin(p)
        if p in (SQ, SK, SV):
            moves[p].z_out()
        moves[p].own_out()

    for p in (SQ, SK, SV, SO, CQ, CK, CV, CO):
        pack(p)

    g3 = m.g3
    live = (iota((T, 1), 0) < m.len[...]).astype(F32)
    g3[z] = (live * m.og[...]).astype(BF)

    def line_start(base, buf):
        for a in range(1, Z):
            copy_at(base + a, buf.at[z], buf.at[z], dev(z_=zs(a))).start()

    def line_wait(base, buf):
        for a in range(1, Z):
            copy_at(base + a, buf.at[z], buf.at[z], dev(z_=zs(a))).wait_recv()

    def line_done(base, buf):
        for a in range(1, Z):
            copy_at(base + a, buf.at[z], buf.at[z], dev(z_=zs(a))).wait_send()

    def act_start(base, bufs):
        for n, buf in enumerate(bufs):
            for a in range(1, Z):
                copy_at(base + n * YZ + a, buf.at[z, y], buf.at[z, y], dev(z_=zs(a))).start()

    def act_forward(base, bufs, a):
        zi = zs(a)
        for n, buf in enumerate(bufs):
            for b in range(1, Y):
                copy_at(
                    base + n * YZ + b * Z + (Z - a) % Z, buf.at[zi, y], buf.at[zi, y], dev(y_=ys(b))
                ).start()

    def act_wait(base, bufs, t):
        at = base + (Y - t // Z) % Y * Z + (Z - t % Z) % Z
        for n, buf in enumerate(bufs):
            copy_at(at + n * YZ, buf.at[z, y], buf.at[z, y], dev(z_=zs(1))).wait_recv()

    def act_done(base, bufs):
        for n, buf in enumerate(bufs):
            for t in range(1, YZ):
                copy_at(base + n * YZ + t, buf.at[z, y], buf.at[z, y], dev(z_=zs(1))).wait_send()

    fip = m.fip
    ndp = 2 * X
    per = D // ndp

    def pack_ff():
        even = m.even
        for k in range(Z):
            for i in range(ndp):
                at = (i * Z + k) * per
                even[:, i * per : (i + 1) * per] = m.fi_in[:, at : at + per].astype(F32)
            put_halves(fip.at[k], even[:, 0:nh], even[:, nh:D], r, rb)
        vo = m.fo_in[...].astype(F32)
        if r % 8:
            lift[0 : Z * r, :] = vo
        for k in range(Z):
            part = lift[k * r : k * r + r, :] if r % 8 else vo[k * r : k * r + r]
            put_halves(gw.at[FO, c, x, y, k], part[:, 0:nh], part[:, nh:D], r, rb)
        gw[FI, c, x, y, z] = fip[z]

    g3_base = take(Z)

    spread = m.spread
    lane = iota((16, D), 1)
    row = iota((16, D), 0)
    spread[...] = ((lane >= row * DK) & (lane < row * DK + DK)).astype(F32)
    m.spread2[...] = jnp.concatenate([spread[...], spread[...]], axis=0).astype(BF)
    tlane = iota((T, 128), 1)
    rbs = HEADS * BUCKETS // (2 * X * YZ)

    def repeat_of(width, step):
        l0, n0 = iota((128, width), 0), iota((128, width), 1)

        def body(k, tot):
            return tot + ((n0 - l0 == k * step) & (l0 < step)).astype(F32)

        return lax.fori_loop(0, width // step, body, jnp.zeros((128, width), F32)).astype(BF)

    m.hot_gain[...] = repeat_of(D, r)
    m.hot_bias[...] = repeat_of(HEADS * BUCKETS, rbs)

    def unpack(p):
        group = 2 * Y * r

        if p == FO:
            group = YZ * r
            parts = [(yy, zz) for yy in range(Y) for zz in range(Z)]
        else:
            parts = [(yy, zz) for zz in range(2) for yy in range(Y)]
        per = YZ // len(parts)

        def body(g, carry):
            x_ = g // (2 * per)
            c_ = (g // per) % 2
            zp = 0 if per == 1 else g % per
            lefts, rights = [], []
            at = 0
            for yy, zz in parts:
                lo, hi = get_halves(gw[p, c_, x_, yy, 2 * zp + zz].astype(F32), r)
                if r % 8 == 0:
                    lefts.append(lo)
                    rights.append(hi)
                else:
                    lift[at : at + r, 0:nh] = lo
                    lift[at : at + r, nh:D] = hi
                at += r
            rows = pl.ds(pl.multiple_of(g * group, 16), group)
            if r % 8 == 0:
                w[p, rows, 0:nh] = jnp.concatenate(lefts, axis=0).astype(BF)
                w[p, rows, nh:D] = jnp.concatenate(rights, axis=0).astype(BF)
            else:
                w[p, rows, :] = lift[0:group, :].astype(BF)
            return carry

        lax.fori_loop(0, X * 2 * per, body, 0)

    gain = m.gain
    bias = m.bias
    def read_small():
        flat = HEADS * BUCKETS
        every = smb[...].reshape(2 * X * YZ * 16, 128)
        wide_g, wide_b = nn(every, m.hot_gain[...]), nn(every, m.hot_bias[...])
        ng, nb = iota((16, D), 1), iota((16, flat), 1)
        gains, tot = jnp.zeros((16, D), F32), jnp.zeros((16, flat), F32)
        at = 0
        for c_ in range(2):
            for x_ in range(X):
                for y_ in range(Y):
                    for z_ in range(Z):
                        k = (x_ * 2 + c_) * YZ + z_ * Y + y_
                        mine = (ng >= k * r) & (ng < k * r + r)
                        gains = jnp.where(mine, wide_g[at : at + 16], gains)
                        mine = (nb >= k * rbs) & (nb < k * rbs + rbs)
                        tot = jnp.where(mine, wide_b[at : at + 16], tot)
                        at += 16
        gain[...] = gains
        per = jnp.broadcast_to(tot[3:4, :], (16, flat))
        h0, n0 = iota((16, flat), 0), iota((16, flat), 1)
        per = jnp.where((n0 >= h0 * BUCKETS) & (n0 < h0 * BUCKETS + BUCKETS), per, 0.0)
        nb, mb = iota((flat, 128), 0), iota((flat, 128), 1)
        dist = jnp.where(mb == 0, 0, 128 - mb)
        hot = ((nb & (BUCKETS - 1)) == bucket_of(dist)).astype(F32).astype(BF)
        table = nn(per.astype(BF), hot)
        for h in range(HEADS):
            wide = jnp.broadcast_to(table[h : h + 1, :], (T, 128))
            rolled = pltpu.roll(wide, 0, 1, stride=1, stride_axis=0)
            bias[h // QUAD, (h % QUAD) * T : (h % QUAD + 1) * T, :] = rolled[:, 0:T]

    tok = m.tok

    def self_forward():
        m.h1[...] = normed(tok[...], gain[0:1, :]).astype(BF)
        h1 = m.h1[...]
        m.qs[...] = nn(h1, w[SQ]).astype(BF)
        m.ks[...] = nn(h1, w[SK]).astype(BF)
        m.vs[...] = nn(h1, w[SV]).astype(BF)
        allowed = iota((WIDE, T), 1) <= (iota((WIDE, T), 0) & (T - 1))
        for t in range(NQ):
            s = nt(stack4(m.qs[:, quad(t)]), m.ks[:, quad(t)]) + bias[t]
            s = jnp.where(allowed, s, NEG)
            e = jnp.exp(s - jnp.max(s, axis=1, keepdims=True))
            pr = e / jnp.sum(e, axis=1, keepdims=True)
            m.ps[t] = pr
            m.os[:, quad(t)] = fold4(nn(pr.astype(BF), m.vs[:, quad(t)])).astype(BF)

    qc = m.qc
    qc_base = take(YZ)

    def self_out():
        x1 = tok[...] + nn(m.os[...], w[SO])
        m.x1[...] = x1
        m.h2[...] = normed(x1, gain[1:2, :]).astype(BF)

    def cross_query():
        qc[z, y] = nn(m.h2[...], w[CQ]).astype(BF)
        act_start(qc_base, [qc])
        act_forward(qc_base, [qc], 0)

    kv, pas = m.kv, m.pas

    chunk = 2 if R % 16 == 0 else 1

    tall = 4 if R % 16 == 0 else 1

    def project(p, off, k0, k1):
        def part(k, carry):
            rows = pl.ds(k // NQ * tall, tall)
            at = k % NQ * WIDE
            cols = pl.ds(pl.multiple_of(at, WIDE), WIDE)
            v = nn(pas[rows].reshape(tall * R, D), w[p, :, cols])
            cols = pl.ds(pl.multiple_of(off + at, WIDE), WIDE)
            kv[rows, :, cols] = v.astype(BF).reshape(tall, R, WIDE)
            return carry

        lax.fori_loop(k0 * NQ, k1 * NQ, part, 0)

    def project_one(q, p, off):
        kv[q, :, off : off + D] = nn(pas[q], w[p]).astype(BF)

    held = Buffers()

    def after(p):
        unpack(p)
        if p == SQ:
            moves["small"].end()
            read_small()
        elif p == SV:
            self_forward()
        elif p == SO:
            self_out()
        elif p == CQ:
            cross_query()
        elif p == CK:
            load_pas.wait()
            project(CK, 0, 0, YZ // tall // 2)

    order = (SQ, SK, SV, SO, CQ, CK, CV, CO, FI, FO)

    def line_out(k):
        if k == 0:
            moves["small"].line_out()
        moves[order[k]].line_out()

    def pair_out(k):
        if k == 0:
            moves["small"].pair_out()
        moves[order[k]].pair_out()
        if k + 3 < 8:
            moves[order[k + 3]].z_out()

    def plane_out(k):
        if k == 0:
            moves["small"].plane_out()
        moves[order[k]].plane_out()

    def core_out(k):
        if k == 0:
            moves["small"].core_out()
        moves[order[k]].core_out()

    def arrive(k):
        moves[order[k]].end()
        after(order[k])

    def query_out(a):
        act_wait(qc_base, [qc], a)
        act_forward(qc_base, [qc], a)

    pair_out(0)
    pair_out(1)
    line_out(0)
    pack_ff()
    pair_out(2)
    line_out(1)
    plane_out(0)
    pair_out(3)
    line_out(2)
    plane_out(1)
    core_out(0)
    pair_out(4)
    line_out(3)
    begin(FI, "exchange")
    plane_out(2)
    arrive(0)
    core_out(1)
    pair_out(5)
    line_out(4)
    plane_out(3)
    arrive(1)
    core_out(2)
    pair_out(6)
    line_out(5)
    line_start(g3_base, g3)
    plane_out(4)
    arrive(2)
    core_out(3)
    line_out(6)
    plane_out(5)
    pair_out(7)
    arrive(3)
    core_out(4)
    arrive(4)
    plane_out(6)
    core_out(5)
    line_out(7)
    begin(FO, "local")
    moves[FI].own_out()
    moves[FO].own_out()
    line_out(8)
    line_out(9)
    arrive(5)
    core_out(6)
    query_out(1)
    project(CK, 0, YZ // tall // 2, YZ // tall)
    arrive(6)
    query_out(2)
    plane_out(7)
    query_out(3)

    po, pst, ryo, ryst, rzo, rzst = m.po, m.pst, m.ryo, m.ryst, m.rzo, m.rzst

    def rs_y_base():
        return take((Y - 1) * Z)

    def rs_y_send(base, src, dst, b, a):
        zi = zs(a)
        copy_at(base + (b - 1) * Z + a, src.at[b, zi], dst.at[b - 1, zi], dev(y_=ys(b))).start()

    def rs_y_wait(base, src, dst, b, a):
        copy_at(base + (b - 1) * Z + a, src.at[b, 0], dst.at[b - 1, 0], dev(y_=ys(1))).wait_recv()

    def rs_y_done(base, src, dst):
        for b in range(1, Y):
            for a in range(Z):
                copy_at(
                    base + (b - 1) * Z + a, src.at[b, 0], dst.at[b - 1, 0], dev(y_=ys(1))
                ).wait_send()

    yo_base, yst_base = rs_y_base(), rs_y_base()
    zo_base, zst_base = take(Z), take(Z)

    def attend(a, b):
        zi = zs(a)
        yi = ys(b)
        qi = zi * Y + yi
        st = jnp.zeros((T, 128), F32)
        for k in range(NQ):
            qb = stack4(qc[zi, yi, :, quad(k)])
            s = nt(qb, kv[qi, :, quad(k)])
            top = jnp.max(s, axis=1, keepdims=True)
            e = jnp.exp(s - top)
            tot = jnp.sum(e, axis=1, keepdims=True)
            u = nn(e.astype(BF), kv[qi, :, D + k * WIDE : D + (k + 1) * WIDE])
            po[b, zi, :, quad(k)] = fold4(u * (1.0 / tot)).astype(BF)
            lse = top + jnp.log(tot)
            for h in range(QUAD):
                st = jnp.where(tlane == k * QUAD + h, lse[h * T : (h + 1) * T], st)
        pst[b, zi] = st.T[0:16]

    def expand(st):
        return lax.dot_general(
            st, spread[...], (((0,), (0,)), ((), ())), preferred_element_type=F32, precision=HIGH
        )

    def expand_low(v):
        hi = v.astype(BF)
        lo = (v - hi.astype(F32)).astype(BF)
        both = jnp.concatenate([hi, lo], axis=0)
        ones = m.spread2[...]
        return tn(both, ones)

    def merge(parts):
        top = parts[0][1]
        for _, st in parts[1:]:
            top = jnp.maximum(top, st)
        ws = [jnp.exp(st - top) for _, st in parts]
        tot = ws[0]
        for v in ws[1:]:
            tot = tot + v
        out = jnp.zeros((T, D), F32)
        for (o, _), v in zip(parts, ws):
            out = out + expand_low(v / tot) * o.astype(F32)
        return out, top + jnp.log(tot)

    def z_send(base, src, dst, a):
        zi = zs(a)
        copy_at(base + a, src.at[0, zi], dst.at[a - 1], dev(z_=zi)).start()

    def z_each(base, src, dst, wait):
        for a in range(1, Z):
            cp = copy_at(base + a, src.at[0, 0], dst.at[a - 1], dev(z_=zs(a)))
            if wait == "recv":
                cp.wait_recv()
            else:
                cp.wait_send()

    def pass_on(a):
        zi = zs(a)
        for b in range(1, Y):
            rs_y_wait(yo_base, po, ryo, b, a)
            rs_y_wait(yst_base, pst, ryst, b, a)
        o, st = merge(
            [(po[0, zi], pst[0, zi])] + [(ryo[b - 1, zi], ryst[b - 1, zi]) for b in range(1, Y)]
        )
        po[0, zi] = o.astype(BF)
        pst[0, zi] = st
        z_send(zo_base, po, rzo, a)
        z_send(zst_base, pst, rzst, a)

    def attend_own(a):
        project_one(zs(a) * Y + y, CV, D)
        attend(a, 0)

    def attend_others(a):
        def body(b, carry):
            project_one(zs(a) * Y + ys(b), CV, D)
            act_wait(qc_base, [qc], b * Z + a)
            attend(a, b)
            rs_y_send(yo_base, po, ryo, b, a)
            rs_y_send(yst_base, pst, ryst, b, a)
            return carry

        lax.fori_loop(1, Y, body, 0)

    def attend_step(k, carry):
        attend_others((k + 1) % Z)
        attend_own(k)
        pass_on(k)

        @pl.when(k == 2)
        def _():
            core_out(7)

        return carry

    attend_own(0)
    attend_others(1)
    plane_out(8)
    plane_out(9)
    lax.fori_loop(1, Z, attend_step, 0)
    arrive(7)
    for b in range(1, Y):
        rs_y_wait(yo_base, po, ryo, b, 0)
        rs_y_wait(yst_base, pst, ryst, b, 0)
    z_each(zo_base, po, rzo, "recv")
    z_each(zst_base, pst, rzst, "recv")
    o, lse = merge(
        [(po[0, z], pst[0, z])]
        + [(ryo[b - 1, z], ryst[b - 1, z]) for b in range(1, Y)]
        + [(rzo[a - 1], rzst[a - 1]) for a in range(1, Z)]
    )
    m.oc[...] = o.astype(BF)
    m.lse[...] = lse
    x2 = m.x1[...] + nn(m.oc[...], w[CO])
    m.x2[...] = x2
    h3 = m.h3
    h3[z] = normed(x2, gain[2:3, :]).astype(BF)
    h3_base = take(Z)
    line_start(h3_base, h3)

    rc, r1, r1y, r2, r2x, rz, act, cot = (getattr(m, k, None) for k in SPOTS[3:])

    def share(buf):
        own = buf.at[x, c]
        near_c = send(own, own, dev(c_=oth))
        return [send(own, own, dev(x_=xs(b))) for b in range(1, X)], near_c

    def share_on(buf, cps):
        far, near_c = cps
        got(far)
        out = [near_c]
        for b in range(1, X):
            block = buf.at[xs(b), c]
            out.append(send(block, block, dev(c_=oth)))
        return out

    def share_acts():
        if sz.inside:
            for n, name in enumerate(ACTS):
                act[n, x, c] = getattr(m, name)[...]
            held.acts = [share(act.at[n]) for n in range(len(ACTS))]

    def share_acts_on():
        if sz.inside:
            held.acts = [share_on(act.at[n], cps) for n, cps in enumerate(held.acts)]

    def share_acts_end():
        if sz.inside:
            for cps in held.acts:
                got(cps)
    drain()
    share_acts()

    core_out(8)
    core_out(9)
    arrive(8)
    line_wait(g3_base, g3)
    arrive(9)
    gb = g3[...].reshape(Z * T, D)
    m.kvacc.at[0 : Z * T, 0:hid][...] = nt(gb, w[FO])
    act_done(qc_base, [qc])
    rs_y_done(yo_base, po, ryo)
    rs_y_done(yst_base, pst, ryst)
    z_each(zo_base, po, rzo, "send")
    z_each(zst_base, pst, rzst, "send")
    py, rzy = Spot(m.py), Spot(m.rzy)
    gl, du = m.gl, m.du
    line_wait(h3_base, h3)
    lifted, slope = gelu_pair(nn(h3[...].reshape(Z * T, D), w[FI]))
    du[...] = (m.kvacc.at[0 : Z * T, 0:hid][...] * slope).astype(BF)
    gl[...] = lifted.astype(BF)
    po[0] = nt(du[...], w[FI]).astype(BF).reshape(Z, T, D)

    def rs_z(part, rzb):
        return [send(part.at[zs(a)], rzb.at[a - 1], dev(z_=zs(a))) for a in range(1, Z)]

    def rs_total(part, rzb):
        tot = part[z].astype(F32)
        for a in range(1, Z):
            tot = tot + rzb[a - 1].astype(F32)
        return tot

    zh = rs_z(po.at[0], rzo)
    py[...] = nn(gl[...], w[FO]).astype(BF).reshape(Z, T, D)
    line_done(h3_base, h3)
    line_done(g3_base, g3)

    acc = m.kvacc.at[:, 0:D]

    def add_to(dst, src):
        dst[...] = (dst[...].astype(F32) + src[...].astype(F32)).astype(BF)

    def add_blocks(rows, dst, src):
        def body(i, carry):
            add_to(dst(i // Z, i % Z), src(i // Z, i % Z))
            return carry

        lax.fori_loop(0, rows * Z, body, 0)

    def pack_grad(p, acc, col):
        group = YZ * r
        if not sz.inside:
            name, off = targets[p]
            out = getattr(m, name) if p in (FI, FO) else getattr(m, name).at[:, off : off + D]
            cp = pltpu.make_async_copy(acc.at[:, col : col + D], out, lsem.at[0])
            cp.start()
            cp.wait()
            return None

        def body(k, carry):
            x_ = k // 2
            c_ = k % 2
            for z_ in range(Z):
                for y_ in range(Y):
                    at = (y_ * Z + z_) * r if p == FO else (z_ * Y + y_) * r
                    rows = pl.ds(pl.multiple_of(k * group + at, 8), r)
                    left, right = acc[rows, col : col + nh], acc[rows, col + nh : col + D]
                    put_halves(gw.at[p, c_, x_, y_, z_], left, right, r, rb)
            return carry

        lax.fori_loop(0, 2 * X, body, 0)
        return [send(gw.at[p, oth], rc.at[WIDE_PIECES.index(p)], dev(c_=oth))]

    def rs_first(p, cps):
        got(cps)
        n = WIDE_PIECES.index(p)
        add_blocks(
            X * Y,
            lambda k, z_: gw.at[p, c, k // Y, k % Y, z_],
            lambda k, z_: rc.at[n, k // Y, k % Y, z_],
        )
        if p in Y_SUMMED_FIRST:
            return [
                send(gw.at[p, c, :, ys(b)], r1y.at[n, b - 1], dev(y_=ys(b))) for b in range(1, Y)
            ]
        return [send(gw.at[p, c, xs(b)], r1.at[n, b - 1], dev(x_=xs(b))) for b in range(1, X)]

    def to_y(p):
        return [send(gw.at[p, c, x, ys(b)], r2.at[p, b - 1], dev(y_=ys(b))) for b in range(1, Y)]

    def rs_second(p, cps):
        got(cps)
        n = WIDE_PIECES.index(p)
        if p in Y_SUMMED_FIRST:
            for b in range(1, Y):
                add_blocks(
                    X,
                    lambda k, z_: gw.at[p, c, k, y, z_],
                    lambda k, z_: r1y.at[n, b - 1, k, z_],
                )
            return [
                send(gw.at[p, c, xs(b), y], r2x.at[n, b - 1], dev(x_=xs(b))) for b in range(1, X)
            ]
        for b in range(1, X):
            add_blocks(
                Y,
                lambda k, z_: gw.at[p, c, x, k, z_],
                lambda k, z_: r1.at[n, b - 1, k, z_],
            )
        return to_y(p)

    def factor_on(p, cps):
        return share_on(cot.at[p], cps)

    def factor_product(p, cps):
        got(cps)
        group = YZ * r
        first = (x * 2 + c) * group
        lanes = first // 128 * 128
        shift = pl.multiple_of(first - lanes, 8)
        lhs = act[ACTS.index(FACTORS[p]), :, :, :, pl.ds(pl.multiple_of(lanes, 128), WIDE)]
        acc[0:WIDE, :] = tn(lhs.reshape(2 * X * T, WIDE), cot[p].reshape(2 * X * T, D))

        def body(i, carry):
            y_ = i % Y
            z_ = i // Y
            rows = pl.ds(pl.multiple_of(shift + i * r, 8), r)
            put_halves(gw.at[p, c, x, y_, z_], acc[rows, 0:nh], acc[rows, nh:D], r, rb)
            return carry

        lax.fori_loop(0, YZ, body, 0)
        return to_y(p)

    def rs_third(p, cps):
        got(cps)
        second = (
            [r2x.at[WIDE_PIECES.index(p), b - 1] for b in range(1, X)]
            if p in Y_SUMMED_FIRST
            else [r2.at[p, b - 1] for b in range(1, Y)]
        )
        for part in second:
            add_blocks(1, lambda k, z_: gw.at[p, c, x, y, z_], lambda k, z_: part.at[z_])
        if p == FO:
            return []
        if p == FI:
            return [
                send(gw.at[p, c, x, y, zs(a)], rz.at[p, a - 1], dev(z_=zs(a)))
                for a in range(1, Z)
            ]
        return [
            send(gw.at[p, c, x, y, k], rz.at[p, n], dev(z_=z_near))
            for n, k in enumerate((z_near, z_cross))
        ]

    def rs_fourth(p, cps):
        got(cps)
        if p in (FI, FO):
            return []
        add_to(gw.at[p, c, x, y, z_far], rz.at[p, 1])
        return [send(gw.at[p, c, x, y, z_far], rz.at[p, 2], dev(z_=z_far))]

    targets = {
        SQ: ("g_sq", 0), SK: ("g_skv", 0), SV: ("g_skv", D), SO: ("g_so", 0),
        CQ: ("g_cq", 0), CK: ("g_ckv", 0), CV: ("g_ckv", D), CO: ("g_co", 0),
        FI: ("g_fi", 0), FO: ("g_fo", 0),
    }

    def rs_last(p, cps):
        got(cps)
        name, off = targets[p]
        if p in (FI, FO):
            for a in range(Z):
                k = a if p == FO else zs((Z - a) % Z)
                if p == FO:
                    v = gw[p, c, x, y, a]
                else:
                    v = rz[p, a - 1] if a else gw[p, c, x, y, z]
                lo, hi = get_halves(v.astype(F32), r)
                if p == FI:
                    m.kvacc[pl.ds(pl.multiple_of(k * r, 8), r), 0:nh] = lo
                    m.kvacc[pl.ds(pl.multiple_of(k * r, 8), r), nh:D] = hi
                else:
                    getattr(m, name)[k * r : k * r + r, 0:nh] = lo
                    getattr(m, name)[k * r : k * r + r, nh:D] = hi
            if p == FI:
                for k in range(Z):
                    for i in range(ndp):
                        at = (i * Z + k) * per
                        getattr(m, name)[:, at : at + per] = m.kvacc[k * r : k * r + r, i * per : (i + 1) * per]
            return None
        v = gw[p, c, x, y, z].astype(F32) + rz[p, 0].astype(F32) + rz[p, 2].astype(F32)
        lo, hi = get_halves(v, r)
        getattr(m, name)[:, off : off + nh] = lo
        getattr(m, name)[:, off + nh : off + D] = hi

    wide_stages = (rs_first, rs_second, rs_third, rs_fourth, rs_last) if sz.inside else ()
    factor_stages = (factor_on, factor_product, rs_third, rs_fourth, rs_last) if sz.inside else ()

    def stages_of(p):
        return factor_stages if p in FACTORS else wide_stages

    moving = {}

    def grad_of(p, lhs, rhs):
        if sz.inside and p in FACTORS:
            cot[p, x, c] = rhs[...]
            moving[p] = (0, share(cot.at[p]))
            return

        def part(k, carry):
            cols = pl.ds(pl.multiple_of(k * WIDE, WIDE), WIDE)
            left = lhs[:, :, cols].reshape(Z * T, WIDE) if len(lhs.shape) == 3 else lhs[:, cols]
            acc[cols, :] = tn(left, rhs[...])
            return carry

        lax.fori_loop(0, NQ, part, 0)
        grad_out(p)

    def grad_out(p, src=None, col=0):
        moving[p] = (0, pack_grad(p, acc if src is None else src, col))

    def push(p):
        k, cps = moving[p]
        if k < len(stages_of(p)):
            moving[p] = (k + 1, stages_of(p)[k](p, cps))

    def push_all(ps):
        for p in ps:
            push(p)

    sent(moves[FI].last + moves[FO].last)
    spare.extend(early[1])
    grad_of(FO, gl, gb)
    grad_of(FI, h3, du)
    push_all([FO, FI])
    share_acts_on()
    sm = m.sm
    sm[...] = jnp.zeros_like(sm)
    got(zh)
    dh3 = rs_total(po.at[0], rzo)
    dv, gg = norm_back(m.x2[...], gain[2:3, :], dh3)
    sm[2:3, :] = gg
    dx2 = live * m.og[...] + dv
    m.dx[...] = dx2
    dx2l = dx2.astype(BF)
    doc = nt(dx2l, w[CO]).astype(BF)
    do, dr = m.do, m.dr
    do[z, y] = doc
    pick = iota((T, D), 0) == (iota((T, D), 1) & (T - 1))

    def as_rows(st):
        v = jnp.sum(jnp.where(pick, expand(st), 0.0), axis=0, keepdims=True)
        parts = [v[:, k * 128 : (k + 1) * 128] for k in range(D // 128)]
        return jnp.concatenate(parts + [jnp.zeros((8 - D // 128, 128), F32)], axis=0)

    prod = doc.astype(F32) * m.oc[...].astype(F32)
    delta = lax.dot_general(
        spread[...], prod, (((1,), (1,)), ((), ())), preferred_element_type=F32, precision=HIGH
    )
    dr[z, y, 0:8] = as_rows(m.lse[...])
    dr[z, y, 8:16] = as_rows(delta)
    do_base = take(2 * YZ)
    act_start(do_base, [do, dr])
    act_forward(do_base, [do, dr], 0)
    grad_of(CO, m.oc, dx2l)

    sent(zh)
    yq_base = rs_y_base()

    def row_of(ref, k):
        return jnp.concatenate([ref[2 * k : 2 * k + 1, :], ref[2 * k + 1 : 2 * k + 2, :]], axis=1)

    zq_base = take(Z)

    def pass_back(a):
        zi = zs(a)
        for b in range(1, Y):
            rs_y_wait(yq_base, po, ryo, b, a)
        tot = po[0, zi].astype(F32)
        for b in range(1, Y):
            tot = tot + ryo[b - 1, zi].astype(F32)
        po[0, zi] = tot.astype(BF)
        z_send(zq_base, po, rzo, a)

    def attend_back(a, b):
        zi = zs(a)
        yi = ys(b)
        qi = zi * Y + yi

        lse_rows = dr[zi, yi, 0:8]
        delta_rows = dr[zi, yi, 8:16]
        for k in range(NQ):
            qb = stack4(qc[zi, yi, :, quad(k)])
            db = stack4(do[zi, yi, :, quad(k)])
            kt = kv[qi, :, quad(k)]
            vt = kv[qi, :, D + k * WIDE : D + (k + 1) * WIDE]
            pt = jnp.exp(nt(kt, qb) - row_of(lse_rows, k))
            ds = (pt * (nt(vt, db) - row_of(delta_rows, k))).astype(BF)
            po[b, zi, :, quad(k)] = fold4(tn(ds, kt)).astype(BF)
            kv[qi, :, quad(k)] = nn(ds, qb).astype(BF)
            kv[qi, :, D + k * WIDE : D + (k + 1) * WIDE] = nn(pt.astype(BF), db).astype(BF)


    kvacc = m.kvacc

    def kv_grad(q):
        def part(k, carry):
            cols = pl.ds(pl.multiple_of(k * WIDE, WIDE), WIDE)
            kvacc[cols, :] += tn(pas[q, :, cols], kv[q])
            return carry

        lax.fori_loop(0, NQ, part, 0)

    def back_own(a):
        attend_back(a, 0)
        kv_grad(zs(a) * Y + y)

    def back_others(a):
        def body(b, carry):
            act_wait(do_base, [do, dr], b * Z + a)
            attend_back(a, b)
            rs_y_send(yq_base, po, ryo, b, a)
            kv_grad(zs(a) * Y + ys(b))
            return carry

        lax.fori_loop(1, Y, body, 0)

    def back_step(k, carry):
        act_wait(do_base, [do, dr], k + 1)
        act_forward(do_base, [do, dr], k + 1)
        back_others(k)

        @pl.when(k == 1)
        def _():
            push(CO)
            share_acts_end()
            held.zy = rs_z(py, rzy)

        @pl.when(k == Z - 2)
        def _():
            push(FI)

        back_own(k + 1)
        return carry

    kvacc[...] = jnp.zeros_like(kvacc)
    back_own(0)
    push(FO)
    lax.fori_loop(0, Z - 1, back_step, 0)
    back_others(Z - 1)
    def row_grads(k0, k1):
        def whole(k, carry):
            pas[k] = (nt(kv[k, :, 0:D], w[CK]) + nt(kv[k, :, D : 2 * D], w[CV])).astype(BF)
            pltpu.make_async_copy(pas.at[k], m.pg.at[k], lsem.at[1 + k]).start()
            return carry

        def part(k, carry):
            rows = pl.ds(k // NQ * chunk, chunk)
            cols = pl.ds(pl.multiple_of(k % NQ * WIDE, WIDE), WIDE)
            v = nt(kv[rows, :, 0:D].reshape(chunk * R, D), w[CK, cols, :])
            v = v + nt(kv[rows, :, D : 2 * D].reshape(chunk * R, D), w[CV, cols, :])
            pas[rows, :, cols] = v.astype(BF).reshape(chunk, R, WIDE)

            @pl.when(k % NQ == NQ - 1)
            def _():
                for q in range(chunk):
                    at = k // NQ * chunk + q
                    pltpu.make_async_copy(pas.at[at], m.pg.at[at], lsem.at[1 + at]).start()

            return carry

        if chunk == 1:
            lax.fori_loop(k0, k1, whole, 0)
        else:
            lax.fori_loop(k0 * NQ, k1 * NQ, part, 0)

    part = YZ // chunk // 4

    def take_dq():
        for b in range(1, Y):
            rs_y_wait(yq_base, po, ryo, b, 0)
        z_each(zq_base, po, rzo, "recv")
        dqc = rs_total(po.at[0], rzo)
        for b in range(1, Y):
            dqc = dqc + ryo[b - 1, z].astype(F32)
        held.dqc = dqc.astype(BF)
        dh2 = nt(held.dqc, w[CQ])
        dv, gg = norm_back(m.x1[...], gain[1:2, :], dh2)
        sm[1:2, :] = gg
        dx1 = m.dx[...] + dv
        m.dx[...] = dx1
        held.dx1l = dx1.astype(BF)

    def self_back():
        m.oc[...] = nt(held.dx1l, w[SO]).astype(BF)
        grads = [[], [], []]
        held.tail = []
        back = (iota((T, 128), 1) == T - 1 - iota((T, 128), 0)).astype(F32).astype(BF)
        for t in range(NQ):
            db = stack4(m.oc[:, quad(t)])
            qb = stack4(m.qs[:, quad(t)])
            pr = m.ps[t]
            dps = nt(db, m.vs[:, quad(t)])
            dss = (pr * (dps - jnp.sum(pr * dps, axis=1, keepdims=True))).astype(BF)
            grads[0].append(fold4(nn(dss, m.ks[:, quad(t)])).astype(BF))
            grads[1].append(tn(dss, qb).astype(BF))
            grads[2].append(tn(pr.astype(BF), db).astype(BF))
            turned = nn(dss, back)
            for h in range(QUAD):
                part = pltpu.roll(turned[h * T : (h + 1) * T], 0, 1, stride=1, stride_axis=0)
                held.tail.append(jnp.sum(part, axis=0, keepdims=True))
        held.dqs, held.dks, held.dvs = (jnp.concatenate(g, axis=1) for g in grads)

    def token_grad():
        dh1 = nt(held.dqs, w[SQ]) + nt(held.dks, w[SK]) + nt(held.dvs, w[SV])
        dv, gg = norm_back(tok[...], gain[0:1, :], dh1)
        sm[0:1, :] = gg
        m.tg[...] = m.dx[...] + dv
        flat = HEADS * BUCKETS
        diag = jnp.concatenate(held.tail + [jnp.zeros((16 - HEADS, 128), F32)], axis=0)
        mi, bi = iota((128, 128), 0), iota((128, 128), 1)
        hot = ((mi >= T - 1) & (bucket_of(mi - (T - 1)) == bi) & (bi < BUCKETS)).astype(F32)
        table = nn_high(diag, hot)
        bb, nb = iota((128, flat), 0), iota((128, flat), 1)
        wide = nn_high(table, ((nb & (BUCKETS - 1)) == bb).astype(F32))
        h0, n0 = iota((16, flat), 0), iota((16, flat), 1)
        own = (n0 >= h0 * BUCKETS) & (n0 < h0 * BUCKETS + BUCKETS)
        sm[3:4, 0:flat] = jnp.sum(jnp.where(own, wide, 0.0), axis=0, keepdims=True)

    rsm = m.rsm
    slot = [0]

    def small_to(devs):
        held.small = []
        for to in devs:
            held.small.append((slot[0], send(sm, rsm.at[slot[0]], to)))
            slot[0] += 1

    def small_got():
        got([cp for _, cp in held.small])
        sent([cp for _, cp in held.small])
        for k, _ in held.small:
            sm[...] += rsm[k]

    def small_step(k):
        if k:
            small_got()
        if k < 4:
            small_to(
                (
                    [dev(c_=oth)],
                    [dev(x_=xs(b)) for b in range(1, X)],
                    [dev(y_=ys(b)) for b in range(1, Y)],
                    [dev(z_=zs(a)) for a in range(1, Z)],
                )[k]
            )

    def block_out():
        got(held.zy)
        m.bo[...] = live * (m.x2[...] + rs_total(py, rzy))

    steps = {
        DO_CK: lambda: grad_out(CK, kvacc, 0),
        DO_CV: lambda: grad_out(CV, kvacc, D),
        DO_PASS: lambda: [pass_back(a) for a in range(1, Z)],
        DO_ROWS1: lambda: row_grads(0, part),
        DO_ROWS2: lambda: row_grads(part, 2 * part),
        DO_ROWS3: lambda: row_grads(2 * part, 3 * part),
        DO_ROWS4: lambda: row_grads(3 * part, YZ // chunk),
        DO_DQ: take_dq,
        DO_CQ: lambda: grad_of(CQ, m.h2, held.dqc),
        DO_SO: lambda: grad_of(SO, m.os, held.dx1l),
        DO_SELFBACK: self_back,
        DO_SV: lambda: grad_of(SV, m.h1, held.dvs),
        DO_SQ: lambda: grad_of(SQ, m.h1, held.dqs),
        DO_SK: lambda: grad_of(SK, m.h1, held.dks),
        DO_DH1: token_grad,
        DO_BO: block_out,
    }
    small_at = [0]

    def run(name):
        if name == DO_SMALL:
            small_step(small_at[0])
            small_at[0] += 1
        elif name < PIECES:
            push(name)
        else:
            steps[name]()

    for name in TAIL:
        run(name)
    assert all(k == len(stages_of(p)) for p, (k, _) in moving.items()), moving
    assert small_at[0] == 5
    me = dp * YZ + fs
    nd, ld = iota((D, 128), 0), iota((D, 128), 1)
    mine = nn_high(sm[...], ((nd == me * r + ld) & (ld < r)).astype(F32))
    mine_b = nn_high(sm[...], ((nd == me * rbs + ld) & (ld < rbs)).astype(F32))
    m.g_ls[...] = mine[0:1, 0:r]
    m.g_lc[...] = mine[1:2, 0:r]
    m.g_lf[...] = mine[2:3, 0:r]
    m.g_rb[...] = mine_b[3:4, 0:rbs]

    act_done(do_base, [do, dr])
    rs_y_done(yq_base, po, ryo)
    z_each(zq_base, po, rzo, "send")
    drain()

    def pg_wait(q, carry):
        pltpu.make_async_copy(pas.at[q], m.pg.at[q], lsem.at[1 + q]).wait()
        return carry

    lax.fori_loop(0, YZ, pg_wait, 0)


def place_kernel(*refs):
    n = len(OUTPUTS)
    given, put, held, sem = refs[:n], refs[n : 2 * n], refs[2 * n : 3 * n], refs[3 * n]
    loads, stores = [], []
    for k in range(n):
        parts = [slice(None)] if len(given[k].shape) < 3 else range(given[k].shape[0])
        for part in parts:
            at = len(loads)
            loads.append(pltpu.make_async_copy(given[k].at[part], held[k].at[part], sem.at[0, at]))
            stores.append(pltpu.make_async_copy(held[k].at[part], put[k].at[part], sem.at[1, at]))
    for cp in loads:
        cp.start()
    for load, store in zip(loads, stores):
        load.wait()
        store.start()
    for cp in stores:
        cp.wait()


def per_device(
    sz,
    targets, passages, tgt_len, out_grad, ln_self, rel_bias, self_q, self_kv, self_out,
    ln_cross, cross_q, cross_kv, cross_out, ln_ff, ff_in, ff_out,
):
    T, D, r, Z = sz.T, sz.D, sz.r, sz.Z
    ndp = 2 * sz.X
    per = sz.Y * sz.rff
    scratch = layout(sz)
    names = tuple(scratch)
    gr = r if sz.inside else D
    vm = pl.BlockSpec(memory_space=pltpu.VMEM)
    hbm = pl.BlockSpec(memory_space=pltpu.HBM)
    shape = jax.ShapeDtypeStruct
    rbs = rel_bias.shape[0]
    out_shape = (
        shape((T, D), F32), shape((T, D), F32), shape(passages.shape, BF),
        shape((1, r), F32), shape((1, rbs), F32),
        shape((gr, D), F32), shape((gr, 2 * D), F32), shape((gr, D), F32),
        shape((1, r), F32), shape((gr, D), F32), shape((gr, 2 * D), F32), shape((gr, D), F32),
        shape((1, r), F32),
        shape((r, Z * D) if sz.inside else (D, D), F32),
        shape((Z * r, D) if sz.inside else (D, D), F32),
    )
    weight_outs = ("g_sq", "g_skv", "g_so", "g_cq", "g_ckv", "g_co", "g_fi", "g_fo")
    apart = ("pg",) if sz.inside else ("pg",) + weight_outs
    outs = pl.pallas_call(
        functools.partial(block_kernel, sz, names),
        out_shape=out_shape,
        in_specs=[hbm if n == "pas_in" else vm for n in INPUTS],
        out_specs=tuple(hbm if n in apart else vm for n in OUTPUTS),
        scratch_shapes=tuple(scratch.values()),
        compiler_params=pltpu.CompilerParams(
            collective_id=0, has_side_effects=True, vmem_limit_bytes=63 * 2**20
        ),
        cost_estimate=pl.CostEstimate(
            flops=20 * 10**9, bytes_accessed=2 * 10**7, transcendentals=4 * 10**6
        ),
    )(
        targets[0], passages, tgt_len[None], out_grad[0], ln_self[None], rel_bias[None],
        self_q, self_kv, self_out, ln_cross[None], cross_q, cross_kv, cross_out,
        ln_ff[None], ff_in, ff_out,
    )
    (bo, tg, pg, g_ls, g_rb, g_sq, g_skv, g_so, g_lc, g_cq, g_ckv, g_co, g_lf, g_fi, g_fo) = outs
    if not sz.inside:
        at = lax.axis_index("fsdp") // sz.Y
        rows = jnp.zeros((ndp, Z, per, D), F32).at[:, at].set(g_fo.reshape(ndp, per, D))
        cols = jnp.zeros((D, ndp, Z, per), F32).at[:, :, at].set(g_fi.reshape(D, ndp, per))
        g_sq, g_skv, g_so, g_cq, g_ckv, g_co, g_fi, g_fo = (
            lax.psum_scatter(g, ("dp", "fsdp"), scatter_dimension=0, tiled=True)
            for g in (
                g_sq, g_skv, g_so, g_cq, g_ckv, g_co,
                cols.reshape(D, Z * D), rows.reshape(Z * D, D),
            )
        )
    outs = (bo, tg, pg, g_ls, g_rb, g_sq, g_skv, g_so, g_lc, g_cq, g_ckv, g_co, g_lf, g_fi, g_fo)
    if sz.inside:
        outs = pl.pallas_call(
            place_kernel,
            out_shape=tuple(shape(o.shape, o.dtype) for o in outs),
            in_specs=[hbm] * len(outs),
            out_specs=(hbm,) * len(outs),
            scratch_shapes=tuple(pltpu.VMEM(o.shape, o.dtype) for o in outs)
            + (pltpu.SemaphoreType.DMA((2, len(outs) - 1 + passages.shape[0])),),
            compiler_params=pltpu.CompilerParams(vmem_limit_bytes=63 * 2**20),
        )(*outs)
    (bo, tg, pg, g_ls, g_rb, g_sq, g_skv, g_so, g_lc, g_cq, g_ckv, g_co, g_lf, g_fi, g_fo) = outs
    return (
        bo[None], tg[None], pg, g_ls[0], g_rb[0], g_sq, g_skv, g_so,
        g_lc[0], g_cq, g_ckv, g_co, g_lf[0], g_fi, g_fo,
    )


def solution(mesh):
    both = ("dp", "fsdp")
    rows3, rows2, rows1 = P(both, None, None), P(both, None), P(both)
    placed = (
        rows3, P("dp", "fsdp", None), rows1, rows3, rows1, rows1, rows2, rows2, rows2,
        rows1, rows2, rows2, rows2, rows1, rows2, rows2,
    )
    outs = (
        rows3, rows3, P("dp", "fsdp", None), rows1, rows1, rows2, rows2, rows2,
        rows1, rows2, rows2, rows2, rows1, rows2, rows2,
    )

    def run(*args):
        targets, passages, self_q, ff_out = args[0], args[1], args[6], args[15]
        sz = Sizes(
            mesh.shape,
            targets.shape[2], passages.shape[1], targets.shape[1],
            self_q.shape[0], ff_out.shape[0],
            ff_out.shape[0] * mesh.shape["dp"] * mesh.shape["fsdp"] // ZDIM,
        )
        return per_device(sz, *args)

    return jax.shard_map(run, mesh=mesh, in_specs=placed, out_specs=outs, check_vma=False)
```

```python
import functools
import math

import jax
import jax.numpy as jnp
from jax import lax
from jax.experimental import pallas as pl
from jax.experimental.pallas import tpu as pltpu
from jax.sharding import PartitionSpec as P

HEADS = 12
DK = 64
BUCKETS = 32
QUAD = 4
WIDE = QUAD * DK
EPS = 1e-06
NEG = -1e30
HIGH = lax.Precision.HIGHEST
BF = jnp.bfloat16
F32 = jnp.float32
PIECES = 10
SQ, SK, SV, SO, CQ, CK, CV, CO, FI, FO = range(PIECES)
WIDE_PIECES = (CK, CV, FI, FO)
Y_SUMMED_FIRST = (CK,)
Z_AT_ONCE = (FI, SQ, SK)
FACTORS = {SQ: "h1", SK: "h1", SV: "h1", SO: "os", CQ: "h2", CO: "oc"}
ACTS = ("h1", "os", "h2", "oc")
Y_GATHERED_LAST = (SQ, SV, CQ)
ZDIM = 4


def up16(n):
    return (n + 15) // 16 * 16


def bucket_limits():
    limits = []
    for target_bucket in range(1, 16):
        distance = 16
        while int(math.log(distance / 16.0) / math.log(8.0) * 16.0) < target_bucket:
            distance = distance + 1
        limits.append(distance)
    return limits


def bucket_of(distance):
    larger = jnp.full_like(distance, 16)
    for limit_value in bucket_limits():
        larger = larger + (distance >= limit_value).astype(jnp.int32)
    return jnp.where(distance < 16, distance, jnp.minimum(larger, 31))


def iota(shape, axis):
    return lax.broadcasted_iota(jnp.int32, shape, axis)


def nn(a, b):
    return lax.dot_general(a, b, (((1,), (0,)), ((), ())), preferred_element_type=F32)


def nt(a, b):
    return lax.dot_general(a, b, (((1,), (1,)), ((), ())), preferred_element_type=F32)


def tn(a, b):
    return lax.dot_general(a, b, (((0,), (0,)), ((), ())), preferred_element_type=F32)


def nn_high(a, b):
    return lax.dot_general(
        a, b, (((1,), (0,)), ((), ())), preferred_element_type=F32, precision=HIGH
    )


def normed(v, gain):
    return v * lax.rsqrt(jnp.mean(v * v, axis=-1, keepdims=True) + EPS) * gain


def norm_back(v, gain, dy):
    s = lax.rsqrt(jnp.mean(v * v, axis=-1, keepdims=True) + EPS)
    dyg = dy * gain
    gain_grad = jnp.sum(dy * v * s, axis=0, keepdims=True)
    dv = s * dyg - v * (s * s * s) * jnp.mean(dyg * v, axis=-1, keepdims=True)
    return dv, gain_grad


def gelu_pair(u):
    cst = 0.7978845608028654
    cubic = 0.044715
    th = jnp.tanh(cst * (u + cubic * u * u * u))
    half = 0.5 * (1.0 + th)
    slope = half + 0.5 * u * (1.0 - th * th) * cst * (1.0 + 3.0 * cubic * u * u)
    return u * half, slope


class Buffers:
    pass


class Spot:
    def __init__(self, base, steps=()):
        self.base, self.steps = base, steps

    @property
    def at(self):
        return Steps(self)

    def ref(self):
        out = self.base
        for step in self.steps:
            out = out.at[step]
        return out

    def __getitem__(self, key):
        return self.ref()[key]

    def __setitem__(self, key, value):
        self.ref()[key] = value


class Steps:
    def __init__(self, spot):
        self.spot = spot

    def __getitem__(self, key):
        return Spot(self.spot.base, self.spot.steps + (key,))


class Sent:
    def __init__(self, make):
        self.make = make

    def wait_recv(self):
        self.make().wait_recv()

    def wait_send(self):
        self.make().wait_send()


class Sizes:
    def __init__(self, mesh_shape, width, rows, targets, shard, ff_shard, hidden):
        self.Z = ZDIM
        self.X = mesh_shape["dp"] // 2
        self.Y = mesh_shape["fsdp"] // self.Z
        self.D = width
        self.R = rows
        self.T = targets
        self.r = shard
        self.rb = up16(2 * shard)
        self.nh = width // 2
        self.inside = shard % 8 == 0
        self.rff = ff_shard
        self.hid = hidden
        assert ff_shard == self.Z * shard and hidden == width


def sems(sz):
    return 156 if sz.inside else 900


def layout(sz):
    X, Y, Z, D, T, R = sz.X, sz.Y, sz.Z, sz.D, sz.T, sz.R
    rb, nh, hid = sz.rb, sz.nh, sz.hid
    nw = len(WIDE_PIECES)
    NQ = HEADS // QUAD
    V = pltpu.VMEM
    sums = dict(
        rc=V((nw, X, Y, Z, rb, nh), BF),
        r1=V((nw, X - 1, Y, Z, rb, nh), BF),
        r1y=V((nw, Y - 1, X, Z, rb, nh), BF),
        r2x=V((nw, X - 1, Z, rb, nh), BF),
        r2=V((PIECES, Y - 1, Z, rb, nh), BF),
        rz=V((PIECES, 3, rb, nh), BF),
        act=V((len(ACTS), X, 2, T, D), BF),
        cot=V((PIECES, X, 2, T, D), BF),
    )
    return dict(
        **(sums if sz.inside else {}),
        gw=V((PIECES, 2, X, Y, Z, rb, nh), BF),
        w=V((PIECES, D, D), BF),
        fip=V((Z, rb, nh), BF),
        kvacc=V((D, 2 * D), F32),
        lift=V((max(Y * Z * sz.r, sz.rff) if sz.r % 8 else 8, D), F32),
        even=V((sz.r, D), F32),
        cell=V((rb, nh), F32),
        smb=V((2, X, Y, Z, 16, 128), BF),
        hot_gain=V((128, D), BF),
        hot_bias=V((128, HEADS * BUCKETS), BF),
        gain=V((16, D), F32),
        bias=V((NQ, WIDE, T), F32),
        spread=V((16, D), F32),
        spread2=V((32, D), BF),
        mask=V((WIDE, WIDE), BF),
        pas=V((Y * Z, R, D), BF),
        kv=V((Y * Z, R, 2 * D), BF),
        h1=V((T, D), BF),
        qs=V((T, D), BF),
        ks=V((T, D), BF),
        vs=V((T, D), BF),
        os=V((T, D), BF),
        ps=V((NQ, WIDE, T), F32),
        x1=V((T, D), F32),
        h2=V((T, D), BF),
        x2=V((T, D), F32),
        oc=V((T, D), BF),
        dx=V((T, D), F32),
        lse=V((16, T), F32),
        qc=V((Z, Y, T, D), BF),
        h3=V((Z, T, D), BF),
        g3=V((Z, T, D), BF),
        do=V((Z, Y, T, D), BF),
        dr=V((Z, Y, 16, 128), F32),
        po=V((Y, Z, T, D), BF),
        pst=V((Y, Z, 16, T), F32),
        ryo=V((Y - 1, Z, T, D), BF),
        ryst=V((Y - 1, Z, 16, T), F32),
        rzo=V((Z - 1, T, D), BF),
        rzst=V((Z - 1, 16, T), F32),
        py=V((Z, T, D), BF),
        rzy=V((Z - 1, T, D), BF),
        gl=V((Z * T, hid), BF),
        du=V((Z * T, hid), BF),
        sm=V((8, D), F32),
        rsm=V((1 + (X - 1) + (Y - 1) + (Z - 1), 8, D), F32),
        ssem=pltpu.SemaphoreType.DMA((sems(sz),)),
        rsem=pltpu.SemaphoreType.DMA((sems(sz),)),
        lsem=pltpu.SemaphoreType.DMA((1 + Y * Z,)),
    )


(
    DO_KVG1, DO_CK, DO_CV, DO_PASS, DO_ROWS1, DO_ROWS2,
    DO_ROWS3, DO_ROWS4, DO_DQ, DO_CQ, DO_SO, DO_SELFBACK,
    DO_SV, DO_SQ, DO_SK, DO_DH1, DO_BO, DO_SMALL,
) = range(PIECES, PIECES + 18)
TAIL = (
    FO, DO_KVG1, FO, DO_CK, DO_CV, FO, DO_PASS, CO,
    CK, CV, FI, DO_ROWS1, DO_DQ, DO_CQ, DO_SO, CO,
    DO_SELFBACK, DO_SV, DO_SQ, DO_SK, DO_DH1, DO_SMALL, FI, DO_BO,
    CV, CO, FI, CK, DO_SMALL, CQ, DO_ROWS2, CO,
    SO, CQ, CV, SV, SO, DO_ROWS3, SQ, SV,
    CV, SK, CQ, SQ, SK, CK, CV, SO,
    DO_SMALL, DO_ROWS4, CQ, SV, CK, SO, SQ, CQ,
    SV, SK, CK, DO_SMALL, SO, SQ, SV, SK,
    DO_SMALL, SQ, SK,
)

SPOTS = ("gw", "smb", "fip", "rc", "r1", "r1y", "r2", "r2x", "rz", "act", "cot")
INPUTS = (
    "tok", "pas_in", "len", "og", "ls", "rel", "sq", "skv", "so",
    "lc", "cq", "ckv", "co", "lf", "fi_in", "fo_in",
)
OUTPUTS = (
    "bo", "tg", "pg", "g_ls", "g_rb", "g_sq", "g_skv", "g_so",
    "g_lc", "g_cq", "g_ckv", "g_co", "g_lf", "g_fi", "g_fo",
)


def block_kernel(sz, names, *refs):
    m = Buffers()
    vars(m).update(zip(INPUTS + OUTPUTS + names, refs))
    for name in SPOTS:
        if hasattr(m, name):
            setattr(m, name, Spot(getattr(m, name)))
    X, Y, Z, D, T, R = sz.X, sz.Y, sz.Z, sz.D, sz.T, sz.R
    r, rb, nh, hid = sz.r, sz.rb, sz.nh, sz.hid
    NQ = HEADS // QUAD
    YZ = Y * Z
    dp = lax.axis_index("dp")
    fs = lax.axis_index("fsdp")
    x, c = dp // 2, dp % 2
    z, y = fs // Y, fs % Y
    oth = 1 - c

    ring_x = [(x + b) % X for b in range(X)]
    ring_y = [(y + b) % Y for b in range(Y)]
    ring_z = [(z + b) % Z for b in range(Z)]

    def around(ring, at, b):
        return ring[b] if isinstance(b, int) else (at + b) % len(ring)

    def xs(b):
        return around(ring_x, x, b)

    def ys(b):
        return around(ring_y, y, b)

    def zs(b):
        return around(ring_z, z, b)

    def any_dev(x_=None, c_=None, y_=None, z_=None):
        x_ = x if x_ is None else x_
        c_ = c if c_ is None else c_
        y_ = y if y_ is None else y_
        z_ = z if z_ is None else z_
        return (x_ * 2 + c_, z_ * Y + y_)

    near = {}

    def dev(x_=None, c_=None, y_=None, z_=None):
        key = (id(x_), id(c_), id(y_), id(z_))
        if key not in near:
            return any_dev(x_, c_, y_, z_)
        return near[key]

    none = id(None)
    near[(none, id(oth), none, none)] = any_dev(c_=oth)
    for v in ring_x:
        near[(id(v), none, none, none)] = any_dev(x_=v)
    for v in ring_y:
        near[(none, none, id(v), none)] = any_dev(y_=v)
    for v in ring_z:
        near[(none, none, none, id(v))] = any_dev(z_=v)

    z_near = z + 1 - 2 * (z % 2)
    z_far = ring_z[2]
    z_cross = (z_near + 2) % Z
    near[(none, none, none, id(z_near))] = any_dev(z_=z_near)

    ssem, rsem, lsem = m.ssem, m.rsem, m.lsem
    n_sems = sems(sz)
    used = [0]
    pending = []

    spare = []
    early = [False, []]

    def take(n=1):
        if n == 1 and spare:
            return spare.pop(0)
        if n == 0:
            return 0
        at = used[0]
        used[0] += n
        assert used[0] <= n_sems
        return at

    def copy_at(i, src, dst, to):
        src = src.ref() if isinstance(src, Spot) else src
        dst = dst.ref() if isinstance(dst, Spot) else dst
        return pltpu.make_async_remote_copy(
            src_ref=src, dst_ref=dst, send_sem=ssem.at[i], recv_sem=rsem.at[i],
            device_id=to, device_id_type=pl.DeviceIdType.MESH,
        )

    def send(src, dst, to):
        i = take()
        cp = Sent(lambda: copy_at(i, src, dst, to))
        cp.make().start()
        pending.append(cp)
        return cp

    def got(cps):
        for cp in cps:
            cp.wait_recv()

    def sent(cps):
        for cp in cps:
            cp.wait_send()
        pending[:] = [cp for cp in pending if all(cp is not done for done in cps)]

    def drain():
        sent(list(pending))

    partners = [dev(c_=oth)]
    partners += [dev(x_=xs(b)) for b in range(1, X)]
    partners += [dev(y_=ys(b)) for b in range(1, Y)]
    partners += [dev(z_=zs(b)) for b in range(1, Z)]
    bar = pltpu.get_barrier_semaphore()
    for p in partners:
        pl.semaphore_signal(bar, inc=1, device_id=p, device_id_type=pl.DeviceIdType.MESH)
    load_pas = pltpu.make_async_copy(m.pas_in, m.pas, lsem.at[0])
    load_pas.start()
    pl.semaphore_wait(bar, len(partners))

    mask = m.mask
    mask[...] = (iota((WIDE, WIDE), 0) // DK == iota((WIDE, WIDE), 1) // DK).astype(F32).astype(BF)

    def stack4(v):
        return jnp.concatenate([v, v, v, v], axis=0) * mask[...]

    def fold4(u):
        lane = iota((T, WIDE), 1)
        out = u[0:T]
        for h in range(1, QUAD):
            out = jnp.where(lane >= h * DK, u[h * T : (h + 1) * T], out)
        return out

    def quad(t):
        return slice(t * WIDE, (t + 1) * WIDE)

    cell, lift = m.cell, m.lift

    def put_halves(dst, left, right, rows, total):
        if rows % 8 == 0 and 2 * rows == total:
            dst[...] = jnp.concatenate([left, right], axis=0).astype(BF)
        else:
            cols = left.shape[1]
            cell[0:total, 0:cols] = jnp.zeros((total, cols), F32)
            cell[0:rows, 0:cols] = left
            cell[rows : 2 * rows, 0:cols] = right
            dst[...] = cell[0:total, 0:cols].astype(BF)

    def get_halves(v, rows):
        if rows % 8 == 0:
            return v[0:rows], v[rows : 2 * rows]
        cell[0 : v.shape[0], 0 : v.shape[1]] = v
        return cell[0:rows, 0 : v.shape[1]], cell[rows : 2 * rows, 0 : v.shape[1]]

    gw, w, smb = m.gw, m.w, m.smb

    class Gather:

        def __init__(self, buf, y_first, feed="gather", first=False):
            self.buf, self.y_first, self.feed = buf, y_first, feed
            self.iz, self.iy, self.ix, self.ic = take(), take(Y - 1), take(X - 1), take()
            self.far = take() if feed == "gather" else 0
            if first:
                early[1].extend([self.iz, self.ic, self.far])
                early[1].extend(range(self.iy, self.iy + Y - 1))
                early[1].extend(range(self.ix, self.ix + X - 1))
            if feed == "exchange":
                own = buf.at[c, x, y, z]
                for a in range(1, Z):
                    copy_at(self.iz, m.fip.at[zs(a)], own, dev(z_=zs(a))).start()
                some = buf.at[c, x, y, 0 : Z - 1]
                pending.append(Sent(lambda: copy_at(self.iz, some, some, dev(z_=z_near))))

        def z_out(self):
            own = self.buf.at[c, x, y, z]
            copy_at(self.far, own, own, dev(z_=z_far)).start()
            copy_at(self.iz, own, own, dev(z_=z_near)).start()

        def pair_out(self):
            block = self.buf.at[c, x, y, z_far]
            far = Sent(lambda: copy_at(self.far, block, block, dev(z_=z_far)))
            far.wait_recv()
            copy_at(self.iz, block, block, dev(z_=z_near)).start()
            pair = self.buf.at[c, x, y, 0:2]
            pending.extend([far, Sent(lambda: copy_at(self.iz, pair, pair, dev(z_=z_near)))])
            self.over(self.y_first, block)
            self.over(not self.y_first, block)

        def over(self, is_y, block):
            if is_y:
                for b in range(1, Y):
                    copy_at(self.iy + b - 1, block, block, dev(y_=ys(b))).start()
            else:
                for b in range(1, X):
                    copy_at(self.ix + b - 1, block, block, dev(x_=xs(b))).start()

        def own_out(self):
            at = (c, x, y) if self.feed == "local" else (c, x, y, z)
            self.over(self.y_first, self.buf.at[at])
            self.over(not self.y_first, self.buf.at[at])

        def line_out(self):
            if self.feed == "local":
                return
            if self.feed == "gather":
                some = self.buf.at[c, x, y, 0:2]
                blocks = (z_near, z_cross)
            else:
                some = self.buf.at[c, x, y, 0 : Z - 1]
                blocks = ring_z[1:]
            copy_at(self.iz, some, some, dev(z_=z_near)).wait_recv()
            for k in blocks:
                block = self.buf.at[c, x, y, k]
                self.over(self.y_first, block)
                self.over(not self.y_first, block)

        def arrived(self, is_y, all_of_it):
            buf = self.buf
            if is_y:
                ref = buf.at[c, 0 : X, y] if all_of_it else buf.at[c, x, y]
                for b in range(1, Y):
                    yield Sent(
                        lambda b=b: copy_at(self.iy + b - 1, ref, ref, dev(y_=ys(b)))
                    )
            else:
                ref = buf.at[c, x] if all_of_it else buf.at[c, x, y]
                for b in range(1, X):
                    yield Sent(
                        lambda b=b: copy_at(self.ix + b - 1, ref, ref, dev(x_=xs(b)))
                    )

        def plane_out(self):
            second = list(self.arrived(self.y_first, False))
            got(second)
            pending.extend(second)
            if self.y_first:
                for b in range(1, Y):
                    self.over(False, self.buf.at[c, x, ys(b)])
            else:
                for b in range(1, X):
                    self.over(True, self.buf.at[c, xs(b), y])

        def core_out(self):
            third = list(self.arrived(not self.y_first, True))
            got(third)
            pending.extend(third)
            plane = self.buf.at[c]
            self.core = [Sent(lambda: copy_at(self.ic, plane, plane, dev(c_=oth)))]
            self.core[0].make().start()
            pending.extend(self.core)
            self.last = third + self.core

        def end(self):
            got(self.core)

    own_small = [jnp.zeros((16, 128), F32)]
    for at, key in enumerate(("ls", "lc", "lf", "rel")):
        v = getattr(m, key)[...].astype(F32)
        v = jnp.concatenate([v, jnp.zeros((1, 128 - v.shape[1]), F32)], axis=1)
        own_small[0] = jnp.where(iota((16, 128), 0) == at, v, own_small[0])
    smb[c, x, y, z] = own_small[0].astype(BF)
    moves = {}

    def begin(p, feed="gather"):
        moves[p] = Gather(gw.at[p], p not in Y_GATHERED_LAST, feed, p < CO)

    moves["small"] = Gather(smb, True, first=True)
    moves["small"].z_out()
    moves["small"].own_out()
    sources = (
        (m.sq, 0), (m.skv, 0), (m.skv, D), (m.so, 0),
        (m.cq, 0), (m.ckv, 0), (m.ckv, D), (m.co, 0),
    )

    def pack(p):
        ref, off = sources[p]
        v = ref[:, off : off + D].astype(F32)
        put_halves(gw.at[p, c, x, y, z], v[:, 0:nh], v[:, nh:D], r, rb)
        begin(p)
        if p in (SQ, SK, SV):
            moves[p].z_out()
        moves[p].own_out()

    for p in (SQ, SK, SV, SO, CQ, CK, CV, CO):
        pack(p)

    g3 = m.g3
    live = (iota((T, 1), 0) < m.len[...]).astype(F32)
    g3[z] = (live * m.og[...]).astype(BF)

    def line_start(base, buf):
        for a in range(1, Z):
            copy_at(base + a, buf.at[z], buf.at[z], dev(z_=zs(a))).start()

    def line_wait(base, buf):
        for a in range(1, Z):
            copy_at(base + a, buf.at[z], buf.at[z], dev(z_=zs(a))).wait_recv()

    def line_done(base, buf):
        for a in range(1, Z):
            copy_at(base + a, buf.at[z], buf.at[z], dev(z_=zs(a))).wait_send()

    def act_start(base, bufs):
        for n, buf in enumerate(bufs):
            for a in range(1, Z):
                copy_at(base + n * YZ + a, buf.at[z, y], buf.at[z, y], dev(z_=zs(a))).start()

    def act_forward(base, bufs, a):
        zi = zs(a)
        for n, buf in enumerate(bufs):
            for b in range(1, Y):
                copy_at(
                    base + n * YZ + b * Z + (Z - a) % Z, buf.at[zi, y], buf.at[zi, y], dev(y_=ys(b))
                ).start()

    def act_wait(base, bufs, t):
        at = base + (Y - t // Z) % Y * Z + (Z - t % Z) % Z
        for n, buf in enumerate(bufs):
            copy_at(at + n * YZ, buf.at[z, y], buf.at[z, y], dev(z_=zs(1))).wait_recv()

    def act_done(base, bufs):
        for n, buf in enumerate(bufs):
            for t in range(1, YZ):
                copy_at(base + n * YZ + t, buf.at[z, y], buf.at[z, y], dev(z_=zs(1))).wait_send()

    fip = m.fip
    ndp = 2 * X
    per = D // ndp

    def pack_ff():
        even = m.even
        for k in range(Z):
            for i in range(ndp):
                at = (i * Z + k) * per
                even[:, i * per : (i + 1) * per] = m.fi_in[:, at : at + per].astype(F32)
            put_halves(fip.at[k], even[:, 0:nh], even[:, nh:D], r, rb)
        vo = m.fo_in[...].astype(F32)
        if r % 8:
            lift[0 : Z * r, :] = vo
        for k in range(Z):
            part = lift[k * r : k * r + r, :] if r % 8 else vo[k * r : k * r + r]
            put_halves(gw.at[FO, c, x, y, k], part[:, 0:nh], part[:, nh:D], r, rb)
        gw[FI, c, x, y, z] = fip[z]

    g3_base = take(Z)

    spread = m.spread
    lane = iota((16, D), 1)
    row = iota((16, D), 0)
    spread[...] = ((lane >= row * DK) & (lane < row * DK + DK)).astype(F32)
    m.spread2[...] = jnp.concatenate([spread[...], spread[...]], axis=0).astype(BF)
    tlane = iota((T, 128), 1)
    rbs = HEADS * BUCKETS // (2 * X * YZ)

    def repeat_of(width, step):
        l0, n0 = iota((128, width), 0), iota((128, width), 1)

        def body(k, tot):
            return tot + ((n0 - l0 == k * step) & (l0 < step)).astype(F32)

        return lax.fori_loop(0, width // step, body, jnp.zeros((128, width), F32)).astype(BF)

    m.hot_gain[...] = repeat_of(D, r)
    m.hot_bias[...] = repeat_of(HEADS * BUCKETS, rbs)

    def unpack(p):
        group = 2 * Y * r

        if p == FO:
            group = YZ * r
            parts = [(yy, zz) for yy in range(Y) for zz in range(Z)]
        else:
            parts = [(yy, zz) for zz in range(2) for yy in range(Y)]
        per = YZ // len(parts)

        def body(g, carry):
            x_ = g // (2 * per)
            c_ = (g // per) % 2
            zp = 0 if per == 1 else g % per
            lefts, rights = [], []
            at = 0
            for yy, zz in parts:
                lo, hi = get_halves(gw[p, c_, x_, yy, 2 * zp + zz].astype(F32), r)
                if r % 8 == 0:
                    lefts.append(lo)
                    rights.append(hi)
                else:
                    lift[at : at + r, 0:nh] = lo
                    lift[at : at + r, nh:D] = hi
                at += r
            rows = pl.ds(pl.multiple_of(g * group, 16), group)
            if r % 8 == 0:
                w[p, rows, 0:nh] = jnp.concatenate(lefts, axis=0).astype(BF)
                w[p, rows, nh:D] = jnp.concatenate(rights, axis=0).astype(BF)
            else:
                w[p, rows, :] = lift[0:group, :].astype(BF)
            return carry

        lax.fori_loop(0, X * 2 * per, body, 0)

    gain = m.gain
    bias = m.bias
    def read_small():
        flat = HEADS * BUCKETS
        every = smb[...].reshape(2 * X * YZ * 16, 128)
        wide_g, wide_b = nn(every, m.hot_gain[...]), nn(every, m.hot_bias[...])
        ng, nb = iota((16, D), 1), iota((16, flat), 1)
        gains, tot = jnp.zeros((16, D), F32), jnp.zeros((16, flat), F32)
        at = 0
        for c_ in range(2):
            for x_ in range(X):
                for y_ in range(Y):
                    for z_ in range(Z):
                        k = (x_ * 2 + c_) * YZ + z_ * Y + y_
                        mine = (ng >= k * r) & (ng < k * r + r)
                        gains = jnp.where(mine, wide_g[at : at + 16], gains)
                        mine = (nb >= k * rbs) & (nb < k * rbs + rbs)
                        tot = jnp.where(mine, wide_b[at : at + 16], tot)
                        at += 16
        gain[...] = gains
        per = jnp.broadcast_to(tot[3:4, :], (16, flat))
        h0, n0 = iota((16, flat), 0), iota((16, flat), 1)
        per = jnp.where((n0 >= h0 * BUCKETS) & (n0 < h0 * BUCKETS + BUCKETS), per, 0.0)
        nb, mb = iota((flat, 128), 0), iota((flat, 128), 1)
        dist = jnp.where(mb == 0, 0, 128 - mb)
        hot = ((nb & (BUCKETS - 1)) == bucket_of(dist)).astype(F32).astype(BF)
        table = nn(per.astype(BF), hot)
        for h in range(HEADS):
            wide = jnp.broadcast_to(table[h : h + 1, :], (T, 128))
            rolled = pltpu.roll(wide, 0, 1, stride=1, stride_axis=0)
            bias[h // QUAD, (h % QUAD) * T : (h % QUAD + 1) * T, :] = rolled[:, 0:T]

    tok = m.tok

    def self_forward():
        m.h1[...] = normed(tok[...], gain[0:1, :]).astype(BF)
        h1 = m.h1[...]
        m.qs[...] = nn(h1, w[SQ]).astype(BF)
        m.ks[...] = nn(h1, w[SK]).astype(BF)
        m.vs[...] = nn(h1, w[SV]).astype(BF)
        allowed = iota((WIDE, T), 1) <= (iota((WIDE, T), 0) & (T - 1))
        for t in range(NQ):
            s = nt(stack4(m.qs[:, quad(t)]), m.ks[:, quad(t)]) + bias[t]
            s = jnp.where(allowed, s, NEG)
            e = jnp.exp(s - jnp.max(s, axis=1, keepdims=True))
            pr = e / jnp.sum(e, axis=1, keepdims=True)
            m.ps[t] = pr
            m.os[:, quad(t)] = fold4(nn(pr.astype(BF), m.vs[:, quad(t)])).astype(BF)

    qc = m.qc
    qc_base = take(YZ)

    def self_out():
        x1 = tok[...] + nn(m.os[...], w[SO])
        m.x1[...] = x1
        m.h2[...] = normed(x1, gain[1:2, :]).astype(BF)

    def cross_query():
        qc[z, y] = nn(m.h2[...], w[CQ]).astype(BF)
        act_start(qc_base, [qc])
        act_forward(qc_base, [qc], 0)

    kv, pas = m.kv, m.pas

    chunk = 2 if R % 16 == 0 else 1

    tall = 4 if R % 16 == 0 else 1

    def project(p, off, k0, k1):
        def part(k, carry):
            rows = pl.ds(k // NQ * tall, tall)
            at = k % NQ * WIDE
            cols = pl.ds(pl.multiple_of(at, WIDE), WIDE)
            v = nn(pas[rows].reshape(tall * R, D), w[p, :, cols])
            cols = pl.ds(pl.multiple_of(off + at, WIDE), WIDE)
            kv[rows, :, cols] = v.astype(BF).reshape(tall, R, WIDE)
            return carry

        lax.fori_loop(k0 * NQ, k1 * NQ, part, 0)

    def project_one(q, p, off):
        kv[q, :, off : off + D] = nn(pas[q], w[p]).astype(BF)

    held = Buffers()

    def after(p):
        unpack(p)
        if p == SQ:
            moves["small"].end()
            read_small()
        elif p == SV:
            self_forward()
        elif p == SO:
            self_out()
        elif p == CQ:
            cross_query()
        elif p == CK:
            load_pas.wait()
            project(CK, 0, 0, YZ // tall // 2)

    order = (SQ, SK, SV, SO, CQ, CK, CV, CO, FI, FO)

    def line_out(k):
        if k == 0:
            moves["small"].line_out()
        moves[order[k]].line_out()

    def pair_out(k):
        if k == 0:
            moves["small"].pair_out()
        moves[order[k]].pair_out()
        if k + 3 < 8:
            moves[order[k + 3]].z_out()

    def plane_out(k):
        if k == 0:
            moves["small"].plane_out()
        moves[order[k]].plane_out()

    def core_out(k):
        if k == 0:
            moves["small"].core_out()
        moves[order[k]].core_out()

    def arrive(k):
        moves[order[k]].end()
        after(order[k])

    def query_out(a):
        act_wait(qc_base, [qc], a)
        act_forward(qc_base, [qc], a)

    pair_out(0)
    pair_out(1)
    line_out(0)
    pack_ff()
    pair_out(2)
    line_out(1)
    plane_out(0)
    pair_out(3)
    line_out(2)
    plane_out(1)
    core_out(0)
    pair_out(4)
    line_out(3)
    begin(FI, "exchange")
    plane_out(2)
    arrive(0)
    core_out(1)
    pair_out(5)
    line_out(4)
    plane_out(3)
    arrive(1)
    core_out(2)
    pair_out(6)
    line_out(5)
    line_start(g3_base, g3)
    plane_out(4)
    arrive(2)
    core_out(3)
    line_out(6)
    plane_out(5)
    pair_out(7)
    arrive(3)
    core_out(4)
    arrive(4)
    plane_out(6)
    core_out(5)
    line_out(7)
    begin(FO, "local")
    moves[FI].own_out()
    moves[FO].own_out()
    line_out(8)
    line_out(9)
    arrive(5)
    core_out(6)
    query_out(1)
    project(CK, 0, YZ // tall // 2, YZ // tall)
    arrive(6)
    query_out(2)
    plane_out(7)
    query_out(3)

    po, pst, ryo, ryst, rzo, rzst = m.po, m.pst, m.ryo, m.ryst, m.rzo, m.rzst

    def rs_y_base():
        return take((Y - 1) * Z)

    def rs_y_send(base, src, dst, b, a):
        zi = zs(a)
        copy_at(base + (b - 1) * Z + a, src.at[b, zi], dst.at[b - 1, zi], dev(y_=ys(b))).start()

    def rs_y_wait(base, src, dst, b, a):
        copy_at(base + (b - 1) * Z + a, src.at[b, 0], dst.at[b - 1, 0], dev(y_=ys(1))).wait_recv()

    def rs_y_done(base, src, dst):
        for b in range(1, Y):
            for a in range(Z):
                copy_at(
                    base + (b - 1) * Z + a, src.at[b, 0], dst.at[b - 1, 0], dev(y_=ys(1))
                ).wait_send()

    yo_base, yst_base = rs_y_base(), rs_y_base()
    zo_base, zst_base = take(Z), take(Z)

    def attend(a, b):
        zi = zs(a)
        yi = ys(b)
        qi = zi * Y + yi
        st = jnp.zeros((T, 128), F32)
        for k in range(NQ):
            qb = stack4(qc[zi, yi, :, quad(k)])
            s = nt(qb, kv[qi, :, quad(k)])
            top = jnp.max(s, axis=1, keepdims=True)
            e = jnp.exp(s - top)
            tot = jnp.sum(e, axis=1, keepdims=True)
            u = nn(e.astype(BF), kv[qi, :, D + k * WIDE : D + (k + 1) * WIDE])
            po[b, zi, :, quad(k)] = fold4(u * (1.0 / tot)).astype(BF)
            lse = top + jnp.log(tot)
            for h in range(QUAD):
                st = jnp.where(tlane == k * QUAD + h, lse[h * T : (h + 1) * T], st)
        pst[b, zi] = st.T[0:16]

    def expand(st):
        return lax.dot_general(
            st, spread[...], (((0,), (0,)), ((), ())), preferred_element_type=F32, precision=HIGH
        )

    def expand_low(v):
        hi = v.astype(BF)
        lo = (v - hi.astype(F32)).astype(BF)
        both = jnp.concatenate([hi, lo], axis=0)
        ones = m.spread2[...]
        return tn(both, ones)

    def merge(parts):
        top = parts[0][1]
        for _, st in parts[1:]:
            top = jnp.maximum(top, st)
        ws = [jnp.exp(st - top) for _, st in parts]
        tot = ws[0]
        for v in ws[1:]:
            tot = tot + v
        out = jnp.zeros((T, D), F32)
        for (o, _), v in zip(parts, ws):
            out = out + expand_low(v / tot) * o.astype(F32)
        return out, top + jnp.log(tot)

    def z_send(base, src, dst, a):
        zi = zs(a)
        copy_at(base + a, src.at[0, zi], dst.at[a - 1], dev(z_=zi)).start()

    def z_each(base, src, dst, wait):
        for a in range(1, Z):
            cp = copy_at(base + a, src.at[0, 0], dst.at[a - 1], dev(z_=zs(a)))
            if wait == "recv":
                cp.wait_recv()
            else:
                cp.wait_send()

    def pass_on(a):
        zi = zs(a)
        for b in range(1, Y):
            rs_y_wait(yo_base, po, ryo, b, a)
            rs_y_wait(yst_base, pst, ryst, b, a)
        o, st = merge(
            [(po[0, zi], pst[0, zi])] + [(ryo[b - 1, zi], ryst[b - 1, zi]) for b in range(1, Y)]
        )
        po[0, zi] = o.astype(BF)
        pst[0, zi] = st
        z_send(zo_base, po, rzo, a)
        z_send(zst_base, pst, rzst, a)

    def attend_own(a):
        project_one(zs(a) * Y + y, CV, D)
        attend(a, 0)

    def attend_others(a):
        def body(b, carry):
            project_one(zs(a) * Y + ys(b), CV, D)
            act_wait(qc_base, [qc], b * Z + a)
            attend(a, b)
            rs_y_send(yo_base, po, ryo, b, a)
            rs_y_send(yst_base, pst, ryst, b, a)
            return carry

        lax.fori_loop(1, Y, body, 0)

    def attend_step(k, carry):
        attend_others((k + 1) % Z)
        attend_own(k)
        pass_on(k)

        @pl.when(k == 2)
        def _():
            core_out(7)

        return carry

    attend_own(0)
    attend_others(1)
    plane_out(8)
    plane_out(9)
    lax.fori_loop(1, Z, attend_step, 0)
    arrive(7)
    for b in range(1, Y):
        rs_y_wait(yo_base, po, ryo, b, 0)
        rs_y_wait(yst_base, pst, ryst, b, 0)
    z_each(zo_base, po, rzo, "recv")
    z_each(zst_base, pst, rzst, "recv")
    o, lse = merge(
        [(po[0, z], pst[0, z])]
        + [(ryo[b - 1, z], ryst[b - 1, z]) for b in range(1, Y)]
        + [(rzo[a - 1], rzst[a - 1]) for a in range(1, Z)]
    )
    m.oc[...] = o.astype(BF)
    m.lse[...] = lse
    x2 = m.x1[...] + nn(m.oc[...], w[CO])
    m.x2[...] = x2
    h3 = m.h3
    h3[z] = normed(x2, gain[2:3, :]).astype(BF)
    h3_base = take(Z)
    line_start(h3_base, h3)

    rc, r1, r1y, r2, r2x, rz, act, cot = (getattr(m, k, None) for k in SPOTS[3:])

    def share(buf):
        own = buf.at[x, c]
        near_c = send(own, own, dev(c_=oth))
        return [send(own, own, dev(x_=xs(b))) for b in range(1, X)], near_c

    def share_on(buf, cps):
        far, near_c = cps
        got(far)
        out = [near_c]
        for b in range(1, X):
            block = buf.at[xs(b), c]
            out.append(send(block, block, dev(c_=oth)))
        return out

    def share_acts():
        if sz.inside:
            for n, name in enumerate(ACTS):
                act[n, x, c] = getattr(m, name)[...]
            held.acts = [share(act.at[n]) for n in range(len(ACTS))]

    def share_acts_on():
        if sz.inside:
            held.acts = [share_on(act.at[n], cps) for n, cps in enumerate(held.acts)]

    def share_acts_end():
        if sz.inside:
            for cps in held.acts:
                got(cps)
    drain()
    share_acts()

    core_out(8)
    core_out(9)
    arrive(8)
    line_wait(g3_base, g3)
    arrive(9)
    gb = g3[...].reshape(Z * T, D)
    m.kvacc.at[0 : Z * T, 0:hid][...] = nt(gb, w[FO])
    act_done(qc_base, [qc])
    rs_y_done(yo_base, po, ryo)
    rs_y_done(yst_base, pst, ryst)
    z_each(zo_base, po, rzo, "send")
    z_each(zst_base, pst, rzst, "send")
    py, rzy = Spot(m.py), Spot(m.rzy)
    gl, du = m.gl, m.du
    line_wait(h3_base, h3)
    lifted, slope = gelu_pair(nn(h3[...].reshape(Z * T, D), w[FI]))
    du[...] = (m.kvacc.at[0 : Z * T, 0:hid][...] * slope).astype(BF)
    gl[...] = lifted.astype(BF)
    po[0] = nt(du[...], w[FI]).astype(BF).reshape(Z, T, D)

    def rs_z(part, rzb):
        return [send(part.at[zs(a)], rzb.at[a - 1], dev(z_=zs(a))) for a in range(1, Z)]

    def rs_total(part, rzb):
        tot = part[z].astype(F32)
        for a in range(1, Z):
            tot = tot + rzb[a - 1].astype(F32)
        return tot

    zh = rs_z(po.at[0], rzo)
    py[...] = nn(gl[...], w[FO]).astype(BF).reshape(Z, T, D)
    line_done(h3_base, h3)
    line_done(g3_base, g3)

    acc = m.kvacc.at[:, 0:D]

    def add_to(dst, src):
        dst[...] = (dst[...].astype(F32) + src[...].astype(F32)).astype(BF)

    def add_blocks(rows, dst, src):
        def body(i, carry):
            add_to(dst(i // Z, i % Z), src(i // Z, i % Z))
            return carry

        lax.fori_loop(0, rows * Z, body, 0)

    def pack_grad(p, acc, col):
        group = YZ * r
        if not sz.inside:
            name, off = targets[p]
            out = getattr(m, name) if p in (FI, FO) else getattr(m, name).at[:, off : off + D]
            cp = pltpu.make_async_copy(acc.at[:, col : col + D], out, lsem.at[0])
            cp.start()
            cp.wait()
            return None

        def body(k, carry):
            x_ = k // 2
            c_ = k % 2
            for z_ in range(Z):
                for y_ in range(Y):
                    at = (y_ * Z + z_) * r if p == FO else (z_ * Y + y_) * r
                    rows = pl.ds(pl.multiple_of(k * group + at, 8), r)
                    left, right = acc[rows, col : col + nh], acc[rows, col + nh : col + D]
                    put_halves(gw.at[p, c_, x_, y_, z_], left, right, r, rb)
            return carry

        lax.fori_loop(0, 2 * X, body, 0)
        return [send(gw.at[p, oth], rc.at[WIDE_PIECES.index(p)], dev(c_=oth))]

    def rs_first(p, cps):
        got(cps)
        n = WIDE_PIECES.index(p)
        add_blocks(
            X * Y,
            lambda k, z_: gw.at[p, c, k // Y, k % Y, z_],
            lambda k, z_: rc.at[n, k // Y, k % Y, z_],
        )
        if p in Y_SUMMED_FIRST:
            return [
                send(gw.at[p, c, :, ys(b)], r1y.at[n, b - 1], dev(y_=ys(b))) for b in range(1, Y)
            ]
        return [send(gw.at[p, c, xs(b)], r1.at[n, b - 1], dev(x_=xs(b))) for b in range(1, X)]

    def to_y(p):
        return [send(gw.at[p, c, x, ys(b)], r2.at[p, b - 1], dev(y_=ys(b))) for b in range(1, Y)]

    def rs_second(p, cps):
        got(cps)
        n = WIDE_PIECES.index(p)
        if p in Y_SUMMED_FIRST:
            for b in range(1, Y):
                add_blocks(
                    X,
                    lambda k, z_: gw.at[p, c, k, y, z_],
                    lambda k, z_: r1y.at[n, b - 1, k, z_],
                )
            return [
                send(gw.at[p, c, xs(b), y], r2x.at[n, b - 1], dev(x_=xs(b))) for b in range(1, X)
            ]
        for b in range(1, X):
            add_blocks(
                Y,
                lambda k, z_: gw.at[p, c, x, k, z_],
                lambda k, z_: r1.at[n, b - 1, k, z_],
            )
        return to_y(p)

    def factor_on(p, cps):
        return share_on(cot.at[p], cps)

    def factor_product(p, cps):
        got(cps)
        group = YZ * r
        first = (x * 2 + c) * group
        lanes = first // 128 * 128
        shift = pl.multiple_of(first - lanes, 8)
        lhs = act[ACTS.index(FACTORS[p]), :, :, :, pl.ds(pl.multiple_of(lanes, 128), WIDE)]
        acc[0:WIDE, :] = tn(lhs.reshape(2 * X * T, WIDE), cot[p].reshape(2 * X * T, D))

        def body(i, carry):
            y_ = i % Y
            z_ = i // Y
            rows = pl.ds(pl.multiple_of(shift + i * r, 8), r)
            put_halves(gw.at[p, c, x, y_, z_], acc[rows, 0:nh], acc[rows, nh:D], r, rb)
            return carry

        lax.fori_loop(0, YZ, body, 0)
        return to_y(p)

    def rs_third(p, cps):
        got(cps)
        second = (
            [r2x.at[WIDE_PIECES.index(p), b - 1] for b in range(1, X)]
            if p in Y_SUMMED_FIRST
            else [r2.at[p, b - 1] for b in range(1, Y)]
        )
        for part in second:
            add_blocks(1, lambda k, z_: gw.at[p, c, x, y, z_], lambda k, z_: part.at[z_])
        if p == FO:
            return []
        if p in Z_AT_ONCE:
            return [
                send(gw.at[p, c, x, y, zs(a)], rz.at[p, a - 1], dev(z_=zs(a)))
                for a in range(1, Z)
            ]
        return [
            send(gw.at[p, c, x, y, k], rz.at[p, n], dev(z_=z_near))
            for n, k in enumerate((z_near, z_cross))
        ]

    def rs_fourth(p, cps):
        got(cps)
        if p == FO or p in Z_AT_ONCE:
            return []
        add_to(gw.at[p, c, x, y, z_far], rz.at[p, 1])
        return [send(gw.at[p, c, x, y, z_far], rz.at[p, 2], dev(z_=z_far))]

    targets = {
        SQ: ("g_sq", 0), SK: ("g_skv", 0), SV: ("g_skv", D), SO: ("g_so", 0),
        CQ: ("g_cq", 0), CK: ("g_ckv", 0), CV: ("g_ckv", D), CO: ("g_co", 0),
        FI: ("g_fi", 0), FO: ("g_fo", 0),
    }

    def rs_last(p, cps):
        got(cps)
        name, off = targets[p]
        if p in (FI, FO):
            for a in range(Z):
                k = a if p == FO else zs((Z - a) % Z)
                if p == FO:
                    v = gw[p, c, x, y, a]
                else:
                    v = rz[p, a - 1] if a else gw[p, c, x, y, z]
                lo, hi = get_halves(v.astype(F32), r)
                if p == FI:
                    m.kvacc[pl.ds(pl.multiple_of(k * r, 8), r), 0:nh] = lo
                    m.kvacc[pl.ds(pl.multiple_of(k * r, 8), r), nh:D] = hi
                else:
                    getattr(m, name)[k * r : k * r + r, 0:nh] = lo
                    getattr(m, name)[k * r : k * r + r, nh:D] = hi
            if p == FI:
                for k in range(Z):
                    for i in range(ndp):
                        at = (i * Z + k) * per
                        getattr(m, name)[:, at : at + per] = m.kvacc[k * r : k * r + r, i * per : (i + 1) * per]
            return None
        v = gw[p, c, x, y, z].astype(F32) + rz[p, 0].astype(F32) + rz[p, 2].astype(F32)
        if p in Z_AT_ONCE:
            v = v + rz[p, 1].astype(F32)
        lo, hi = get_halves(v, r)
        getattr(m, name)[:, off : off + nh] = lo
        getattr(m, name)[:, off + nh : off + D] = hi

    wide_stages = (rs_first, rs_second, rs_third, rs_fourth, rs_last) if sz.inside else ()
    factor_stages = (factor_on, factor_product, rs_third, rs_fourth, rs_last) if sz.inside else ()

    def stages_of(p):
        return factor_stages if p in FACTORS else wide_stages

    moving = {}

    def grad_of(p, lhs, rhs):
        if sz.inside and p in FACTORS:
            cot[p, x, c] = rhs[...]
            moving[p] = (0, share(cot.at[p]))
            return

        def part(k, carry):
            cols = pl.ds(pl.multiple_of(k * WIDE, WIDE), WIDE)
            left = lhs[:, :, cols].reshape(Z * T, WIDE) if len(lhs.shape) == 3 else lhs[:, cols]
            acc[cols, :] = tn(left, rhs[...])
            return carry

        lax.fori_loop(0, NQ, part, 0)
        grad_out(p)

    def grad_out(p, src=None, col=0):
        moving[p] = (0, pack_grad(p, acc if src is None else src, col))

    def push(p):
        k, cps = moving[p]
        if k < len(stages_of(p)):
            moving[p] = (k + 1, stages_of(p)[k](p, cps))

    def push_all(ps):
        for p in ps:
            push(p)

    sent(moves[FI].last + moves[FO].last)
    spare.extend(early[1])
    grad_of(FO, gl, gb)
    grad_of(FI, h3, du)
    push_all([FO, FI])
    share_acts_on()
    sm = m.sm
    sm[...] = jnp.zeros_like(sm)
    do, dr = m.do, m.dr
    do_base = take(2 * YZ)
    pick = iota((T, D), 0) == (iota((T, D), 1) & (T - 1))

    def as_rows(st):
        v = jnp.sum(jnp.where(pick, expand(st), 0.0), axis=0, keepdims=True)
        parts = [v[:, k * 128 : (k + 1) * 128] for k in range(D // 128)]
        return jnp.concatenate(parts + [jnp.zeros((8 - D // 128, 128), F32)], axis=0)

    dr[z, y, 0:8] = as_rows(m.lse[...])
    got(zh)
    dh3 = rs_total(po.at[0], rzo)
    dv, gg = norm_back(m.x2[...], gain[2:3, :], dh3)
    sm[2:3, :] = gg
    dx2 = live * m.og[...] + dv
    m.dx[...] = dx2
    dx2l = dx2.astype(BF)
    doc = nt(dx2l, w[CO]).astype(BF)
    do[z, y] = doc
    act_start(do_base, [do])
    act_forward(do_base, [do], 0)
    prod = doc.astype(F32) * m.oc[...].astype(F32)
    delta = lax.dot_general(
        spread[...], prod, (((1,), (1,)), ((), ())), preferred_element_type=F32, precision=HIGH
    )
    dr[z, y, 8:16] = as_rows(delta)
    act_start(do_base + YZ, [dr])
    act_forward(do_base + YZ, [dr], 0)
    grad_of(CO, m.oc, dx2l)

    sent(zh)
    yq_base = rs_y_base()

    def row_of(ref, k):
        return jnp.concatenate([ref[2 * k : 2 * k + 1, :], ref[2 * k + 1 : 2 * k + 2, :]], axis=1)

    zq_base = take(Z)

    def pass_back(a):
        zi = zs(a)
        for b in range(1, Y):
            rs_y_wait(yq_base, po, ryo, b, a)
        tot = po[0, zi].astype(F32)
        for b in range(1, Y):
            tot = tot + ryo[b - 1, zi].astype(F32)
        po[0, zi] = tot.astype(BF)
        z_send(zq_base, po, rzo, a)

    def attend_back(a, b):
        zi = zs(a)
        yi = ys(b)
        qi = zi * Y + yi

        lse_rows = dr[zi, yi, 0:8]
        delta_rows = dr[zi, yi, 8:16]
        for k in range(NQ):
            qb = stack4(qc[zi, yi, :, quad(k)])
            db = stack4(do[zi, yi, :, quad(k)])
            kt = kv[qi, :, quad(k)]
            vt = kv[qi, :, D + k * WIDE : D + (k + 1) * WIDE]
            pt = jnp.exp(nt(kt, qb) - row_of(lse_rows, k))
            ds = (pt * (nt(vt, db) - row_of(delta_rows, k))).astype(BF)
            po[b, zi, :, quad(k)] = fold4(tn(ds, kt)).astype(BF)
            kv[qi, :, quad(k)] = nn(ds, qb).astype(BF)
            kv[qi, :, D + k * WIDE : D + (k + 1) * WIDE] = nn(pt.astype(BF), db).astype(BF)


    kvacc = m.kvacc

    def kv_grad(q):
        def part(k, carry):
            cols = pl.ds(pl.multiple_of(k * WIDE, WIDE), WIDE)
            kvacc[cols, :] += tn(pas[q, :, cols], kv[q])
            return carry

        lax.fori_loop(0, NQ, part, 0)

    def kv_grads(t0, t1):
        def body(t, carry):
            kv_grad(zs(t // Y) * Y + ys(t % Y))
            return carry

        lax.fori_loop(t0, t1, body, 0)

    def back_own(a):
        attend_back(a, 0)

    def back_others(a):
        def body(b, carry):
            act_wait(do_base, [do, dr], b * Z + a)
            attend_back(a, b)
            rs_y_send(yq_base, po, ryo, b, a)
            return carry

        lax.fori_loop(1, Y, body, 0)

    def back_step(k, carry):
        act_wait(do_base, [do, dr], k + 1)
        act_forward(do_base, [do, dr], k + 1)
        back_others(k)

        @pl.when(k < Z - 2)
        def _():
            kv_grads(k * Y + 1, k * Y + Y)

        @pl.when(k == 1)
        def _():
            push(CO)
            share_acts_end()
            held.zy = rs_z(py, rzy)

        @pl.when(k == Z - 2)
        def _():
            push(FI)

        back_own(k + 1)

        @pl.when(k < Z - 2)
        def _():
            kv_grads(k * Y + Y, k * Y + Y + 1)

        return carry

    kvacc[...] = jnp.zeros_like(kvacc)
    back_own(0)
    kv_grad(z * Y + y)
    push(FO)
    lax.fori_loop(0, Z - 1, back_step, 0)
    back_others(Z - 1)
    def row_grads(k0, k1):
        def whole(k, carry):
            pas[k] = (nt(kv[k, :, 0:D], w[CK]) + nt(kv[k, :, D : 2 * D], w[CV])).astype(BF)
            pltpu.make_async_copy(pas.at[k], m.pg.at[k], lsem.at[1 + k]).start()
            return carry

        def part(k, carry):
            rows = pl.ds(k // NQ * chunk, chunk)
            cols = pl.ds(pl.multiple_of(k % NQ * WIDE, WIDE), WIDE)
            v = nt(kv[rows, :, 0:D].reshape(chunk * R, D), w[CK, cols, :])
            v = v + nt(kv[rows, :, D : 2 * D].reshape(chunk * R, D), w[CV, cols, :])
            pas[rows, :, cols] = v.astype(BF).reshape(chunk, R, WIDE)

            @pl.when(k % NQ == NQ - 1)
            def _():
                for q in range(chunk):
                    at = k // NQ * chunk + q
                    pltpu.make_async_copy(pas.at[at], m.pg.at[at], lsem.at[1 + at]).start()

            return carry

        if chunk == 1:
            lax.fori_loop(k0, k1, whole, 0)
        else:
            lax.fori_loop(k0 * NQ, k1 * NQ, part, 0)

    part = YZ // chunk // 4

    def take_dq():
        for b in range(1, Y):
            rs_y_wait(yq_base, po, ryo, b, 0)
        z_each(zq_base, po, rzo, "recv")
        dqc = rs_total(po.at[0], rzo)
        for b in range(1, Y):
            dqc = dqc + ryo[b - 1, z].astype(F32)
        held.dqc = dqc.astype(BF)
        dh2 = nt(held.dqc, w[CQ])
        dv, gg = norm_back(m.x1[...], gain[1:2, :], dh2)
        sm[1:2, :] = gg
        dx1 = m.dx[...] + dv
        m.dx[...] = dx1
        held.dx1l = dx1.astype(BF)

    def self_back():
        m.oc[...] = nt(held.dx1l, w[SO]).astype(BF)
        grads = [[], [], []]
        held.tail = []
        back = (iota((T, 128), 1) == T - 1 - iota((T, 128), 0)).astype(F32).astype(BF)
        for t in range(NQ):
            db = stack4(m.oc[:, quad(t)])
            qb = stack4(m.qs[:, quad(t)])
            pr = m.ps[t]
            dps = nt(db, m.vs[:, quad(t)])
            dss = (pr * (dps - jnp.sum(pr * dps, axis=1, keepdims=True))).astype(BF)
            grads[0].append(fold4(nn(dss, m.ks[:, quad(t)])).astype(BF))
            grads[1].append(tn(dss, qb).astype(BF))
            grads[2].append(tn(pr.astype(BF), db).astype(BF))
            turned = nn(dss, back)
            for h in range(QUAD):
                part = pltpu.roll(turned[h * T : (h + 1) * T], 0, 1, stride=1, stride_axis=0)
                held.tail.append(jnp.sum(part, axis=0, keepdims=True))
        held.dqs, held.dks, held.dvs = (jnp.concatenate(g, axis=1) for g in grads)

    def token_grad():
        dh1 = nt(held.dqs, w[SQ]) + nt(held.dks, w[SK]) + nt(held.dvs, w[SV])
        dv, gg = norm_back(tok[...], gain[0:1, :], dh1)
        sm[0:1, :] = gg
        m.tg[...] = m.dx[...] + dv
        flat = HEADS * BUCKETS
        diag = jnp.concatenate(held.tail + [jnp.zeros((16 - HEADS, 128), F32)], axis=0)
        mi, bi = iota((128, 128), 0), iota((128, 128), 1)
        hot = ((mi >= T - 1) & (bucket_of(mi - (T - 1)) == bi) & (bi < BUCKETS)).astype(F32)
        table = nn_high(diag, hot)
        bb, nb = iota((128, flat), 0), iota((128, flat), 1)
        wide = nn_high(table, ((nb & (BUCKETS - 1)) == bb).astype(F32))
        h0, n0 = iota((16, flat), 0), iota((16, flat), 1)
        own = (n0 >= h0 * BUCKETS) & (n0 < h0 * BUCKETS + BUCKETS)
        sm[3:4, 0:flat] = jnp.sum(jnp.where(own, wide, 0.0), axis=0, keepdims=True)

    rsm = m.rsm
    slot = [0]

    def small_to(devs):
        held.small = []
        for to in devs:
            held.small.append((slot[0], send(sm, rsm.at[slot[0]], to)))
            slot[0] += 1

    def small_got():
        got([cp for _, cp in held.small])
        sent([cp for _, cp in held.small])
        for k, _ in held.small:
            sm[...] += rsm[k]

    def small_step(k):
        if k:
            small_got()
        if k < 4:
            small_to(
                (
                    [dev(c_=oth)],
                    [dev(x_=xs(b)) for b in range(1, X)],
                    [dev(y_=ys(b)) for b in range(1, Y)],
                    [dev(z_=zs(a)) for a in range(1, Z)],
                )[k]
            )

    def block_out():
        got(held.zy)
        m.bo[...] = live * (m.x2[...] + rs_total(py, rzy))

    steps = {
        DO_CK: lambda: grad_out(CK, kvacc, 0),
        DO_CV: lambda: grad_out(CV, kvacc, D),
        DO_KVG1: lambda: kv_grads((Z - 2) * Y + 1, YZ),
        DO_PASS: lambda: [pass_back(a) for a in range(1, Z)],
        DO_ROWS1: lambda: row_grads(0, part),
        DO_ROWS2: lambda: row_grads(part, 2 * part),
        DO_ROWS3: lambda: row_grads(2 * part, 3 * part),
        DO_ROWS4: lambda: row_grads(3 * part, YZ // chunk),
        DO_DQ: take_dq,
        DO_CQ: lambda: grad_of(CQ, m.h2, held.dqc),
        DO_SO: lambda: grad_of(SO, m.os, held.dx1l),
        DO_SELFBACK: self_back,
        DO_SV: lambda: grad_of(SV, m.h1, held.dvs),
        DO_SQ: lambda: grad_of(SQ, m.h1, held.dqs),
        DO_SK: lambda: grad_of(SK, m.h1, held.dks),
        DO_DH1: token_grad,
        DO_BO: block_out,
    }
    small_at = [0]

    def run(name):
        if name == DO_SMALL:
            small_step(small_at[0])
            small_at[0] += 1
        elif name < PIECES:
            push(name)
        else:
            steps[name]()

    for name in TAIL:
        run(name)
    assert all(k == len(stages_of(p)) for p, (k, _) in moving.items()), moving
    assert small_at[0] == 5
    me = dp * YZ + fs
    nd, ld = iota((D, 128), 0), iota((D, 128), 1)
    mine = nn_high(sm[...], ((nd == me * r + ld) & (ld < r)).astype(F32))
    mine_b = nn_high(sm[...], ((nd == me * rbs + ld) & (ld < rbs)).astype(F32))
    m.g_ls[...] = mine[0:1, 0:r]
    m.g_lc[...] = mine[1:2, 0:r]
    m.g_lf[...] = mine[2:3, 0:r]
    m.g_rb[...] = mine_b[3:4, 0:rbs]

    act_done(do_base, [do, dr])
    rs_y_done(yq_base, po, ryo)
    z_each(zq_base, po, rzo, "send")
    drain()

    def pg_wait(q, carry):
        pltpu.make_async_copy(pas.at[q], m.pg.at[q], lsem.at[1 + q]).wait()
        return carry

    lax.fori_loop(0, YZ, pg_wait, 0)


def place_kernel(*refs):
    n = len(OUTPUTS)
    given, put, held, sem = refs[:n], refs[n : 2 * n], refs[2 * n : 3 * n], refs[3 * n]
    loads, stores = [], []
    for k in range(n):
        parts = [slice(None)] if len(given[k].shape) < 3 else range(given[k].shape[0])
        for part in parts:
            at = len(loads)
            loads.append(pltpu.make_async_copy(given[k].at[part], held[k].at[part], sem.at[0, at]))
            stores.append(pltpu.make_async_copy(held[k].at[part], put[k].at[part], sem.at[1, at]))
    for cp in loads:
        cp.start()
    for load, store in zip(loads, stores):
        load.wait()
        store.start()
    for cp in stores:
        cp.wait()


def per_device(
    sz,
    targets, passages, tgt_len, out_grad, ln_self, rel_bias, self_q, self_kv, self_out,
    ln_cross, cross_q, cross_kv, cross_out, ln_ff, ff_in, ff_out,
):
    T, D, r, Z = sz.T, sz.D, sz.r, sz.Z
    ndp = 2 * sz.X
    per = sz.Y * sz.rff
    scratch = layout(sz)
    names = tuple(scratch)
    gr = r if sz.inside else D
    vm = pl.BlockSpec(memory_space=pltpu.VMEM)
    hbm = pl.BlockSpec(memory_space=pltpu.HBM)
    shape = jax.ShapeDtypeStruct
    rbs = rel_bias.shape[0]
    out_shape = (
        shape((T, D), F32), shape((T, D), F32), shape(passages.shape, BF),
        shape((1, r), F32), shape((1, rbs), F32),
        shape((gr, D), F32), shape((gr, 2 * D), F32), shape((gr, D), F32),
        shape((1, r), F32), shape((gr, D), F32), shape((gr, 2 * D), F32), shape((gr, D), F32),
        shape((1, r), F32),
        shape((r, Z * D) if sz.inside else (D, D), F32),
        shape((Z * r, D) if sz.inside else (D, D), F32),
    )
    weight_outs = ("g_sq", "g_skv", "g_so", "g_cq", "g_ckv", "g_co", "g_fi", "g_fo")
    apart = ("pg",) if sz.inside else ("pg",) + weight_outs
    outs = pl.pallas_call(
        functools.partial(block_kernel, sz, names),
        out_shape=out_shape,
        in_specs=[hbm if n == "pas_in" else vm for n in INPUTS],
        out_specs=tuple(hbm if n in apart else vm for n in OUTPUTS),
        scratch_shapes=tuple(scratch.values()),
        compiler_params=pltpu.CompilerParams(
            collective_id=0, has_side_effects=True, vmem_limit_bytes=63 * 2**20
        ),
        cost_estimate=pl.CostEstimate(
            flops=20 * 10**9, bytes_accessed=2 * 10**7, transcendentals=4 * 10**6
        ),
    )(
        targets[0], passages, tgt_len[None], out_grad[0], ln_self[None], rel_bias[None],
        self_q, self_kv, self_out, ln_cross[None], cross_q, cross_kv, cross_out,
        ln_ff[None], ff_in, ff_out,
    )
    (bo, tg, pg, g_ls, g_rb, g_sq, g_skv, g_so, g_lc, g_cq, g_ckv, g_co, g_lf, g_fi, g_fo) = outs
    if not sz.inside:
        at = lax.axis_index("fsdp") // sz.Y
        rows = jnp.zeros((ndp, Z, per, D), F32).at[:, at].set(g_fo.reshape(ndp, per, D))
        cols = jnp.zeros((D, ndp, Z, per), F32).at[:, :, at].set(g_fi.reshape(D, ndp, per))
        g_sq, g_skv, g_so, g_cq, g_ckv, g_co, g_fi, g_fo = (
            lax.psum_scatter(g, ("dp", "fsdp"), scatter_dimension=0, tiled=True)
            for g in (
                g_sq, g_skv, g_so, g_cq, g_ckv, g_co,
                cols.reshape(D, Z * D), rows.reshape(Z * D, D),
            )
        )
    outs = (bo, tg, pg, g_ls, g_rb, g_sq, g_skv, g_so, g_lc, g_cq, g_ckv, g_co, g_lf, g_fi, g_fo)
    if sz.inside:
        outs = pl.pallas_call(
            place_kernel,
            out_shape=tuple(shape(o.shape, o.dtype) for o in outs),
            in_specs=[hbm] * len(outs),
            out_specs=(hbm,) * len(outs),
            scratch_shapes=tuple(pltpu.VMEM(o.shape, o.dtype) for o in outs)
            + (pltpu.SemaphoreType.DMA((2, len(outs) - 1 + passages.shape[0])),),
            compiler_params=pltpu.CompilerParams(vmem_limit_bytes=63 * 2**20),
        )(*outs)
    (bo, tg, pg, g_ls, g_rb, g_sq, g_skv, g_so, g_lc, g_cq, g_ckv, g_co, g_lf, g_fi, g_fo) = outs
    return (
        bo[None], tg[None], pg, g_ls[0], g_rb[0], g_sq, g_skv, g_so,
        g_lc[0], g_cq, g_ckv, g_co, g_lf[0], g_fi, g_fo,
    )


def solution(mesh):
    both = ("dp", "fsdp")
    rows3, rows2, rows1 = P(both, None, None), P(both, None), P(both)
    placed = (
        rows3, P("dp", "fsdp", None), rows1, rows3, rows1, rows1, rows2, rows2, rows2,
        rows1, rows2, rows2, rows2, rows1, rows2, rows2,
    )
    outs = (
        rows3, rows3, P("dp", "fsdp", None), rows1, rows1, rows2, rows2, rows2,
        rows1, rows2, rows2, rows2, rows1, rows2, rows2,
    )

    def run(*args):
        targets, passages, self_q, ff_out = args[0], args[1], args[6], args[15]
        sz = Sizes(
            mesh.shape,
            targets.shape[2], passages.shape[1], targets.shape[1],
            self_q.shape[0], ff_out.shape[0],
            ff_out.shape[0] * mesh.shape["dp"] * mesh.shape["fsdp"] // ZDIM,
        )
        return per_device(sz, *args)

    return jax.shard_map(run, mesh=mesh, in_specs=placed, out_specs=outs, check_vma=False)
```

```python
import functools
import math

import jax
import jax.numpy as jnp
from jax import lax
from jax.experimental import pallas as pl
from jax.experimental.pallas import tpu as pltpu
from jax.sharding import PartitionSpec as P

HEADS = 12
DK = 64
BUCKETS = 32
QUAD = 4
WIDE = QUAD * DK
EPS = 1e-06
NEG = -1e30
HIGH = lax.Precision.HIGHEST
BF = jnp.bfloat16
F32 = jnp.float32
PIECES = 10
SQ, SK, SV, SO, CQ, CK, CV, CO, FI, FO = range(PIECES)
WIDE_PIECES = (CK, CV, FI, FO)
Y_SUMMED_FIRST = (CK,)
Z_AT_ONCE = (FI, SQ, SK)
FACTORS = {SQ: "h1", SK: "h1", SV: "h1", SO: "os", CQ: "h2", CO: "oc"}
ACTS = ("h1", "os", "h2", "oc")
Y_GATHERED_LAST = (SQ, SV, CQ)
ZDIM = 4


def up16(n):
    return (n + 15) // 16 * 16


def bucket_limits():
    limits = []
    for target_bucket in range(1, 16):
        distance = 16
        while int(math.log(distance / 16.0) / math.log(8.0) * 16.0) < target_bucket:
            distance = distance + 1
        limits.append(distance)
    return limits


def bucket_of(distance):
    larger = jnp.full_like(distance, 16)
    for limit_value in bucket_limits():
        larger = larger + (distance >= limit_value).astype(jnp.int32)
    return jnp.where(distance < 16, distance, jnp.minimum(larger, 31))


def iota(shape, axis):
    return lax.broadcasted_iota(jnp.int32, shape, axis)


def nn(a, b):
    return lax.dot_general(a, b, (((1,), (0,)), ((), ())), preferred_element_type=F32)


def nt(a, b):
    return lax.dot_general(a, b, (((1,), (1,)), ((), ())), preferred_element_type=F32)


def tn(a, b):
    return lax.dot_general(a, b, (((0,), (0,)), ((), ())), preferred_element_type=F32)


def nn_high(a, b):
    return lax.dot_general(
        a, b, (((1,), (0,)), ((), ())), preferred_element_type=F32, precision=HIGH
    )


def normed(v, gain):
    return v * lax.rsqrt(jnp.mean(v * v, axis=-1, keepdims=True) + EPS) * gain


def norm_back(v, gain, dy):
    s = lax.rsqrt(jnp.mean(v * v, axis=-1, keepdims=True) + EPS)
    dyg = dy * gain
    gain_grad = jnp.sum(dy * v * s, axis=0, keepdims=True)
    dv = s * dyg - v * (s * s * s) * jnp.mean(dyg * v, axis=-1, keepdims=True)
    return dv, gain_grad


def gelu_pair(u):
    cst = 0.7978845608028654
    cubic = 0.044715
    th = jnp.tanh(cst * (u + cubic * u * u * u))
    half = 0.5 * (1.0 + th)
    slope = half + 0.5 * u * (1.0 - th * th) * cst * (1.0 + 3.0 * cubic * u * u)
    return u * half, slope


class Buffers:
    pass


class Spot:
    def __init__(self, base, steps=()):
        self.base, self.steps = base, steps

    @property
    def at(self):
        return Steps(self)

    def ref(self):
        out = self.base
        for step in self.steps:
            out = out.at[step]
        return out

    def __getitem__(self, key):
        return self.ref()[key]

    def __setitem__(self, key, value):
        self.ref()[key] = value


class Steps:
    def __init__(self, spot):
        self.spot = spot

    def __getitem__(self, key):
        return Spot(self.spot.base, self.spot.steps + (key,))


class Sent:
    def __init__(self, make):
        self.make = make

    def wait_recv(self):
        self.make().wait_recv()

    def wait_send(self):
        self.make().wait_send()


class Sizes:
    def __init__(self, mesh_shape, width, rows, targets, shard, ff_shard, hidden):
        self.Z = ZDIM
        self.X = mesh_shape["dp"] // 2
        self.Y = mesh_shape["fsdp"] // self.Z
        self.D = width
        self.R = rows
        self.T = targets
        self.r = shard
        self.rb = up16(2 * shard)
        self.nh = width // 2
        self.inside = shard % 8 == 0
        self.rff = ff_shard
        self.hid = hidden
        assert ff_shard == self.Z * shard and hidden == width


def sems(sz):
    return 156 if sz.inside else 900


def layout(sz):
    X, Y, Z, D, T, R = sz.X, sz.Y, sz.Z, sz.D, sz.T, sz.R
    rb, nh, hid = sz.rb, sz.nh, sz.hid
    nw = len(WIDE_PIECES)
    NQ = HEADS // QUAD
    V = pltpu.VMEM
    sums = dict(
        rc=V((nw, X, Y, Z, rb, nh), BF),
        r1=V((nw, X - 1, Y, Z, rb, nh), BF),
        r1y=V((nw, Y - 1, X, Z, rb, nh), BF),
        r2x=V((nw, X - 1, Z, rb, nh), BF),
        r2=V((PIECES, Y - 1, Z, rb, nh), BF),
        rz=V((PIECES, 3, rb, nh), BF),
        act=V((len(ACTS), X, 2, T, D), BF),
        cot=V((PIECES, X, 2, T, D), BF),
    )
    return dict(
        **(sums if sz.inside else {}),
        gw=V((PIECES, 2, X, Y, Z, rb, nh), BF),
        w=V((PIECES, D, D), BF),
        fip=V((Z, rb, nh), BF),
        kvacc=V((D, 2 * D), F32),
        lift=V((max(Y * Z * sz.r, sz.rff) if sz.r % 8 else 8, D), F32),
        even=V((sz.r, D), F32),
        cell=V((rb, nh), F32),
        smb=V((2, X, Y, Z, 16, 128), BF),
        hot_gain=V((128, D), BF),
        hot_bias=V((128, HEADS * BUCKETS), BF),
        gain=V((16, D), F32),
        bias=V((NQ, WIDE, T), F32),
        spread=V((16, D), F32),
        spread2=V((32, D), BF),
        mask=V((WIDE, WIDE), BF),
        pas=V((Y * Z, R, D), BF),
        kv=V((Y * Z, R, 2 * D), BF),
        h1=V((T, D), BF),
        qs=V((T, D), BF),
        ks=V((T, D), BF),
        vs=V((T, D), BF),
        os=V((T, D), BF),
        ps=V((NQ, WIDE, T), F32),
        x1=V((T, D), F32),
        h2=V((T, D), BF),
        x2=V((T, D), F32),
        oc=V((T, D), BF),
        dx=V((T, D), F32),
        lse=V((16, T), F32),
        qc=V((Z, Y, T, D), BF),
        h3=V((Z, T, D), BF),
        g3=V((Z, T, D), BF),
        do=V((Z, Y, T, D), BF),
        dr=V((Z, Y, 16, 128), F32),
        po=V((Y, Z, T, D), BF),
        pst=V((Y, Z, 16, T), F32),
        ryo=V((Y - 1, Z, T, D), BF),
        ryst=V((Y - 1, Z, 16, T), F32),
        rzo=V((Z - 1, T, D), BF),
        rzst=V((Z - 1, 16, T), F32),
        py=V((Z, T, D), BF),
        rzy=V((Z - 1, T, D), BF),
        gl=V((Z * T, hid), BF),
        du=V((Z * T, hid), BF),
        sm=V((8, D), F32),
        rsm=V((1 + (X - 1) + (Y - 1) + (Z - 1), 8, D), F32),
        ssem=pltpu.SemaphoreType.DMA((sems(sz),)),
        rsem=pltpu.SemaphoreType.DMA((sems(sz),)),
        lsem=pltpu.SemaphoreType.DMA((1 + Y * Z,)),
    )


(
    DO_KVG1, DO_CK, DO_CV, DO_PASS, DO_ROWS1, DO_ROWS2,
    DO_ROWS3, DO_ROWS4, DO_DQ, DO_CQ, DO_SO, DO_SELFBACK,
    DO_SV, DO_SQ, DO_SK, DO_DH1, DO_BO, DO_SMALL,
) = range(PIECES, PIECES + 18)
TAIL = (
    FO, DO_KVG1, FO, DO_CK, DO_CV, FO, DO_PASS, CO,
    CK, CV, FI, DO_ROWS1, DO_DQ, DO_CQ, DO_SO, CO,
    DO_SELFBACK, DO_SV, DO_SQ, DO_SK, DO_DH1, DO_SMALL, FI, DO_BO,
    CV, CO, FI, CK, DO_SMALL, CQ, DO_ROWS2, CO,
    SO, CQ, CV, SV, SO, DO_ROWS3, SQ, SV,
    CV, SK, CQ, SQ, SK, CK, CV, SO,
    DO_SMALL, DO_ROWS4, CQ, SV, CK, SO, SQ, CQ,
    SV, SK, CK, DO_SMALL, SO, SQ, SV, SK,
    DO_SMALL, SQ, SK,
)

SPOTS = ("gw", "smb", "fip", "rc", "r1", "r1y", "r2", "r2x", "rz", "act", "cot")
INPUTS = (
    "tok", "pas_in", "len", "og", "ls", "rel", "sq", "skv", "so",
    "lc", "cq", "ckv", "co", "lf", "fi_in", "fo_in",
)
OUTPUTS = (
    "bo", "tg", "pg", "g_ls", "g_rb", "g_sq", "g_skv", "g_so",
    "g_lc", "g_cq", "g_ckv", "g_co", "g_lf", "g_fi", "g_fo",
)


def block_kernel(sz, names, *refs):
    m = Buffers()
    vars(m).update(zip(INPUTS + OUTPUTS + names, refs))
    for name in SPOTS:
        if hasattr(m, name):
            setattr(m, name, Spot(getattr(m, name)))
    X, Y, Z, D, T, R = sz.X, sz.Y, sz.Z, sz.D, sz.T, sz.R
    r, rb, nh, hid = sz.r, sz.rb, sz.nh, sz.hid
    NQ = HEADS // QUAD
    YZ = Y * Z
    dp = lax.axis_index("dp")
    fs = lax.axis_index("fsdp")
    x, c = dp // 2, dp % 2
    z, y = fs // Y, fs % Y
    oth = 1 - c

    ring_x = [(x + b) % X for b in range(X)]
    ring_y = [(y + b) % Y for b in range(Y)]
    ring_z = [(z + b) % Z for b in range(Z)]

    def around(ring, at, b):
        return ring[b] if isinstance(b, int) else (at + b) % len(ring)

    def xs(b):
        return around(ring_x, x, b)

    def ys(b):
        return around(ring_y, y, b)

    def zs(b):
        return around(ring_z, z, b)

    def any_dev(x_=None, c_=None, y_=None, z_=None):
        x_ = x if x_ is None else x_
        c_ = c if c_ is None else c_
        y_ = y if y_ is None else y_
        z_ = z if z_ is None else z_
        return (x_ * 2 + c_, z_ * Y + y_)

    near = {}

    def dev(x_=None, c_=None, y_=None, z_=None):
        key = (id(x_), id(c_), id(y_), id(z_))
        if key not in near:
            return any_dev(x_, c_, y_, z_)
        return near[key]

    none = id(None)
    near[(none, id(oth), none, none)] = any_dev(c_=oth)
    for v in ring_x:
        near[(id(v), none, none, none)] = any_dev(x_=v)
    for v in ring_y:
        near[(none, none, id(v), none)] = any_dev(y_=v)
    for v in ring_z:
        near[(none, none, none, id(v))] = any_dev(z_=v)

    z_near = z + 1 - 2 * (z % 2)
    z_far = ring_z[2]
    z_cross = (z_near + 2) % Z
    near[(none, none, none, id(z_near))] = any_dev(z_=z_near)

    ssem, rsem, lsem = m.ssem, m.rsem, m.lsem
    n_sems = sems(sz)
    used = [0]
    pending = []

    spare = []
    early = [False, []]

    def take(n=1):
        if n == 1 and spare:
            return spare.pop(0)
        if n == 0:
            return 0
        at = used[0]
        used[0] += n
        assert used[0] <= n_sems
        return at

    def copy_at(i, src, dst, to):
        src = src.ref() if isinstance(src, Spot) else src
        dst = dst.ref() if isinstance(dst, Spot) else dst
        return pltpu.make_async_remote_copy(
            src_ref=src, dst_ref=dst, send_sem=ssem.at[i], recv_sem=rsem.at[i],
            device_id=to, device_id_type=pl.DeviceIdType.MESH,
        )

    def send(src, dst, to):
        i = take()
        cp = Sent(lambda: copy_at(i, src, dst, to))
        cp.make().start()
        pending.append(cp)
        return cp

    def got(cps):
        for cp in cps:
            cp.wait_recv()

    def sent(cps):
        for cp in cps:
            cp.wait_send()
        pending[:] = [cp for cp in pending if all(cp is not done for done in cps)]

    def drain():
        sent(list(pending))

    partners = [dev(c_=oth)]
    partners += [dev(x_=xs(b)) for b in range(1, X)]
    partners += [dev(y_=ys(b)) for b in range(1, Y)]
    partners += [dev(z_=zs(b)) for b in range(1, Z)]
    bar = pltpu.get_barrier_semaphore()
    for p in partners:
        pl.semaphore_signal(bar, inc=1, device_id=p, device_id_type=pl.DeviceIdType.MESH)
    load_pas = pltpu.make_async_copy(m.pas_in, m.pas, lsem.at[0])
    load_pas.start()

    mask = m.mask
    mask[...] = (iota((WIDE, WIDE), 0) // DK == iota((WIDE, WIDE), 1) // DK).astype(F32).astype(BF)

    def stack4(v):
        return jnp.concatenate([v, v, v, v], axis=0) * mask[...]

    def fold4(u):
        lane = iota((T, WIDE), 1)
        out = u[0:T]
        for h in range(1, QUAD):
            out = jnp.where(lane >= h * DK, u[h * T : (h + 1) * T], out)
        return out

    def quad(t):
        return slice(t * WIDE, (t + 1) * WIDE)

    cell, lift = m.cell, m.lift

    def put_halves(dst, left, right, rows, total):
        if rows % 8 == 0 and 2 * rows == total:
            dst[...] = jnp.concatenate([left, right], axis=0).astype(BF)
        else:
            cols = left.shape[1]
            cell[0:total, 0:cols] = jnp.zeros((total, cols), F32)
            cell[0:rows, 0:cols] = left
            cell[rows : 2 * rows, 0:cols] = right
            dst[...] = cell[0:total, 0:cols].astype(BF)

    def get_halves(v, rows):
        if rows % 8 == 0:
            return v[0:rows], v[rows : 2 * rows]
        cell[0 : v.shape[0], 0 : v.shape[1]] = v
        return cell[0:rows, 0 : v.shape[1]], cell[rows : 2 * rows, 0 : v.shape[1]]

    gw, w, smb = m.gw, m.w, m.smb

    class Gather:

        def __init__(self, buf, y_first, feed="gather", first=False):
            self.buf, self.y_first, self.feed = buf, y_first, feed
            self.iz, self.iy, self.ix, self.ic = take(), take(Y - 1), take(X - 1), take()
            self.far = take() if feed == "gather" else 0
            if first:
                early[1].extend([self.iz, self.ic, self.far])
                early[1].extend(range(self.iy, self.iy + Y - 1))
                early[1].extend(range(self.ix, self.ix + X - 1))
            if feed == "exchange":
                own = buf.at[c, x, y, z]
                for a in range(1, Z):
                    copy_at(self.iz, m.fip.at[zs(a)], own, dev(z_=zs(a))).start()
                some = buf.at[c, x, y, 0 : Z - 1]
                pending.append(Sent(lambda: copy_at(self.iz, some, some, dev(z_=z_near))))

        def z_out(self):
            own = self.buf.at[c, x, y, z]
            copy_at(self.far, own, own, dev(z_=z_far)).start()
            copy_at(self.iz, own, own, dev(z_=z_near)).start()

        def pair_out(self):
            block = self.buf.at[c, x, y, z_far]
            far = Sent(lambda: copy_at(self.far, block, block, dev(z_=z_far)))
            far.wait_recv()
            copy_at(self.iz, block, block, dev(z_=z_near)).start()
            pair = self.buf.at[c, x, y, 0:2]
            pending.extend([far, Sent(lambda: copy_at(self.iz, pair, pair, dev(z_=z_near)))])
            self.over(self.y_first, block)
            self.over(not self.y_first, block)

        def over(self, is_y, block):
            if is_y:
                for b in range(1, Y):
                    copy_at(self.iy + b - 1, block, block, dev(y_=ys(b))).start()
            else:
                for b in range(1, X):
                    copy_at(self.ix + b - 1, block, block, dev(x_=xs(b))).start()

        def own_out(self):
            at = (c, x, y) if self.feed == "local" else (c, x, y, z)
            self.over(self.y_first, self.buf.at[at])
            self.over(not self.y_first, self.buf.at[at])

        def line_out(self):
            if self.feed == "local":
                return
            if self.feed == "gather":
                some = self.buf.at[c, x, y, 0:2]
                blocks = (z_near, z_cross)
            else:
                some = self.buf.at[c, x, y, 0 : Z - 1]
                blocks = ring_z[1:]
            copy_at(self.iz, some, some, dev(z_=z_near)).wait_recv()
            for k in blocks:
                block = self.buf.at[c, x, y, k]
                self.over(self.y_first, block)
                self.over(not self.y_first, block)

        def arrived(self, is_y, all_of_it):
            buf = self.buf
            if is_y:
                ref = buf.at[c, 0 : X, y] if all_of_it else buf.at[c, x, y]
                for b in range(1, Y):
                    yield Sent(
                        lambda b=b: copy_at(self.iy + b - 1, ref, ref, dev(y_=ys(b)))
                    )
            else:
                ref = buf.at[c, x] if all_of_it else buf.at[c, x, y]
                for b in range(1, X):
                    yield Sent(
                        lambda b=b: copy_at(self.ix + b - 1, ref, ref, dev(x_=xs(b)))
                    )

        def plane_out(self):
            second = list(self.arrived(self.y_first, False))
            got(second)
            pending.extend(second)
            if self.y_first:
                for b in range(1, Y):
                    self.over(False, self.buf.at[c, x, ys(b)])
            else:
                for b in range(1, X):
                    self.over(True, self.buf.at[c, xs(b), y])

        def core_out(self):
            third = list(self.arrived(not self.y_first, True))
            got(third)
            pending.extend(third)
            plane = self.buf.at[c]
            self.core = [Sent(lambda: copy_at(self.ic, plane, plane, dev(c_=oth)))]
            self.core[0].make().start()
            pending.extend(self.core)
            self.last = third + self.core

        def end(self):
            got(self.core)

    own_small = [jnp.zeros((16, 128), F32)]
    for at, key in enumerate(("ls", "lc", "lf", "rel")):
        v = getattr(m, key)[...].astype(F32)
        v = jnp.concatenate([v, jnp.zeros((1, 128 - v.shape[1]), F32)], axis=1)
        own_small[0] = jnp.where(iota((16, 128), 0) == at, v, own_small[0])
    smb[c, x, y, z] = own_small[0].astype(BF)
    moves = {}

    def begin(p, feed="gather"):
        moves[p] = Gather(gw.at[p], p not in Y_GATHERED_LAST, feed, p < CO)

    moves["small"] = Gather(smb, True, first=True)
    sources = (
        (m.sq, 0), (m.skv, 0), (m.skv, D), (m.so, 0),
        (m.cq, 0), (m.ckv, 0), (m.ckv, D), (m.co, 0),
    )

    def store(p):
        ref, off = sources[p]
        v = ref[:, off : off + D].astype(F32)
        put_halves(gw.at[p, c, x, y, z], v[:, 0:nh], v[:, nh:D], r, rb)

    for p in (SQ, SK, SV, SO, CQ, CK, CV, CO):
        store(p)
    pl.semaphore_wait(bar, len(partners))
    moves["small"].z_out()
    moves["small"].own_out()
    def pack(p):
        begin(p)
        if p in (SQ, SK, SV):
            moves[p].z_out()
        moves[p].own_out()

    for p in (SQ, SK, SV, SO, CQ, CK, CV, CO):
        pack(p)

    g3 = m.g3
    live = (iota((T, 1), 0) < m.len[...]).astype(F32)
    g3[z] = (live * m.og[...]).astype(BF)

    def line_start(base, buf):
        for a in range(1, Z):
            copy_at(base + a, buf.at[z], buf.at[z], dev(z_=zs(a))).start()

    def line_wait(base, buf):
        for a in range(1, Z):
            copy_at(base + a, buf.at[z], buf.at[z], dev(z_=zs(a))).wait_recv()

    def line_done(base, buf):
        for a in range(1, Z):
            copy_at(base + a, buf.at[z], buf.at[z], dev(z_=zs(a))).wait_send()

    def act_start(base, bufs):
        for n, buf in enumerate(bufs):
            for a in range(1, Z):
                copy_at(base + n * YZ + a, buf.at[z, y], buf.at[z, y], dev(z_=zs(a))).start()

    def act_forward(base, bufs, a):
        zi = zs(a)
        for n, buf in enumerate(bufs):
            for b in range(1, Y):
                copy_at(
                    base + n * YZ + b * Z + (Z - a) % Z, buf.at[zi, y], buf.at[zi, y], dev(y_=ys(b))
                ).start()

    def act_wait(base, bufs, t):
        at = base + (Y - t // Z) % Y * Z + (Z - t % Z) % Z
        for n, buf in enumerate(bufs):
            copy_at(at + n * YZ, buf.at[z, y], buf.at[z, y], dev(z_=zs(1))).wait_recv()

    def act_done(base, bufs):
        for n, buf in enumerate(bufs):
            for t in range(1, YZ):
                copy_at(base + n * YZ + t, buf.at[z, y], buf.at[z, y], dev(z_=zs(1))).wait_send()

    fip = m.fip
    ndp = 2 * X
    per = D // ndp

    def pack_ff():
        even = m.even
        for k in range(Z):
            for i in range(ndp):
                at = (i * Z + k) * per
                even[:, i * per : (i + 1) * per] = m.fi_in[:, at : at + per].astype(F32)
            put_halves(fip.at[k], even[:, 0:nh], even[:, nh:D], r, rb)
        vo = m.fo_in[...].astype(F32)
        if r % 8:
            lift[0 : Z * r, :] = vo
        for k in range(Z):
            part = lift[k * r : k * r + r, :] if r % 8 else vo[k * r : k * r + r]
            put_halves(gw.at[FO, c, x, y, k], part[:, 0:nh], part[:, nh:D], r, rb)
        gw[FI, c, x, y, z] = fip[z]

    g3_base = take(Z)

    spread = m.spread
    lane = iota((16, D), 1)
    row = iota((16, D), 0)
    spread[...] = ((lane >= row * DK) & (lane < row * DK + DK)).astype(F32)
    m.spread2[...] = jnp.concatenate([spread[...], spread[...]], axis=0).astype(BF)
    tlane = iota((T, 128), 1)
    rbs = HEADS * BUCKETS // (2 * X * YZ)

    def repeat_of(width, step):
        l0, n0 = iota((128, width), 0), iota((128, width), 1)

        def body(k, tot):
            return tot + ((n0 - l0 == k * step) & (l0 < step)).astype(F32)

        return lax.fori_loop(0, width // step, body, jnp.zeros((128, width), F32)).astype(BF)

    m.hot_gain[...] = repeat_of(D, r)
    m.hot_bias[...] = repeat_of(HEADS * BUCKETS, rbs)

    def unpack(p):
        group = 2 * Y * r

        if p == FO:
            group = YZ * r
            parts = [(yy, zz) for yy in range(Y) for zz in range(Z)]
        else:
            parts = [(yy, zz) for zz in range(2) for yy in range(Y)]
        per = YZ // len(parts)

        def body(g, carry):
            x_ = g // (2 * per)
            c_ = (g // per) % 2
            zp = 0 if per == 1 else g % per
            lefts, rights = [], []
            at = 0
            for yy, zz in parts:
                lo, hi = get_halves(gw[p, c_, x_, yy, 2 * zp + zz].astype(F32), r)
                if r % 8 == 0:
                    lefts.append(lo)
                    rights.append(hi)
                else:
                    lift[at : at + r, 0:nh] = lo
                    lift[at : at + r, nh:D] = hi
                at += r
            rows = pl.ds(pl.multiple_of(g * group, 16), group)
            if r % 8 == 0:
                w[p, rows, 0:nh] = jnp.concatenate(lefts, axis=0).astype(BF)
                w[p, rows, nh:D] = jnp.concatenate(rights, axis=0).astype(BF)
            else:
                w[p, rows, :] = lift[0:group, :].astype(BF)
            return carry

        lax.fori_loop(0, X * 2 * per, body, 0)

    gain = m.gain
    bias = m.bias
    def read_small():
        flat = HEADS * BUCKETS
        every = smb[...].reshape(2 * X * YZ * 16, 128)
        wide_g, wide_b = nn(every, m.hot_gain[...]), nn(every, m.hot_bias[...])
        ng, nb = iota((16, D), 1), iota((16, flat), 1)
        gains, tot = jnp.zeros((16, D), F32), jnp.zeros((16, flat), F32)
        at = 0
        for c_ in range(2):
            for x_ in range(X):
                for y_ in range(Y):
                    for z_ in range(Z):
                        k = (x_ * 2 + c_) * YZ + z_ * Y + y_
                        mine = (ng >= k * r) & (ng < k * r + r)
                        gains = jnp.where(mine, wide_g[at : at + 16], gains)
                        mine = (nb >= k * rbs) & (nb < k * rbs + rbs)
                        tot = jnp.where(mine, wide_b[at : at + 16], tot)
                        at += 16
        gain[...] = gains
        per = jnp.broadcast_to(tot[3:4, :], (16, flat))
        h0, n0 = iota((16, flat), 0), iota((16, flat), 1)
        per = jnp.where((n0 >= h0 * BUCKETS) & (n0 < h0 * BUCKETS + BUCKETS), per, 0.0)
        nb, mb = iota((flat, 128), 0), iota((flat, 128), 1)
        dist = jnp.where(mb == 0, 0, 128 - mb)
        hot = ((nb & (BUCKETS - 1)) == bucket_of(dist)).astype(F32).astype(BF)
        table = nn(per.astype(BF), hot)
        for h in range(HEADS):
            wide = jnp.broadcast_to(table[h : h + 1, :], (T, 128))
            rolled = pltpu.roll(wide, 0, 1, stride=1, stride_axis=0)
            bias[h // QUAD, (h % QUAD) * T : (h % QUAD + 1) * T, :] = rolled[:, 0:T]

    tok = m.tok

    def self_forward():
        m.h1[...] = normed(tok[...], gain[0:1, :]).astype(BF)
        h1 = m.h1[...]
        m.qs[...] = nn(h1, w[SQ]).astype(BF)
        m.ks[...] = nn(h1, w[SK]).astype(BF)
        m.vs[...] = nn(h1, w[SV]).astype(BF)
        allowed = iota((WIDE, T), 1) <= (iota((WIDE, T), 0) & (T - 1))
        for t in range(NQ):
            s = nt(stack4(m.qs[:, quad(t)]), m.ks[:, quad(t)]) + bias[t]
            s = jnp.where(allowed, s, NEG)
            e = jnp.exp(s - jnp.max(s, axis=1, keepdims=True))
            pr = e / jnp.sum(e, axis=1, keepdims=True)
            m.ps[t] = pr
            m.os[:, quad(t)] = fold4(nn(pr.astype(BF), m.vs[:, quad(t)])).astype(BF)

    qc = m.qc
    qc_base = take(YZ)

    def self_out():
        x1 = tok[...] + nn(m.os[...], w[SO])
        m.x1[...] = x1
        m.h2[...] = normed(x1, gain[1:2, :]).astype(BF)

    def cross_query():
        qc[z, y] = nn(m.h2[...], w[CQ]).astype(BF)
        act_start(qc_base, [qc])
        act_forward(qc_base, [qc], 0)

    kv, pas = m.kv, m.pas

    chunk = 2 if R % 16 == 0 else 1

    tall = 4 if R % 16 == 0 else 1

    def project(p, off, k0, k1):
        def part(k, carry):
            rows = pl.ds(k // NQ * tall, tall)
            at = k % NQ * WIDE
            cols = pl.ds(pl.multiple_of(at, WIDE), WIDE)
            v = nn(pas[rows].reshape(tall * R, D), w[p, :, cols])
            cols = pl.ds(pl.multiple_of(off + at, WIDE), WIDE)
            kv[rows, :, cols] = v.astype(BF).reshape(tall, R, WIDE)
            return carry

        lax.fori_loop(k0 * NQ, k1 * NQ, part, 0)

    def project_one(q, p, off):
        kv[q, :, off : off + D] = nn(pas[q], w[p]).astype(BF)

    held = Buffers()

    def after(p):
        unpack(p)
        if p == SQ:
            moves["small"].end()
            read_small()
        elif p == SV:
            self_forward()
        elif p == SO:
            self_out()
        elif p == CQ:
            cross_query()
        elif p == CK:
            load_pas.wait()
            project(CK, 0, 0, YZ // tall // 2)

    order = (SQ, SK, SV, SO, CQ, CK, CV, CO, FI, FO)

    def line_out(k):
        if k == 0:
            moves["small"].line_out()
        moves[order[k]].line_out()

    def pair_out(k):
        if k == 0:
            moves["small"].pair_out()
        moves[order[k]].pair_out()
        if k + 3 < 8:
            moves[order[k + 3]].z_out()

    def plane_out(k):
        if k == 0:
            moves["small"].plane_out()
        moves[order[k]].plane_out()

    def core_out(k):
        if k == 0:
            moves["small"].core_out()
        moves[order[k]].core_out()

    def arrive(k):
        moves[order[k]].end()
        after(order[k])

    def query_out(a):
        act_wait(qc_base, [qc], a)
        act_forward(qc_base, [qc], a)

    pair_out(0)
    pair_out(1)
    line_out(0)
    pack_ff()
    pair_out(2)
    line_out(1)
    plane_out(0)
    pair_out(3)
    line_out(2)
    plane_out(1)
    core_out(0)
    pair_out(4)
    line_out(3)
    begin(FI, "exchange")
    plane_out(2)
    arrive(0)
    core_out(1)
    pair_out(5)
    line_out(4)
    plane_out(3)
    arrive(1)
    core_out(2)
    pair_out(6)
    line_out(5)
    line_start(g3_base, g3)
    plane_out(4)
    arrive(2)
    core_out(3)
    line_out(6)
    plane_out(5)
    pair_out(7)
    arrive(3)
    core_out(4)
    arrive(4)
    plane_out(6)
    core_out(5)
    line_out(7)
    begin(FO, "local")
    moves[FI].own_out()
    moves[FO].own_out()
    line_out(8)
    line_out(9)
    arrive(5)
    core_out(6)
    query_out(1)
    project(CK, 0, YZ // tall // 2, YZ // tall)
    arrive(6)
    query_out(2)
    plane_out(7)
    query_out(3)

    po, pst, ryo, ryst, rzo, rzst = m.po, m.pst, m.ryo, m.ryst, m.rzo, m.rzst

    def rs_y_base():
        return take((Y - 1) * Z)

    def rs_y_send(base, src, dst, b, a):
        zi = zs(a)
        copy_at(base + (b - 1) * Z + a, src.at[b, zi], dst.at[b - 1, zi], dev(y_=ys(b))).start()

    def rs_y_wait(base, src, dst, b, a):
        copy_at(base + (b - 1) * Z + a, src.at[b, 0], dst.at[b - 1, 0], dev(y_=ys(1))).wait_recv()

    def rs_y_done(base, src, dst):
        for b in range(1, Y):
            for a in range(Z):
                copy_at(
                    base + (b - 1) * Z + a, src.at[b, 0], dst.at[b - 1, 0], dev(y_=ys(1))
                ).wait_send()

    yo_base, yst_base = rs_y_base(), rs_y_base()
    zo_base, zst_base = take(Z), take(Z)

    def attend(a, b):
        zi = zs(a)
        yi = ys(b)
        qi = zi * Y + yi
        st = jnp.zeros((T, 128), F32)
        for k in range(NQ):
            qb = stack4(qc[zi, yi, :, quad(k)])
            s = nt(qb, kv[qi, :, quad(k)])
            top = jnp.max(s, axis=1, keepdims=True)
            e = jnp.exp(s - top)
            tot = jnp.sum(e, axis=1, keepdims=True)
            u = nn(e.astype(BF), kv[qi, :, D + k * WIDE : D + (k + 1) * WIDE])
            po[b, zi, :, quad(k)] = fold4(u * (1.0 / tot)).astype(BF)
            lse = top + jnp.log(tot)
            for h in range(QUAD):
                st = jnp.where(tlane == k * QUAD + h, lse[h * T : (h + 1) * T], st)
        pst[b, zi] = st.T[0:16]

    def expand(st):
        return lax.dot_general(
            st, spread[...], (((0,), (0,)), ((), ())), preferred_element_type=F32, precision=HIGH
        )

    def expand_low(v):
        hi = v.astype(BF)
        lo = (v - hi.astype(F32)).astype(BF)
        both = jnp.concatenate([hi, lo], axis=0)
        ones = m.spread2[...]
        return tn(both, ones)

    def merge(parts):
        top = parts[0][1]
        for _, st in parts[1:]:
            top = jnp.maximum(top, st)
        ws = [jnp.exp(st - top) for _, st in parts]
        tot = ws[0]
        for v in ws[1:]:
            tot = tot + v
        out = jnp.zeros((T, D), F32)
        for (o, _), v in zip(parts, ws):
            out = out + expand_low(v / tot) * o.astype(F32)
        return out, top + jnp.log(tot)

    def z_send(base, src, dst, a):
        zi = zs(a)
        copy_at(base + a, src.at[0, zi], dst.at[a - 1], dev(z_=zi)).start()

    def z_each(base, src, dst, wait):
        for a in range(1, Z):
            cp = copy_at(base + a, src.at[0, 0], dst.at[a - 1], dev(z_=zs(a)))
            if wait == "recv":
                cp.wait_recv()
            else:
                cp.wait_send()

    def pass_on(a):
        zi = zs(a)
        for b in range(1, Y):
            rs_y_wait(yo_base, po, ryo, b, a)
            rs_y_wait(yst_base, pst, ryst, b, a)
        o, st = merge(
            [(po[0, zi], pst[0, zi])] + [(ryo[b - 1, zi], ryst[b - 1, zi]) for b in range(1, Y)]
        )
        po[0, zi] = o.astype(BF)
        pst[0, zi] = st
        z_send(zo_base, po, rzo, a)
        z_send(zst_base, pst, rzst, a)

    def attend_own(a):
        project_one(zs(a) * Y + y, CV, D)
        attend(a, 0)

    def attend_others(a):
        def body(b, carry):
            project_one(zs(a) * Y + ys(b), CV, D)
            act_wait(qc_base, [qc], b * Z + a)
            attend(a, b)
            rs_y_send(yo_base, po, ryo, b, a)
            rs_y_send(yst_base, pst, ryst, b, a)
            return carry

        lax.fori_loop(1, Y, body, 0)

    def attend_step(k, carry):
        attend_others((k + 1) % Z)
        attend_own(k)
        pass_on(k)

        @pl.when(k == 2)
        def _():
            core_out(7)

        return carry

    attend_own(0)
    attend_others(1)
    plane_out(8)
    plane_out(9)
    lax.fori_loop(1, Z, attend_step, 0)
    arrive(7)
    for b in range(1, Y):
        rs_y_wait(yo_base, po, ryo, b, 0)
        rs_y_wait(yst_base, pst, ryst, b, 0)
    z_each(zo_base, po, rzo, "recv")
    z_each(zst_base, pst, rzst, "recv")
    o, lse = merge(
        [(po[0, z], pst[0, z])]
        + [(ryo[b - 1, z], ryst[b - 1, z]) for b in range(1, Y)]
        + [(rzo[a - 1], rzst[a - 1]) for a in range(1, Z)]
    )
    m.oc[...] = o.astype(BF)
    m.lse[...] = lse
    x2 = m.x1[...] + nn(m.oc[...], w[CO])
    m.x2[...] = x2
    h3 = m.h3
    h3[z] = normed(x2, gain[2:3, :]).astype(BF)
    h3_base = take(Z)
    line_start(h3_base, h3)

    rc, r1, r1y, r2, r2x, rz, act, cot = (getattr(m, k, None) for k in SPOTS[3:])

    def share(buf):
        own = buf.at[x, c]
        near_c = send(own, own, dev(c_=oth))
        return [send(own, own, dev(x_=xs(b))) for b in range(1, X)], near_c

    def share_on(buf, cps):
        far, near_c = cps
        got(far)
        out = [near_c]
        for b in range(1, X):
            block = buf.at[xs(b), c]
            out.append(send(block, block, dev(c_=oth)))
        return out

    def share_acts():
        if sz.inside:
            for n, name in enumerate(ACTS):
                act[n, x, c] = getattr(m, name)[...]
            held.acts = [share(act.at[n]) for n in range(len(ACTS))]

    def share_acts_on():
        if sz.inside:
            held.acts = [share_on(act.at[n], cps) for n, cps in enumerate(held.acts)]

    def share_acts_end():
        if sz.inside:
            for cps in held.acts:
                got(cps)
    drain()
    share_acts()

    core_out(8)
    core_out(9)
    arrive(8)
    line_wait(g3_base, g3)
    arrive(9)
    gb = g3[...].reshape(Z * T, D)
    m.kvacc.at[0 : Z * T, 0:hid][...] = nt(gb, w[FO])
    act_done(qc_base, [qc])
    rs_y_done(yo_base, po, ryo)
    rs_y_done(yst_base, pst, ryst)
    z_each(zo_base, po, rzo, "send")
    z_each(zst_base, pst, rzst, "send")
    py, rzy = Spot(m.py), Spot(m.rzy)
    gl, du = m.gl, m.du
    line_wait(h3_base, h3)
    lifted, slope = gelu_pair(nn(h3[...].reshape(Z * T, D), w[FI]))
    du[...] = (m.kvacc.at[0 : Z * T, 0:hid][...] * slope).astype(BF)
    gl[...] = lifted.astype(BF)
    po[0] = nt(du[...], w[FI]).astype(BF).reshape(Z, T, D)

    def rs_z(part, rzb):
        return [send(part.at[zs(a)], rzb.at[a - 1], dev(z_=zs(a))) for a in range(1, Z)]

    def rs_total(part, rzb):
        tot = part[z].astype(F32)
        for a in range(1, Z):
            tot = tot + rzb[a - 1].astype(F32)
        return tot

    zh = rs_z(po.at[0], rzo)
    py[...] = nn(gl[...], w[FO]).astype(BF).reshape(Z, T, D)
    line_done(h3_base, h3)
    line_done(g3_base, g3)

    acc = m.kvacc.at[:, 0:D]

    def add_to(dst, src):
        dst[...] = (dst[...].astype(F32) + src[...].astype(F32)).astype(BF)

    def add_blocks(rows, dst, src):
        def body(i, carry):
            add_to(dst(i // Z, i % Z), src(i // Z, i % Z))
            return carry

        lax.fori_loop(0, rows * Z, body, 0)

    def pack_grad(p, acc, col):
        group = YZ * r
        if not sz.inside:
            name, off = targets[p]
            out = getattr(m, name) if p in (FI, FO) else getattr(m, name).at[:, off : off + D]
            cp = pltpu.make_async_copy(acc.at[:, col : col + D], out, lsem.at[0])
            cp.start()
            cp.wait()
            return None

        def body(k, carry):
            x_ = k // 2
            c_ = k % 2
            for z_ in range(Z):
                for y_ in range(Y):
                    at = (y_ * Z + z_) * r if p == FO else (z_ * Y + y_) * r
                    rows = pl.ds(pl.multiple_of(k * group + at, 8), r)
                    left, right = acc[rows, col : col + nh], acc[rows, col + nh : col + D]
                    put_halves(gw.at[p, c_, x_, y_, z_], left, right, r, rb)
            return carry

        lax.fori_loop(0, 2 * X, body, 0)
        return [send(gw.at[p, oth], rc.at[WIDE_PIECES.index(p)], dev(c_=oth))]

    def rs_first(p, cps):
        got(cps)
        n = WIDE_PIECES.index(p)
        add_blocks(
            X * Y,
            lambda k, z_: gw.at[p, c, k // Y, k % Y, z_],
            lambda k, z_: rc.at[n, k // Y, k % Y, z_],
        )
        if p in Y_SUMMED_FIRST:
            return [
                send(gw.at[p, c, :, ys(b)], r1y.at[n, b - 1], dev(y_=ys(b))) for b in range(1, Y)
            ]
        return [send(gw.at[p, c, xs(b)], r1.at[n, b - 1], dev(x_=xs(b))) for b in range(1, X)]

    def to_y(p):
        return [send(gw.at[p, c, x, ys(b)], r2.at[p, b - 1], dev(y_=ys(b))) for b in range(1, Y)]

    def rs_second(p, cps):
        got(cps)
        n = WIDE_PIECES.index(p)
        if p in Y_SUMMED_FIRST:
            for b in range(1, Y):
                add_blocks(
                    X,
                    lambda k, z_: gw.at[p, c, k, y, z_],
                    lambda k, z_: r1y.at[n, b - 1, k, z_],
                )
            return [
                send(gw.at[p, c, xs(b), y], r2x.at[n, b - 1], dev(x_=xs(b))) for b in range(1, X)
            ]
        for b in range(1, X):
            add_blocks(
                Y,
                lambda k, z_: gw.at[p, c, x, k, z_],
                lambda k, z_: r1.at[n, b - 1, k, z_],
            )
        return to_y(p)

    def factor_on(p, cps):
        return share_on(cot.at[p], cps)

    def factor_product(p, cps):
        got(cps)
        group = YZ * r
        first = (x * 2 + c) * group
        lanes = first // 128 * 128
        shift = pl.multiple_of(first - lanes, 8)
        lhs = act[ACTS.index(FACTORS[p]), :, :, :, pl.ds(pl.multiple_of(lanes, 128), WIDE)]
        acc[0:WIDE, :] = tn(lhs.reshape(2 * X * T, WIDE), cot[p].reshape(2 * X * T, D))

        def body(i, carry):
            y_ = i % Y
            z_ = i // Y
            rows = pl.ds(pl.multiple_of(shift + i * r, 8), r)
            put_halves(gw.at[p, c, x, y_, z_], acc[rows, 0:nh], acc[rows, nh:D], r, rb)
            return carry

        lax.fori_loop(0, YZ, body, 0)
        return to_y(p)

    def rs_third(p, cps):
        got(cps)
        second = (
            [r2x.at[WIDE_PIECES.index(p), b - 1] for b in range(1, X)]
            if p in Y_SUMMED_FIRST
            else [r2.at[p, b - 1] for b in range(1, Y)]
        )
        for part in second:
            add_blocks(1, lambda k, z_: gw.at[p, c, x, y, z_], lambda k, z_: part.at[z_])
        if p == FO:
            return []
        if p in Z_AT_ONCE:
            return [
                send(gw.at[p, c, x, y, zs(a)], rz.at[p, a - 1], dev(z_=zs(a)))
                for a in range(1, Z)
            ]
        return [
            send(gw.at[p, c, x, y, k], rz.at[p, n], dev(z_=z_near))
            for n, k in enumerate((z_near, z_cross))
        ]

    def rs_fourth(p, cps):
        got(cps)
        if p == FO or p in Z_AT_ONCE:
            return []
        add_to(gw.at[p, c, x, y, z_far], rz.at[p, 1])
        return [send(gw.at[p, c, x, y, z_far], rz.at[p, 2], dev(z_=z_far))]

    targets = {
        SQ: ("g_sq", 0), SK: ("g_skv", 0), SV: ("g_skv", D), SO: ("g_so", 0),
        CQ: ("g_cq", 0), CK: ("g_ckv", 0), CV: ("g_ckv", D), CO: ("g_co", 0),
        FI: ("g_fi", 0), FO: ("g_fo", 0),
    }

    def rs_last(p, cps):
        got(cps)
        name, off = targets[p]
        if p in (FI, FO):
            for a in range(Z):
                k = a if p == FO else zs((Z - a) % Z)
                if p == FO:
                    v = gw[p, c, x, y, a]
                else:
                    v = rz[p, a - 1] if a else gw[p, c, x, y, z]
                lo, hi = get_halves(v.astype(F32), r)
                if p == FI:
                    m.kvacc[pl.ds(pl.multiple_of(k * r, 8), r), 0:nh] = lo
                    m.kvacc[pl.ds(pl.multiple_of(k * r, 8), r), nh:D] = hi
                else:
                    getattr(m, name)[k * r : k * r + r, 0:nh] = lo
                    getattr(m, name)[k * r : k * r + r, nh:D] = hi
            if p == FI:
                for k in range(Z):
                    for i in range(ndp):
                        at = (i * Z + k) * per
                        getattr(m, name)[:, at : at + per] = m.kvacc[k * r : k * r + r, i * per : (i + 1) * per]
            return None
        v = gw[p, c, x, y, z].astype(F32) + rz[p, 0].astype(F32) + rz[p, 2].astype(F32)
        if p in Z_AT_ONCE:
            v = v + rz[p, 1].astype(F32)
        lo, hi = get_halves(v, r)
        getattr(m, name)[:, off : off + nh] = lo
        getattr(m, name)[:, off + nh : off + D] = hi

    wide_stages = (rs_first, rs_second, rs_third, rs_fourth, rs_last) if sz.inside else ()
    factor_stages = (factor_on, factor_product, rs_third, rs_fourth, rs_last) if sz.inside else ()

    def stages_of(p):
        return factor_stages if p in FACTORS else wide_stages

    moving = {}

    def grad_of(p, lhs, rhs):
        if sz.inside and p in FACTORS:
            cot[p, x, c] = rhs[...]
            moving[p] = (0, share(cot.at[p]))
            return

        def part(k, carry):
            cols = pl.ds(pl.multiple_of(k * WIDE, WIDE), WIDE)
            left = lhs[:, :, cols].reshape(Z * T, WIDE) if len(lhs.shape) == 3 else lhs[:, cols]
            acc[cols, :] = tn(left, rhs[...])
            return carry

        lax.fori_loop(0, NQ, part, 0)
        grad_out(p)

    def grad_out(p, src=None, col=0):
        moving[p] = (0, pack_grad(p, acc if src is None else src, col))

    def push(p):
        k, cps = moving[p]
        if k < len(stages_of(p)):
            moving[p] = (k + 1, stages_of(p)[k](p, cps))

    def push_all(ps):
        for p in ps:
            push(p)

    sent(moves[FI].last + moves[FO].last)
    spare.extend(early[1])
    grad_of(FO, gl, gb)
    grad_of(FI, h3, du)
    push_all([FO, FI])
    share_acts_on()
    sm = m.sm
    sm[...] = jnp.zeros_like(sm)
    do, dr = m.do, m.dr
    do_base = take(2 * YZ)
    pick = iota((T, D), 0) == (iota((T, D), 1) & (T - 1))

    def as_rows(st):
        v = jnp.sum(jnp.where(pick, expand(st), 0.0), axis=0, keepdims=True)
        parts = [v[:, k * 128 : (k + 1) * 128] for k in range(D // 128)]
        return jnp.concatenate(parts + [jnp.zeros((8 - D // 128, 128), F32)], axis=0)

    dr[z, y, 0:8] = as_rows(m.lse[...])
    if sz.inside:
        m.kvacc[...] = jnp.zeros_like(m.kvacc)
    got(zh)
    dh3 = rs_total(po.at[0], rzo)
    dv, gg = norm_back(m.x2[...], gain[2:3, :], dh3)
    sm[2:3, :] = gg
    dx2 = live * m.og[...] + dv
    m.dx[...] = dx2
    dx2l = dx2.astype(BF)
    doc = nt(dx2l, w[CO]).astype(BF)
    do[z, y] = doc
    act_start(do_base, [do])
    act_forward(do_base, [do], 0)
    prod = doc.astype(F32) * m.oc[...].astype(F32)
    delta = lax.dot_general(
        spread[...], prod, (((1,), (1,)), ((), ())), preferred_element_type=F32, precision=HIGH
    )
    dr[z, y, 8:16] = as_rows(delta)
    act_start(do_base + YZ, [dr])
    act_forward(do_base + YZ, [dr], 0)
    grad_of(CO, m.oc, dx2l)

    sent(zh)
    yq_base = rs_y_base()

    def row_of(ref, k):
        return jnp.concatenate([ref[2 * k : 2 * k + 1, :], ref[2 * k + 1 : 2 * k + 2, :]], axis=1)

    zq_base = take(Z)

    def pass_back(a):
        zi = zs(a)
        for b in range(1, Y):
            rs_y_wait(yq_base, po, ryo, b, a)
        tot = po[0, zi].astype(F32)
        for b in range(1, Y):
            tot = tot + ryo[b - 1, zi].astype(F32)
        po[0, zi] = tot.astype(BF)
        z_send(zq_base, po, rzo, a)

    def attend_back(a, b):
        zi = zs(a)
        yi = ys(b)
        qi = zi * Y + yi

        lse_rows = dr[zi, yi, 0:8]
        delta_rows = dr[zi, yi, 8:16]
        for k in range(NQ):
            qb = stack4(qc[zi, yi, :, quad(k)])
            db = stack4(do[zi, yi, :, quad(k)])
            kt = kv[qi, :, quad(k)]
            vt = kv[qi, :, D + k * WIDE : D + (k + 1) * WIDE]
            pt = jnp.exp(nt(kt, qb) - row_of(lse_rows, k))
            ds = (pt * (nt(vt, db) - row_of(delta_rows, k))).astype(BF)
            po[b, zi, :, quad(k)] = fold4(tn(ds, kt)).astype(BF)
            kv[qi, :, quad(k)] = nn(ds, qb).astype(BF)
            kv[qi, :, D + k * WIDE : D + (k + 1) * WIDE] = nn(pt.astype(BF), db).astype(BF)


    kvacc = m.kvacc

    def kv_grad(q):
        def part(k, carry):
            cols = pl.ds(pl.multiple_of(k * WIDE, WIDE), WIDE)
            kvacc[cols, :] += tn(pas[q, :, cols], kv[q])
            return carry

        lax.fori_loop(0, NQ, part, 0)

    def kv_grads(t0, t1):
        def body(t, carry):
            kv_grad(zs(t // Y) * Y + ys(t % Y))
            return carry

        lax.fori_loop(t0, t1, body, 0)

    def back_own(a):
        attend_back(a, 0)

    def back_others(a):
        def body(b, carry):
            act_wait(do_base, [do, dr], b * Z + a)
            attend_back(a, b)
            rs_y_send(yq_base, po, ryo, b, a)
            return carry

        lax.fori_loop(1, Y, body, 0)

    def back_step(k, carry):
        act_wait(do_base, [do, dr], k + 1)
        act_forward(do_base, [do, dr], k + 1)
        back_others(k)

        @pl.when(k < Z - 2)
        def _():
            kv_grads(k * Y + 1, k * Y + Y)

        @pl.when(k == 1)
        def _():
            push(CO)
            share_acts_end()
            held.zy = rs_z(py, rzy)

        @pl.when(k == Z - 2)
        def _():
            push(FI)

        back_own(k + 1)

        @pl.when(k < Z - 2)
        def _():
            kv_grads(k * Y + Y, k * Y + Y + 1)

        return carry

    if not sz.inside:
        kvacc[...] = jnp.zeros_like(kvacc)
    back_own(0)
    kv_grad(z * Y + y)
    push(FO)
    lax.fori_loop(0, Z - 1, back_step, 0)
    back_others(Z - 1)
    def row_grads(k0, k1):
        def whole(k, carry):
            pas[k] = (nt(kv[k, :, 0:D], w[CK]) + nt(kv[k, :, D : 2 * D], w[CV])).astype(BF)
            pltpu.make_async_copy(pas.at[k], m.pg.at[k], lsem.at[1 + k]).start()
            return carry

        def part(k, carry):
            rows = pl.ds(k // NQ * chunk, chunk)
            cols = pl.ds(pl.multiple_of(k % NQ * WIDE, WIDE), WIDE)
            v = nt(kv[rows, :, 0:D].reshape(chunk * R, D), w[CK, cols, :])
            v = v + nt(kv[rows, :, D : 2 * D].reshape(chunk * R, D), w[CV, cols, :])
            pas[rows, :, cols] = v.astype(BF).reshape(chunk, R, WIDE)

            @pl.when(k % NQ == NQ - 1)
            def _():
                for q in range(chunk):
                    at = k // NQ * chunk + q
                    pltpu.make_async_copy(pas.at[at], m.pg.at[at], lsem.at[1 + at]).start()

            return carry

        if chunk == 1:
            lax.fori_loop(k0, k1, whole, 0)
        else:
            lax.fori_loop(k0 * NQ, k1 * NQ, part, 0)

    part = YZ // chunk // 4

    def take_dq():
        for b in range(1, Y):
            rs_y_wait(yq_base, po, ryo, b, 0)
        z_each(zq_base, po, rzo, "recv")
        dqc = rs_total(po.at[0], rzo)
        for b in range(1, Y):
            dqc = dqc + ryo[b - 1, z].astype(F32)
        held.dqc = dqc.astype(BF)
        dh2 = nt(held.dqc, w[CQ])
        dv, gg = norm_back(m.x1[...], gain[1:2, :], dh2)
        sm[1:2, :] = gg
        dx1 = m.dx[...] + dv
        m.dx[...] = dx1
        held.dx1l = dx1.astype(BF)

    def self_back():
        m.oc[...] = nt(held.dx1l, w[SO]).astype(BF)
        grads = [[], [], []]
        held.tail = []
        back = (iota((T, 128), 1) == T - 1 - iota((T, 128), 0)).astype(F32).astype(BF)
        for t in range(NQ):
            db = stack4(m.oc[:, quad(t)])
            qb = stack4(m.qs[:, quad(t)])
            pr = m.ps[t]
            dps = nt(db, m.vs[:, quad(t)])
            dss = (pr * (dps - jnp.sum(pr * dps, axis=1, keepdims=True))).astype(BF)
            grads[0].append(fold4(nn(dss, m.ks[:, quad(t)])).astype(BF))
            grads[1].append(tn(dss, qb).astype(BF))
            grads[2].append(tn(pr.astype(BF), db).astype(BF))
            turned = nn(dss, back)
            for h in range(QUAD):
                part = pltpu.roll(turned[h * T : (h + 1) * T], 0, 1, stride=1, stride_axis=0)
                held.tail.append(jnp.sum(part, axis=0, keepdims=True))
        held.dqs, held.dks, held.dvs = (jnp.concatenate(g, axis=1) for g in grads)

    def token_grad():
        dh1 = nt(held.dqs, w[SQ]) + nt(held.dks, w[SK]) + nt(held.dvs, w[SV])
        dv, gg = norm_back(tok[...], gain[0:1, :], dh1)
        sm[0:1, :] = gg
        m.tg[...] = m.dx[...] + dv
        flat = HEADS * BUCKETS
        diag = jnp.concatenate(held.tail + [jnp.zeros((16 - HEADS, 128), F32)], axis=0)
        mi, bi = iota((128, 128), 0), iota((128, 128), 1)
        hot = ((mi >= T - 1) & (bucket_of(mi - (T - 1)) == bi) & (bi < BUCKETS)).astype(F32)
        table = nn_high(diag, hot)
        bb, nb = iota((128, flat), 0), iota((128, flat), 1)
        wide = nn_high(table, ((nb & (BUCKETS - 1)) == bb).astype(F32))
        h0, n0 = iota((16, flat), 0), iota((16, flat), 1)
        own = (n0 >= h0 * BUCKETS) & (n0 < h0 * BUCKETS + BUCKETS)
        sm[3:4, 0:flat] = jnp.sum(jnp.where(own, wide, 0.0), axis=0, keepdims=True)

    rsm = m.rsm
    slot = [0]

    def small_to(devs):
        held.small = []
        for to in devs:
            held.small.append((slot[0], send(sm, rsm.at[slot[0]], to)))
            slot[0] += 1

    def small_got():
        got([cp for _, cp in held.small])
        sent([cp for _, cp in held.small])
        for k, _ in held.small:
            sm[...] += rsm[k]

    def small_step(k):
        if k:
            small_got()
        if k < 4:
            small_to(
                (
                    [dev(c_=oth)],
                    [dev(x_=xs(b)) for b in range(1, X)],
                    [dev(y_=ys(b)) for b in range(1, Y)],
                    [dev(z_=zs(a)) for a in range(1, Z)],
                )[k]
            )

    def block_out():
        got(held.zy)
        m.bo[...] = live * (m.x2[...] + rs_total(py, rzy))

    steps = {
        DO_CK: lambda: grad_out(CK, kvacc, 0),
        DO_CV: lambda: grad_out(CV, kvacc, D),
        DO_KVG1: lambda: kv_grads((Z - 2) * Y + 1, YZ),
        DO_PASS: lambda: [pass_back(a) for a in range(1, Z)],
        DO_ROWS1: lambda: row_grads(0, part),
        DO_ROWS2: lambda: row_grads(part, 2 * part),
        DO_ROWS3: lambda: row_grads(2 * part, 3 * part),
        DO_ROWS4: lambda: row_grads(3 * part, YZ // chunk),
        DO_DQ: take_dq,
        DO_CQ: lambda: grad_of(CQ, m.h2, held.dqc),
        DO_SO: lambda: grad_of(SO, m.os, held.dx1l),
        DO_SELFBACK: self_back,
        DO_SV: lambda: grad_of(SV, m.h1, held.dvs),
        DO_SQ: lambda: grad_of(SQ, m.h1, held.dqs),
        DO_SK: lambda: grad_of(SK, m.h1, held.dks),
        DO_DH1: token_grad,
        DO_BO: block_out,
    }
    small_at = [0]

    def run(name):
        if name == DO_SMALL:
            small_step(small_at[0])
            small_at[0] += 1
        elif name < PIECES:
            push(name)
        else:
            steps[name]()

    for name in TAIL:
        run(name)
    assert all(k == len(stages_of(p)) for p, (k, _) in moving.items()), moving
    assert small_at[0] == 5
    me = dp * YZ + fs
    nd, ld = iota((D, 128), 0), iota((D, 128), 1)
    mine = nn_high(sm[...], ((nd == me * r + ld) & (ld < r)).astype(F32))
    mine_b = nn_high(sm[...], ((nd == me * rbs + ld) & (ld < rbs)).astype(F32))
    m.g_ls[...] = mine[0:1, 0:r]
    m.g_lc[...] = mine[1:2, 0:r]
    m.g_lf[...] = mine[2:3, 0:r]
    m.g_rb[...] = mine_b[3:4, 0:rbs]

    act_done(do_base, [do, dr])
    rs_y_done(yq_base, po, ryo)
    z_each(zq_base, po, rzo, "send")
    drain()

    def pg_wait(q, carry):
        pltpu.make_async_copy(pas.at[q], m.pg.at[q], lsem.at[1 + q]).wait()
        return carry

    lax.fori_loop(0, YZ, pg_wait, 0)


def place_kernel(*refs):
    n = len(OUTPUTS)
    given, put, held, sem = refs[:n], refs[n : 2 * n], refs[2 * n : 3 * n], refs[3 * n]
    loads, stores = [], []
    for k in range(n):
        parts = [slice(None)] if len(given[k].shape) < 3 else range(given[k].shape[0])
        for part in parts:
            at = len(loads)
            loads.append(pltpu.make_async_copy(given[k].at[part], held[k].at[part], sem.at[0, at]))
            stores.append(pltpu.make_async_copy(held[k].at[part], put[k].at[part], sem.at[1, at]))
    for cp in loads:
        cp.start()
    for load, store in zip(loads, stores):
        load.wait()
        store.start()
    for cp in stores:
        cp.wait()


def per_device(
    sz,
    targets, passages, tgt_len, out_grad, ln_self, rel_bias, self_q, self_kv, self_out,
    ln_cross, cross_q, cross_kv, cross_out, ln_ff, ff_in, ff_out,
):
    T, D, r, Z = sz.T, sz.D, sz.r, sz.Z
    ndp = 2 * sz.X
    per = sz.Y * sz.rff
    scratch = layout(sz)
    names = tuple(scratch)
    gr = r if sz.inside else D
    vm = pl.BlockSpec(memory_space=pltpu.VMEM)
    hbm = pl.BlockSpec(memory_space=pltpu.HBM)
    shape = jax.ShapeDtypeStruct
    rbs = rel_bias.shape[0]
    out_shape = (
        shape((T, D), F32), shape((T, D), F32), shape(passages.shape, BF),
        shape((1, r), F32), shape((1, rbs), F32),
        shape((gr, D), F32), shape((gr, 2 * D), F32), shape((gr, D), F32),
        shape((1, r), F32), shape((gr, D), F32), shape((gr, 2 * D), F32), shape((gr, D), F32),
        shape((1, r), F32),
        shape((r, Z * D) if sz.inside else (D, D), F32),
        shape((Z * r, D) if sz.inside else (D, D), F32),
    )
    weight_outs = ("g_sq", "g_skv", "g_so", "g_cq", "g_ckv", "g_co", "g_fi", "g_fo")
    apart = ("pg",) if sz.inside else ("pg",) + weight_outs
    outs = pl.pallas_call(
        functools.partial(block_kernel, sz, names),
        out_shape=out_shape,
        in_specs=[hbm if n == "pas_in" else vm for n in INPUTS],
        out_specs=tuple(hbm if n in apart else vm for n in OUTPUTS),
        scratch_shapes=tuple(scratch.values()),
        compiler_params=pltpu.CompilerParams(
            collective_id=0, has_side_effects=True, vmem_limit_bytes=63 * 2**20
        ),
        cost_estimate=pl.CostEstimate(
            flops=20 * 10**9, bytes_accessed=2 * 10**7, transcendentals=4 * 10**6
        ),
    )(
        targets[0], passages, tgt_len[None], out_grad[0], ln_self[None], rel_bias[None],
        self_q, self_kv, self_out, ln_cross[None], cross_q, cross_kv, cross_out,
        ln_ff[None], ff_in, ff_out,
    )
    (bo, tg, pg, g_ls, g_rb, g_sq, g_skv, g_so, g_lc, g_cq, g_ckv, g_co, g_lf, g_fi, g_fo) = outs
    if not sz.inside:
        at = lax.axis_index("fsdp") // sz.Y
        rows = jnp.zeros((ndp, Z, per, D), F32).at[:, at].set(g_fo.reshape(ndp, per, D))
        cols = jnp.zeros((D, ndp, Z, per), F32).at[:, :, at].set(g_fi.reshape(D, ndp, per))
        g_sq, g_skv, g_so, g_cq, g_ckv, g_co, g_fi, g_fo = (
            lax.psum_scatter(g, ("dp", "fsdp"), scatter_dimension=0, tiled=True)
            for g in (
                g_sq, g_skv, g_so, g_cq, g_ckv, g_co,
                cols.reshape(D, Z * D), rows.reshape(Z * D, D),
            )
        )
    outs = (bo, tg, pg, g_ls, g_rb, g_sq, g_skv, g_so, g_lc, g_cq, g_ckv, g_co, g_lf, g_fi, g_fo)
    if sz.inside:
        outs = pl.pallas_call(
            place_kernel,
            out_shape=tuple(shape(o.shape, o.dtype) for o in outs),
            in_specs=[hbm] * len(outs),
            out_specs=(hbm,) * len(outs),
            scratch_shapes=tuple(pltpu.VMEM(o.shape, o.dtype) for o in outs)
            + (pltpu.SemaphoreType.DMA((2, len(outs) - 1 + passages.shape[0])),),
            compiler_params=pltpu.CompilerParams(vmem_limit_bytes=63 * 2**20),
        )(*outs)
    (bo, tg, pg, g_ls, g_rb, g_sq, g_skv, g_so, g_lc, g_cq, g_ckv, g_co, g_lf, g_fi, g_fo) = outs
    return (
        bo[None], tg[None], pg, g_ls[0], g_rb[0], g_sq, g_skv, g_so,
        g_lc[0], g_cq, g_ckv, g_co, g_lf[0], g_fi, g_fo,
    )


def solution(mesh):
    both = ("dp", "fsdp")
    rows3, rows2, rows1 = P(both, None, None), P(both, None), P(both)
    placed = (
        rows3, P("dp", "fsdp", None), rows1, rows3, rows1, rows1, rows2, rows2, rows2,
        rows1, rows2, rows2, rows2, rows1, rows2, rows2,
    )
    outs = (
        rows3, rows3, P("dp", "fsdp", None), rows1, rows1, rows2, rows2, rows2,
        rows1, rows2, rows2, rows2, rows1, rows2, rows2,
    )

    def run(*args):
        targets, passages, self_q, ff_out = args[0], args[1], args[6], args[15]
        sz = Sizes(
            mesh.shape,
            targets.shape[2], passages.shape[1], targets.shape[1],
            self_q.shape[0], ff_out.shape[0],
            ff_out.shape[0] * mesh.shape["dp"] * mesh.shape["fsdp"] // ZDIM,
        )
        return per_device(sz, *args)

    return jax.shard_map(run, mesh=mesh, in_specs=placed, out_specs=outs, check_vma=False)
```
